32 devices in a mesh: dp: 16 (over z, y, x), tensor: 2 (over core).
Axes of the slice: x: 2, y: 2, z: 4, core: 2. Of those that a mesh axis runs over, the one named last changes fastest.
Arguments:
- hidden_in: bfloat16 [2, 16, 512, 768], P(None, 'dp'), may hold values from -6 to 6
- lengths: int32 [2, 16], P(None, 'dp'), may hold values from 16 to 512, as said below
- labels: int32 [2, 16], P(None, 'dp'), may hold values from 0 to 2
- out_cot: bfloat16 [2, 16, 512, 768], P(None, 'dp'), may hold values from -6 to 6
- input_weight: bfloat16 [3, 768, 768], P(None, 'dp', 'tensor'), may hold values from -0.21875 to 0.21875
- input_bias: bfloat16 [2, 768], P(None, ('tensor', 'dp')), may hold values from -3 to 3
- out_weight: bfloat16 [768, 768], P('tensor', 'dp'), may hold values from -1.75 to 1.75
- out_bias: bfloat16 [768], P('dp'), may hold values from -3 to 3
- first_gain: bfloat16 [768], P('dp'), may hold values from 0.5 to 1.5
- first_shift: bfloat16 [768], P('dp'), may hold values from -2 to 2
- up_weight: bfloat16 [768, 3072], P('dp', 'tensor'), may hold values from -0.21875 to 0.21875
- up_bias: bfloat16 [3072], P(('tensor', 'dp')), may hold values from -3 to 3
- down_weight: bfloat16 [3072, 768], P('tensor', 'dp'), may hold values from -0.21875 to 0.21875
- down_bias: bfloat16 [768], P('dp'), may hold values from -3 to 3
- second_gain: bfloat16 [768], P('dp'), may hold values from 0.5 to 1.5
- second_shift: bfloat16 [768], P('dp'), may hold values from -2 to 2
- pool_weight: bfloat16 [768, 768], P('dp'), may hold values from -0.21875 to 0.21875
- pool_bias: bfloat16 [768], P('dp'), may hold values from -3 to 3
- class_weight: bfloat16 [768, 3], P('dp'), may hold values from -0.4375 to 0.4375
- class_bias: bfloat16 [3], replicated, may hold values from -3 to 3
Outputs:
- block_out: bfloat16 [2, 16, 512, 768], P(None, 'dp')
- logits: float32 [2, 16, 3], P(None, 'dp')
- hidden_gradient: bfloat16 [2, 16, 512, 768], P(None, 'dp')
- input_weight_gradient: float32 [3, 768, 768], P(None, 'dp', 'tensor')
- input_bias_gradient: float32 [2, 768], P(None, ('tensor', 'dp'))
- out_weight_gradient: float32 [768, 768], P('tensor', 'dp')
- out_bias_gradient: float32 [768], P('dp')
- first_gain_gradient: float32 [768], P('dp')
- first_shift_gradient: float32 [768], P('dp')
- up_weight_gradient: float32 [768, 3072], P('dp', 'tensor')
- up_bias_gradient: float32 [3072], P(('tensor', 'dp'))
- down_weight_gradient: float32 [3072, 768], P('tensor', 'dp')
- down_bias_gradient: float32 [768], P('dp')
- second_gain_gradient: float32 [768], P('dp')
- second_shift_gradient: float32 [768], P('dp')
- pool_weight_gradient: float32 [768, 768], P('dp')
- pool_bias_gradient: float32 [768], P('dp')
- class_weight_gradient: float32 [768, 3], P('dp')
- class_bias_gradient: float32 [3], replicated
The draws below stay inside these ranges and needn't reach their ends.
Inputs may be any that keep to these rules, and one draw needn't show every extreme that they name: `lengths`: each sequence's valid tokens; in every draw some sequence has exactly 512 and some exactly 16.
All inputs are finite; a program needn't handle non-finite values.
Results may differ from the reference program's by a relative error of at most 0.023.
Values may be sent and summed in bfloat16 or wider, within the bound.
No kernel may reach another device: no remote copies, remote signals or barrier semaphores. Data moves between devices by JAX's collectives and lax.ppermute only.
A program may use at most 192 MiB of HBM per device.

```python
import math
import jax
import jax.numpy as jnp
from jax import lax

D = 768
HEADS = 12
HD = 64
FF = 3072
CLASSES = 3
LEN = 512
SHORTEST = 16
MICRO = 2
SEQS = 16


def draw_lengths(key, part):
    key = jax.random.fold_in(key, 11)
    seq_count = MICRO * SEQS
    first_key, second_key, third_key = jax.random.split(key, 3)
    drawn_lengths = jax.random.randint(first_key, (seq_count,), SHORTEST, LEN + 1)
    longest = jax.random.randint(second_key, (), 0, seq_count)
    offset = jax.random.randint(third_key, (), 1, seq_count)
    shortest_at = (longest + offset) % seq_count
    drawn_lengths = drawn_lengths.at[longest].set(LEN).at[shortest_at].set(SHORTEST)
    return drawn_lengths.reshape(MICRO, SEQS).astype(jnp.int32)


def set_ends(entries, own_key, smallest, top_value):
    shape = entries.shape
    place = [jax.random.randint(jax.random.fold_in(own_key, axis), (), 0, shape[axis]) for axis in range(len(shape))]
    entries = entries.at[tuple(place)].set(smallest)
    longest = shape.index(max(shape))
    place[longest] = (place[longest] + 1) % shape[longest]
    return entries.at[tuple(place)].set(top_value)


def raised(values, stream_key, source, target, blocks, factor):
    owner, partner = [(jnp.arange(values.shape[axis_at]) // (values.shape[axis_at] // blocks)).reshape([-1 if axis == axis_at else 1 for axis in range(values.ndim)]) for axis_at in (source, target)]
    chosen = jax.random.permutation(stream_key, blocks)[partner]
    strong = (owner == chosen) | (owner == (partner + blocks // 2) % blocks)
    return jnp.where(strong, factor * values, values)


def block_levels(key, shape, cuts, least, high):
    factor_of = 1.0
    for dim, parts in cuts:
        draws = jax.random.uniform(jax.random.fold_in(jax.random.fold_in(key, 6), dim), (parts,), jnp.float32, least / len(cuts), high / len(cuts))
        factor_of = factor_of * jnp.repeat(jnp.exp(draws), shape[dim] // parts).reshape((-1,) + (1,) * (len(shape) - 1 - dim))
    return factor_of


def scatter_about(rng, shape, spread, limit, cuts=(), kind=jnp.bfloat16):
    level = block_levels(rng, shape, cuts, -0.22, 0.18) if cuts else 1.0
    values = jax.random.normal(rng, shape, jnp.float32) * spread * level
    return jnp.minimum(jnp.maximum(values, -limit), limit).astype(kind)


def noise_with(rng, dims, scale, reach, cuts, heavy, held_as=jnp.bfloat16):
    entries = scale * jax.random.normal(rng, dims, jnp.float32)
    if cuts:
        entries = entries * block_levels(rng, dims, cuts, -0.22, 0.18)
    return jnp.clip(raised(entries, jax.random.fold_in(rng, 3), *heavy), -reach, reach).astype(held_as)


def setup_inputs(seed: int = 0) -> dict:
    splits = jax.random.split(jax.random.key(seed), 21)
    return {
        "hidden_in": noise_with(splits[0], (MICRO, SEQS, LEN, D), 1.0, 6.0, ((1, 16),), (1, 3, 16, 2.0)),
        "lengths": draw_lengths(jax.random.fold_in(splits[20], 71), 0),
        "labels": set_ends(jax.random.randint(splits[2], (MICRO, SEQS), 0, CLASSES), jax.random.fold_in(splits[2], 1), 0, CLASSES - 1).astype(jnp.int32),
        "out_cot": scatter_about(splits[3], (MICRO, SEQS, LEN, D), 1.0, 6.0, ((1, 16),)),
        "input_weight": scatter_about(splits[4], (3, D, D), D ** -0.5, 0.21875, ((1, 16), (2, 2))),
        "input_bias": scatter_about(splits[5], (2, D), 0.5, 3.0, ((1, 32),)),
        "out_weight": scatter_about(splits[6], (D, D), (D // 64) ** -0.5, 1.75, ((0, 2), (1, 16))),
        "out_bias": scatter_about(splits[7], (D,), 0.5, 3.0, ((0, 16),)),
        "first_gain": jnp.clip(1.0 + 0.1 * jax.random.normal(splits[8], (D,), jnp.float32), 0.5, 1.5).astype(jnp.bfloat16),
        "first_shift": scatter_about(splits[9], (D,), 0.3, 2.0, ((0, 16),)),
        "up_weight": scatter_about(splits[10], (D, FF), D ** -0.5, 0.21875, ((0, 16), (1, 2))),
        "up_bias": scatter_about(splits[11], (FF,), 0.5, 3.0, ((0, 32),)),
        "down_weight": scatter_about(splits[12], (FF, D), (FF // 4) ** -0.5, 0.21875, ((0, 2), (1, 16))),
        "down_bias": scatter_about(splits[13], (D,), 0.5, 3.0, ((0, 16),)),
        "second_gain": jnp.clip(1.0 + 0.1 * jax.random.normal(splits[14], (D,), jnp.float32), 0.5, 1.5).astype(jnp.bfloat16),
        "second_shift": scatter_about(splits[15], (D,), 0.3, 2.0, ((0, 16),)),
        "pool_weight": scatter_about(splits[16], (D, D), D ** -0.5, 0.21875, ((0, 16),)),
        "pool_bias": scatter_about(splits[17], (D,), 0.5, 3.0, ((0, 16),)),
        "class_weight": scatter_about(splits[18], (D, CLASSES), (D // 4) ** -0.5, 0.4375, ((0, 16),)),
        "class_bias": scatter_about(splits[19], (CLASSES,), 0.5, 3.0),
    }


@jax.custom_vjp
def low(v):
    return lax.optimization_barrier(v.astype(jnp.bfloat16)).astype(jnp.float32)

@jax.custom_vjp
def low_back(v):
    return v

def low_keep(v):
    return (low(v), None)

def low_pass(kept, grad):
    return (grad,)

def back_keep(v):
    return (v, None)

def back_low(kept, grad):
    return (low(grad),)
low.defvjp(low_keep, low_pass)
low_back.defvjp(back_keep, back_low)
EPS = 1e-06
HIGHEST = lax.Precision.HIGHEST

def product(left, right):
    return jnp.einsum('...i,ij->...j', left, right, precision=HIGHEST)

def layer_norm(total, norm_gain, norm_shift):
    centered = total - lax.optimization_barrier(jnp.mean(total, -1, keepdims=True))
    normed = centered * lax.rsqrt(lax.optimization_barrier(jnp.mean(centered * centered, -1, keepdims=True)) + EPS)
    return normed * norm_gain + norm_shift

def group_loss(parameters, inputs, lengths, cotangent, labels):
    input_weight, input_bias, out_weight, out_bias, first_gain, first_shift, up_weight, up_bias, down_weight, down_bias, second_gain, second_shift, pool_weight, pool_bias, class_weight, class_bias = parameters
    group_size = inputs.shape[0]
    valid_tokens = jnp.arange(LEN)[None, :] < lengths[:, None]
    head_shape = (group_size, LEN, HEADS, HD)
    query_rows = low_back(low(product(inputs, input_weight[0]) + input_bias[0]))
    key_rows = low_back(low(product(inputs, input_weight[1])))
    value_rows = low_back(low(product(inputs, input_weight[2]) + input_bias[1]))
    scores = jnp.einsum('gqhe,gkhe->ghqk', query_rows.reshape(head_shape), key_rows.reshape(head_shape), precision=HIGHEST) * (1.0 / math.sqrt(HD))
    scores = low_back(jnp.where(valid_tokens[:, None, None, :], scores, -1e+30))
    weights_low = low(jax.nn.softmax(scores, axis=-1))
    attended = jnp.einsum('ghqk,gkhe->gqhe', weights_low, value_rows.reshape(head_shape), precision=HIGHEST).reshape(group_size, LEN, D)
    attended = low_back(low(attended))
    first = low(layer_norm(inputs + low_back(product(attended, out_weight)) + out_bias, first_gain, first_shift))
    hidden = low_back(product(first, up_weight) + up_bias)
    active = low(jax.nn.gelu(hidden, approximate=False))
    final_norm = layer_norm(first + low_back(product(active, down_weight)) + down_bias, second_gain, second_shift)
    output = final_norm * valid_tokens[..., None].astype(final_norm.dtype)
    head_rows = low(final_norm[:, 0, :])
    pooled = low(jnp.tanh(product(head_rows, pool_weight) + pool_bias))
    logits = product(pooled, class_weight) + class_bias
    onehot = (jnp.arange(CLASSES)[None, :] == labels[:, None]).astype(logits.dtype)
    total_loss = jnp.sum(cotangent * output) + jnp.sum(jax.nn.logsumexp(logits, axis=-1) - lax.optimization_barrier(jnp.sum(logits * onehot, -1)))
    return (total_loss, (output, logits))

def reference(hidden_in, lengths, labels, out_cot, input_weight, input_bias, out_weight, out_bias, first_gain, first_shift, up_weight, up_bias, down_weight, down_bias, second_gain, second_shift, pool_weight, pool_bias, class_weight, class_bias):
    seq_count = MICRO * SEQS
    group_size = math.gcd(seq_count, max(1, 4096 // LEN))
    blocks = seq_count // group_size

    def arrange(array):
        return array.reshape((blocks, group_size) + array.shape[2:])
    inputs = arrange(hidden_in.astype(jnp.float32))
    length_blocks = arrange(lengths)
    label_blocks = arrange(labels)
    cotangents = arrange(out_cot.astype(jnp.float32))
    parameters = tuple((weight.astype(jnp.float32) for weight in (input_weight, input_bias, out_weight, out_bias, first_gain, first_shift, up_weight, up_bias, down_weight, down_bias, second_gain, second_shift, pool_weight, pool_bias, class_weight, class_bias)))

    def whole_loss(inputs_all, *weights):

        def scan_step(running, pieces):
            piece_loss, auxiliary = jax.checkpoint(group_loss)(weights, pieces[0], pieces[1], pieces[2], pieces[3])
            return (running + piece_loss, auxiliary)
        total_loss, auxiliary = lax.scan(scan_step, jnp.zeros((), jnp.float32), (inputs_all, length_blocks, cotangents, label_blocks))
        return (total_loss, auxiliary)
    total_loss, pullback, auxiliary = jax.vjp(whole_loss, inputs, *parameters, has_aux=True)
    gradients = pullback(jnp.ones_like(total_loss))
    output, logits = auxiliary
    return (output.reshape(MICRO, SEQS, LEN, D).astype(jnp.bfloat16), logits.reshape(MICRO, SEQS, CLASSES), gradients[0].reshape(MICRO, SEQS, LEN, D).astype(jnp.bfloat16), gradients[1], gradients[2], gradients[3], gradients[4], gradients[5], gradients[6], gradients[7], gradients[8], gradients[9], gradients[10], gradients[11], gradients[12], gradients[13], gradients[14], gradients[15], gradients[16])
```

```python
import math

import jax
import jax.numpy as jnp
from jax import lax
from jax.sharding import PartitionSpec as P

HD = 64
EPS = 1e-06
BF = jnp.bfloat16
F32 = jnp.float32


def xor_masks(size):
    bits = [1 << k for k in range(size.bit_length() - 1)]
    high, low = bits[2:][::-1], bits[:2]
    return high + low, high + low[::-1]


def block_mask(index, masks):
    mask = 0
    for k, bit in enumerate(masks):
        if (index >> k) & 1:
            mask ^= bit
    return mask


def swap(array, mask):
    size = lax.axis_size("dp")
    return lax.ppermute(array, "dp", [(i, i ^ mask) for i in range(size)])


def swap_core(array):
    return lax.ppermute(array, "tensor", [(0, 1), (1, 0)])


def gather_blocks(shard, masks):
    held = shard[None]
    for mask in masks:
        held = jnp.concatenate([held, swap(held, mask)], 0)
    return held


def scatter_blocks(blocks, masks):
    for mask in masks[::-1]:
        half = blocks.shape[0] // 2
        arrived = swap(blocks[half:], mask)
        blocks = blocks[:half] + arrived
    return blocks[0]


def in_order(blocks, masks, me):
    size = len(blocks)
    place = [0] * size
    for j in range(size):
        place[block_mask(j, masks)] = j
    chosen = jnp.array(place)[jnp.arange(size) ^ me]
    return jnp.take(blocks, chosen, axis=0)


def out_of_order(blocks, masks, me):
    owners = jnp.array([block_mask(j, masks) for j in range(len(blocks))]) ^ me
    return jnp.take(blocks, owners, axis=0)


def layer_norm(total):
    centered = total - jnp.mean(total, -1, keepdims=True)
    root = lax.rsqrt(jnp.mean(centered * centered, -1, keepdims=True) + EPS)
    return centered * root, root


def norm_backward(delta, normed, root, norm_gain):
    scaled = delta * norm_gain
    return root * (
        scaled
        - jnp.mean(scaled, -1, keepdims=True)
        - normed * jnp.mean(scaled * normed, -1, keepdims=True)
    )


def dot(left, right, dims=((1,), (0,))):
    return lax.dot_general(left, right, (dims, ((), ())), preferred_element_type=F32)


NT = ((1,), (1,))
TN = ((0,), (0,))


def per_device(
    hidden_in,
    lengths,
    labels,
    out_cot,
    input_weight,
    input_bias,
    out_weight,
    out_bias,
    first_gain,
    first_shift,
    up_weight,
    up_bias,
    down_weight,
    down_bias,
    second_gain,
    second_shift,
    pool_weight,
    pool_bias,
    class_weight,
    class_bias,
):
    size = lax.axis_size("dp")
    me = lax.axis_index("dp")
    core = lax.axis_index("tensor")
    length, width = hidden_in.shape[2:]
    rows = width // size
    half = input_weight.shape[2]
    hidden_half = up_weight.shape[1]
    heads = width // HD
    classes = class_bias.shape[0]
    order_x, order_y = xor_masks(size)

    def own(array):
        return lax.dynamic_index_in_dim(array.reshape((-1,) + array.shape[2:]), core, 0, False)

    x = own(hidden_in)
    cotangent = own(out_cot)
    count = own(lengths)
    label = own(labels)

    split_rows = jnp.concatenate([input_bias.reshape(1, rows), up_bias.reshape(2, rows)], 0)
    small = jnp.concatenate(
        [
            jnp.stack(
                [out_bias, first_gain, first_shift, down_bias, second_gain, second_shift, pool_bias]
            ),
            class_weight.T,
            split_rows,
            swap_core(split_rows),
        ],
        0,
    )
    small = in_order(gather_blocks(small, order_x), order_x, me)
    vectors = small.transpose(1, 0, 2).reshape(-1, width).astype(F32)
    out_vector, gain_one, shift_one, down_vector, gain_two, shift_two, pool_vector = vectors[:7]
    class_rows = vectors[7 : 7 + classes]
    bias_rows = small[:, [10, 13]].astype(F32)
    query_bias = bias_rows[:, :, : rows // 2].transpose(1, 0, 2).reshape(-1)
    value_bias = bias_rows[:, :, rows // 2 :].transpose(1, 0, 2).reshape(-1)
    up_vector = jnp.concatenate(
        [small[:, 11:13].reshape(-1), small[:, 14:16].reshape(-1)], 0
    ).astype(F32)

    def fetch(shard, masks):
        blocks = gather_blocks(shard, masks)
        other = swap_core(blocks)
        return [in_order(b, masks, me).reshape(width, -1) for b in (blocks, other)]

    query_key = fetch(jnp.concatenate([input_weight[0], input_weight[1]], 1), order_x)
    value_out = fetch(jnp.concatenate([input_weight[2], out_weight.T], 1), order_y)
    up_matrix = jnp.concatenate(fetch(up_weight, order_x), 1)
    down_matrix = jnp.concatenate(fetch(down_weight.T, order_y), 1)
    pool_half = lax.dynamic_slice_in_dim(pool_weight, core * half, half, 1)
    pool_halves = fetch(pool_half, order_x)
    pool_matrix = jnp.where(
        core == 0,
        jnp.concatenate(pool_halves, 1),
        jnp.concatenate(pool_halves[::-1], 1),
    )
    query_matrix, key_matrix = [
        jnp.concatenate([m[:, k * half : (k + 1) * half] for m in query_key], 1) for k in (0, 1)
    ]
    value_matrix, out_matrix = [
        jnp.concatenate([m[:, k * half : (k + 1) * half] for m in value_out], 1) for k in (0, 1)
    ]

    scale = 1.0 / math.sqrt(HD)
    query = (dot(x, query_matrix) + query_bias).astype(BF)
    key = dot(x, key_matrix).astype(BF)
    value = (dot(x, value_matrix) + value_bias).astype(BF)

    def split(array):
        return array.reshape(length, heads, HD)

    valid = jnp.arange(length) < count
    scores = jnp.einsum("qhe,khe->hqk", split(query), split(key), preferred_element_type=F32)
    scores = jnp.where(valid[None, None, :], scores * scale, -1e30)
    probs_wide = jax.nn.softmax(scores, axis=-1)
    probs = probs_wide.astype(BF)
    attended = jnp.einsum("hqk,khe->qhe", probs, split(value), preferred_element_type=F32)
    attended = attended.astype(BF).reshape(length, width)

    normed_one, root_one = layer_norm(x.astype(F32) + dot(attended, out_matrix, NT) + out_vector)
    first = (normed_one * gain_one + shift_one).astype(BF)
    hidden = dot(first, up_matrix) + up_vector
    active_wide, gelu_pullback = jax.vjp(lambda h: jax.nn.gelu(h, approximate=False), hidden)
    active = active_wide.astype(BF)

    normed_two, root_two = layer_norm(
        first.astype(F32) + dot(active, down_matrix, NT) + down_vector
    )
    mask = valid[:, None].astype(F32)
    final = normed_two * gain_two + shift_two
    block = (final * mask).astype(BF)
    head = final[:1].astype(BF)
    pooled_wide = jnp.tanh(dot(head, pool_matrix) + pool_vector)
    pooled = pooled_wide.astype(BF)
    logits = dot(pooled, class_rows.astype(BF), NT) + class_bias.astype(F32)
    onehot = (jnp.arange(classes) == label).astype(F32)
    logit_delta = jax.nn.softmax(logits, axis=-1) - onehot
    pre_delta = jnp.sum(logit_delta.T * class_rows, 0, keepdims=True) * (
        1.0 - pooled_wide * pooled_wide
    )
    head_delta = dot(pre_delta.astype(BF), pool_matrix, NT)
    delta = cotangent.astype(F32) * mask
    delta = delta.at[:1].add(head_delta)
    gain_two_grad = jnp.sum(delta * normed_two, 0)
    shift_two_grad = jnp.sum(delta, 0)
    second_delta = norm_backward(delta, normed_two, root_two, gain_two)
    down_bias_grad = jnp.sum(second_delta, 0)
    feed_delta = second_delta.astype(BF)
    down_grad = dot(feed_delta, active, TN)

    active_delta = dot(feed_delta, down_matrix)
    hidden_delta = gelu_pullback(active_delta)[0].astype(BF)
    up_bias_grad = jnp.sum(hidden_delta.astype(F32), 0)
    up_grad = dot(first, hidden_delta, TN)
    first_delta = second_delta + dot(hidden_delta, up_matrix, NT)

    gain_one_grad = jnp.sum(first_delta * normed_one, 0)
    shift_one_grad = jnp.sum(first_delta, 0)
    total_delta = norm_backward(first_delta, normed_one, root_one, gain_one)
    out_bias_grad = jnp.sum(total_delta, 0)
    branch_delta = total_delta.astype(BF)
    out_grad = dot(branch_delta, attended, TN)
    attended_delta = split(dot(branch_delta, out_matrix).astype(BF))
    prob_delta = jnp.einsum("qhe,khe->hqk", attended_delta, split(value), preferred_element_type=F32)
    score_delta = probs_wide * (prob_delta - jnp.sum(probs_wide * prob_delta, -1, keepdims=True))
    score_delta = score_delta.astype(BF)
    query_delta = jnp.einsum("hqk,khe->qhe", score_delta, split(key), preferred_element_type=F32)
    key_delta = jnp.einsum("hqk,qhe->khe", score_delta, split(query), preferred_element_type=F32)
    value_delta = jnp.einsum("hqk,qhe->khe", probs, attended_delta, preferred_element_type=F32)
    query_delta = (query_delta * scale).astype(BF).reshape(length, width)
    key_delta = (key_delta * scale).astype(BF).reshape(length, width)
    value_delta = value_delta.astype(BF).reshape(length, width)
    query_grad, key_grad, value_grad = [dot(x, d, TN) for d in (query_delta, key_delta, value_delta)]
    query_bias_grad = jnp.sum(query_delta.astype(F32), 0)
    value_bias_grad = jnp.sum(value_delta.astype(F32), 0)
    input_delta = (
        total_delta
        + dot(query_delta, query_matrix, NT)
        + dot(key_delta, key_matrix, NT)
        + dot(value_delta, value_matrix, NT)
    ).astype(BF)

    def spread(own_half, other_half, masks):
        total = own_half + swap_core(other_half)
        return scatter_blocks(out_of_order(total.reshape(size, rows, -1), masks, me), masks)

    def halves(*arrays):
        cut = [a.astype(BF) for a in arrays]
        return [
            jnp.concatenate([a[:, : a.shape[1] // 2] for a in cut], 1),
            jnp.concatenate([a[:, a.shape[1] // 2 :] for a in cut], 1),
        ]

    down_share = spread(*halves(down_grad), order_y)
    up_share = spread(*halves(up_grad), order_x)
    query_key_share = spread(*halves(query_grad, key_grad), order_x)
    value_out_share = spread(*halves(value_grad, out_grad), order_y)

    def share_rows(array, which):
        cut = array.reshape(2, size, -1)
        return cut[which]

    def bias_share(which):
        return jnp.concatenate(
            [share_rows(a, which) for a in (query_bias_grad, value_bias_grad, up_bias_grad)], 1
        )

    both = jnp.stack(
        [
            out_bias_grad,
            gain_one_grad,
            shift_one_grad,
            down_bias_grad,
            gain_two_grad,
            shift_two_grad,
        ]
    )
    both = both.reshape(6, size, rows).transpose(1, 0, 2).reshape(size, 6 * rows)
    kept = jnp.concatenate([both, bias_share(0)], 1)
    sent = jnp.concatenate([both, bias_share(1)], 1)
    vector_share = scatter_blocks(
        out_of_order(kept + swap_core(sent), order_x, me)[:, None], order_x
    )[0]
    vector_grads = vector_share[: 6 * rows].reshape(6, rows)
    input_bias_grad = vector_share[6 * rows : 7 * rows].reshape(2, rows // 2)
    up_bias_share = vector_share[7 * rows :]

    lane = 128
    tail = jnp.pad(jnp.concatenate([logit_delta, logits], 1), ((0, 0), (0, lane - 2 * classes)))
    ramp = jnp.concatenate(
        [head.astype(F32), pooled.astype(F32), pre_delta, tail], 1
    )
    pair = jnp.concatenate([ramp, swap_core(ramp)], 0)
    pair_logits = pair[:, 3 * width + classes : 3 * width + 2 * classes]
    logits_out = jnp.where(core == 0, pair_logits, pair_logits[::-1])
    ramps = gather_blocks(pair, order_x).reshape(-1, 3 * width + lane)
    heads_all, pooled_all, pre_all = [ramps[:, k * width : (k + 1) * width] for k in range(3)]
    logit_deltas = ramps[:, 3 * width : 3 * width + classes]
    own_columns = lambda a: lax.dynamic_slice_in_dim(a, me * rows, rows, 1)
    pool_grad = dot(own_columns(heads_all).astype(BF), pre_all.astype(BF), TN)
    pool_bias_grad = jnp.sum(own_columns(pre_all), 0)
    class_grad = lax.dot_general(
        own_columns(pooled_all),
        logit_deltas,
        (TN, ((), ())),
        precision=lax.Precision.HIGHEST,
    )
    class_bias_grad = jnp.sum(logit_deltas, 0)

    block_out = lax.all_gather(block, "tensor", axis=0)[:, None]
    input_grad = lax.all_gather(input_delta, "tensor", axis=0)[:, None]
    return (
        block_out,
        logits_out[:, None],
        input_grad,
        jnp.stack(
            [
                query_key_share[:, :half],
                query_key_share[:, half:],
                value_out_share[:, :half],
            ]
        ).astype(F32),
        input_bias_grad,
        value_out_share[:, half:].T.astype(F32),
        vector_grads[0],
        vector_grads[1],
        vector_grads[2],
        up_share.astype(F32),
        up_bias_share,
        down_share.T.astype(F32),
        vector_grads[3],
        vector_grads[4],
        vector_grads[5],
        pool_grad,
        pool_bias_grad,
        class_grad,
        class_bias_grad,
    )


def solution(mesh):
    placed = (
        P(None, "dp", None, None),
        P(None, "dp"),
        P(None, "dp"),
        P(None, "dp", None, None),
        P(None, "dp", "tensor"),
        P(None, ("tensor", "dp")),
        P("tensor", "dp"),
        P("dp"),
        P("dp"),
        P("dp"),
        P("dp", "tensor"),
        P(("tensor", "dp")),
        P("tensor", "dp"),
        P("dp"),
        P("dp"),
        P("dp"),
        P("dp", None),
        P("dp"),
        P("dp", None),
        P(),
    )
    return jax.shard_map(
        per_device,
        mesh=mesh,
        in_specs=placed,
        out_specs=(
            P(None, "dp", None, None),
            P(None, "dp", None),
            P(None, "dp", None, None),
            P(None, "dp", "tensor"),
            P(None, ("tensor", "dp")),
            P("tensor", "dp"),
            P("dp"),
            P("dp"),
            P("dp"),
            P("dp", "tensor"),
            P(("tensor", "dp")),
            P("tensor", "dp"),
            P("dp"),
            P("dp"),
            P("dp"),
            P("dp", None),
            P("dp"),
            P("dp", None),
            P(),
        ),
        check_vma=False,
    )
```

```python
import functools
import math

import jax
import jax.numpy as jnp
from jax import lax
from jax.experimental import pallas as pl
from jax.experimental.pallas import tpu as pltpu
from jax.sharding import PartitionSpec as P

HD = 64
LANES = 128
BLOCKS = 16
EPS = 1e-06
BF = jnp.bfloat16
F32 = jnp.float32
NN = ((1,), (0,))
NT = ((1,), (1,))
TN = ((0,), (0,))
HBM = pl.BlockSpec(memory_space=pltpu.HBM)
SCALARS = pl.BlockSpec(memory_space=pltpu.SMEM)
VMEM_BYTES = 48 * 1024 * 1024
COST = 1024

OUT_B, GAIN_1, SHIFT_1, DOWN_B, GAIN_2, SHIFT_2, POOL_B, CLASS, QUERY_B, VALUE_B, UP_B = (
    0, 1, 2, 3, 4, 5, 6, 7, 10, 11, 12,
)
SHARED, PAIR_ROW, UP_ROW = 10, 10, 11


def dot(left, right, dims=NN):
    return lax.dot_general(left, right, (dims, ((), ())), preferred_element_type=F32)


def begin(source, target, sem):
    copy = pltpu.make_async_copy(source, target, sem)
    copy.start()
    return copy


def row_block(me, mask, rows):
    return pl.ds(pl.multiple_of((me ^ mask) * rows, 16), rows)


def fetch(pieces, masks, me, target, sem, columns=None):
    rows = target.shape[0] // BLOCKS
    start, width = columns or (0, pieces[0].shape[2])
    for h in range(2):
        for j in range(BLOCKS):
            piece = pieces[2 * h + j // (BLOCKS // 2)]
            begin(
                piece.at[j % (BLOCKS // 2), :, pl.ds(start, width)],
                target.at[row_block(me, masks[j], rows), pl.ds(h * width, width)],
                sem,
            )


def landed(target, sem):
    pltpu.make_async_copy(target, target, sem).wait()


def hand_out(source, blocks, masks, me, lower, upper, sem):
    rows = source.shape[0] // BLOCKS
    for b in blocks:
        mask = me ^ b
        place = sum(((mask >> (masks[1 << k].bit_length() - 1)) & 1) << k for k in range(4))
        block = source.at[pl.ds(b * rows, rows), :]

        @pl.when(place < BLOCKS // 2)
        def _():
            begin(block, lower.at[place], sem)

        @pl.when(place >= BLOCKS // 2)
        def _():
            begin(block, upper.at[place - BLOCKS // 2], sem)


def pair_product(lefts, rights, grad, masks, me, lower, upper, sem):
    step = 4
    rows = grad.shape[0] // BLOCKS
    for c in range(BLOCKS // step):
        span = slice(c * step * rows, (c + 1) * step * rows)
        total = dot(lefts[0][span, :], rights[0][...]) + dot(lefts[1][span, :], rights[1][...])
        grad[span, :] = total.astype(BF)
        hand_out(grad, range(c * step, (c + 1) * step), masks, me, lower, upper, sem)


def row_loop(length, step, body, init=None):
    def run(i, carry):
        return body(pl.ds(pl.multiple_of(i * step, step), step), i * step, carry)

    return lax.fori_loop(0, length // step, run, init)


def mean(array):
    return jnp.mean(array, -1, keepdims=True)


def normalize(total):
    centered = total - mean(total)
    root = lax.rsqrt(mean(centered * centered) + EPS)
    return centered * root, root


def norm_backward(delta, normed, root, gain):
    scaled = delta * gain
    return root * (scaled - mean(scaled) - normed * mean(scaled * normed))


def column_sum(array):
    return jnp.sum(array, 0, keepdims=True)


def unpack_vectors(extra, vec, h):
    width = vec.shape[1]
    rows, part = width // BLOCKS, width // BLOCKS // 2
    for b in range(BLOCKS):
        own = extra[b * rows : b * rows + 16, :]
        if h == 0:
            vec[0:SHARED, b * rows : (b + 1) * rows] = own[0:SHARED, 0:rows]
        at = h * width // 2 + b * part
        vec[QUERY_B : QUERY_B + 1, at : at + part] = own[PAIR_ROW : PAIR_ROW + 1, 0:part]
        vec[VALUE_B : VALUE_B + 1, at : at + part] = own[PAIR_ROW : PAIR_ROW + 1, part:rows]
        row, at = UP_B + 2 * h + b // (BLOCKS // 2), b % (BLOCKS // 2) * 2 * rows
        vec[row : row + 1, at : at + 2 * rows] = own[UP_ROW : UP_ROW + 1, 0 : 2 * rows]


def pack_vectors(shared, query, value, up, extra):
    width = shared.shape[1]
    rows, part = width // BLOCKS, width // BLOCKS // 2
    extra[...] = jnp.zeros(extra.shape, F32)
    for b in range(BLOCKS):
        top = b * rows
        extra[top : top + 8, 0:rows] = shared[:, b * rows : (b + 1) * rows]
        at = b * part
        extra[top + PAIR_ROW : top + PAIR_ROW + 1, 0:part] = query[:, at : at + part]
        extra[top + PAIR_ROW : top + PAIR_ROW + 1, part:rows] = value[:, at : at + part]
        at = b * 2 * rows
        extra[top + UP_ROW : top + UP_ROW + 1, 0 : 2 * rows] = up[:, at : at + 2 * rows]


def attend_kernel(masks_a, masks_b, info, hidden, *refs):
    qk, vo = refs[0:4], refs[4:8]
    q_out, k_out, v_out, att_own_out, att_other_out, p_out, first_out, first_t_out = refs[8:16]
    x_t_out, x_t_other_out, normed_out, root_out, vec_out = refs[16:21]
    x, other_x, wa, wb, q, k, v, att, p, first, flip, other_flip, total, root, vec, extra, sems = refs[21:]
    me, core = info[0], info[1]
    count = info[2 + core]
    length, width = x.shape
    half = width // 2
    begin(hidden.at[core], x, sems.at[0])
    begin(hidden.at[1 - core], other_x, sems.at[14])
    fetch(qk, masks_a, me, wa, sems.at[1], (0, width))
    fetch(vo, masks_b, me, wb, sems.at[2])
    outs = []
    landed(x, sems.at[0])
    flip[...] = x[...].T
    outs.append(begin(flip, x_t_out, sems.at[3]))
    landed(other_x, sems.at[14])
    other_flip[...] = other_x[...].T
    outs.append(begin(other_flip, x_t_other_out, sems.at[15]))
    landed(wb, sems.at[2])
    part = wb.shape[1] // 2
    for h in range(2):
        extra[...] = wb[:, h * part + width : (h + 1) * part].astype(F32)
        unpack_vectors(extra, vec, h)
    outs.append(begin(vec, vec_out, sems.at[13]))
    landed(wa, sems.at[1])
    for h in range(2):
        own = slice(h * half, (h + 1) * half)
        both = dot(x[...], wa[:, h * width : (h + 1) * width])
        q[:, own] = (both[:, :half] + vec[QUERY_B : QUERY_B + 1, own]).astype(BF) * (1.0 / math.sqrt(HD))
        k[:, own] = both[:, half:].astype(BF)
    for h in range(2):
        own = slice(h * half, (h + 1) * half)
        values = dot(x[...], wb[:, h * part : h * part + half])
        v[:, own] = (values + vec[VALUE_B : VALUE_B + 1, own]).astype(BF)
    outs.append(begin(q, q_out, sems.at[4]))
    outs.append(begin(k, k_out, sems.at[5]))
    outs.append(begin(v, v_out, sems.at[6]))
    keys = lax.broadcasted_iota(jnp.int32, (1, length), 1)
    bias = jnp.where(keys < count, 0.0, -1e30).astype(F32)
    lane = lax.broadcasted_iota(jnp.int32, (1, LANES), 1)
    span_rows = length // 2

    def pair_step(pair, _):
        cols = pl.ds(pl.multiple_of(pair * LANES, LANES), LANES)
        slot = pair % 2

        @pl.when(pair >= 2)
        def _():
            pltpu.make_async_copy(p.at[slot], p.at[slot], sems.at[7 + slot]).wait()

        k_pair = k[:, cols]
        v_pair = v[:, cols]
        for c in range(2):
            span = slice(c * span_rows, (c + 1) * span_rows)
            q_pair = q[span, cols]
            acc = None
            for a in range(2):
                mine = (lane < HD) if a == 0 else (lane >= HD)
                scores = dot(jnp.where(mine, q_pair, 0.0).astype(BF), k_pair, NT) + bias
                top = jnp.max(scores, -1, keepdims=True)
                weights = jnp.exp(scores - top)
                sums = jnp.sum(weights, -1, keepdims=True)
                probs = (weights * (1.0 / sums)).astype(BF)
                p[slot, a, span, :] = probs
                term = dot(probs, jnp.where(mine, v_pair, 0.0).astype(BF))
                acc = term if acc is None else acc + term
            att[span, cols] = acc.astype(BF)
        begin(p.at[slot], p_out.at[pair], sems.at[7 + slot])
        return 0

    lax.fori_loop(0, width // LANES, pair_step, 0)
    outs.append(begin(att.at[:, pl.ds(0, half)], att_own_out, sems.at[9]))
    outs.append(begin(att.at[:, pl.ds(half, half)], att_other_out, sems.at[16]))
    total[...] = dot(att[:, :half], wb[:, half:width], NT) + dot(
        att[:, half:], wb[:, part + half : part + width], NT
    )

    def norm_rows(rows, _, carry):
        normed, own_root = normalize(x[rows, :].astype(F32) + total[rows, :] + vec[OUT_B : OUT_B + 1, :])
        total[rows, :] = normed
        root[rows, :] = jnp.broadcast_to(own_root, (own_root.shape[0], LANES))
        first[rows, :] = (normed * vec[GAIN_1 : GAIN_1 + 1, :] + vec[SHIFT_1 : SHIFT_1 + 1, :]).astype(BF)
        return carry

    row_loop(length, 64, norm_rows, 0)
    outs.append(begin(first, first_out, sems.at[10]))
    outs.append(begin(total, normed_out, sems.at[11]))
    outs.append(begin(root, root_out, sems.at[12]))
    outs[0].wait()
    flip[...] = first[...].T
    outs[0] = begin(flip, first_t_out, sems.at[3])
    for slot in range(2):
        pltpu.make_async_copy(p.at[slot], p.at[slot], sems.at[7 + slot]).wait()
    for copy in outs:
        copy.wait()


def up_kernel(masks, info, vec, first_in, *refs):
    pieces = refs[0:4]
    own_out, other_out, slope_out = refs[4:7]
    first, w, active, slope, sems = refs[7:]
    me = info[0]
    begin(first_in, first, sems.at[0])
    fetch(pieces, masks, me, w, sems.at[1])
    length, width = first.shape
    hidden_width = w.shape[1]
    chunk = 256
    landed(first, sems.at[0])
    landed(w, sems.at[1])
    outs = []
    for c in range(hidden_width // chunk):
        cols = slice(c * chunk, (c + 1) * chunk)
        row = UP_B + c * chunk // width
        at = c * chunk % width
        hidden = dot(first[...], w[:, cols]) + vec[row : row + 1, at : at + chunk]
        cdf = 0.5 + 0.5 * lax.erf(hidden * math.sqrt(0.5))
        density = jnp.exp(hidden * hidden * -0.5) * (1.0 / math.sqrt(2.0 * math.pi))
        active[:, cols] = (hidden * cdf).astype(BF)
        slope[:, cols] = (cdf + hidden * density).astype(BF)
        if (c + 1) * chunk == hidden_width // 2:
            outs.append(begin(active.at[:, pl.ds(0, hidden_width // 2)], own_out, sems.at[2]))
    outs.append(begin(active.at[:, pl.ds(hidden_width // 2, hidden_width // 2)], other_out, sems.at[4]))
    outs.append(begin(slope, slope_out, sems.at[3]))
    for copy in outs:
        copy.wait()


def ramp_kernel(masks, pool_masks, info, class_bias, vec, cotangent, own_in, other_in, first_in, *refs):
    pieces, pool_pieces = refs[0:4], refs[4:8]
    block_out, ramp_out, feed_out, feed_t_out, second_out, sums_out = refs[8:14]
    active, first, cot, w, pool, total, root, block, feed, feed_t, second, grads, ramp, sems = refs[14:]
    me, core = info[0], info[1]
    count, label = info[2 + core], info[4 + core]
    cut = w.shape[1] // 2
    begin(own_in, active.at[:, pl.ds(0, cut)], sems.at[0])
    begin(other_in, active.at[:, pl.ds(cut, cut)], sems.at[0])
    begin(first_in, first, sems.at[1])
    begin(cotangent.at[core], cot, sems.at[2])
    fetch(pieces, masks, me, w, sems.at[3])
    length, width = first.shape
    half = width // 2
    rows = width // BLOCKS
    for h in range(2):
        side = core if h == 0 else 1 - core
        for j in range(BLOCKS):
            begin(
                pool_pieces[2 * h + j // (BLOCKS // 2)].at[j % (BLOCKS // 2), :, pl.ds(width, half)],
                pool.at[
                    row_block(me, pool_masks[j], rows),
                    pl.ds(pl.multiple_of(side * half, LANES), half),
                ],
                sems.at[4],
            )
    outs = []
    landed(active, sems.at[0])
    landed(w, sems.at[3])
    total[...] = dot(active[...], w[...], NT)
    landed(first, sems.at[1])
    gain, shift = vec[GAIN_2 : GAIN_2 + 1, :], vec[SHIFT_2 : SHIFT_2 + 1, :]

    def row_ids(start, step):
        return start + lax.broadcasted_iota(jnp.int32, (step, 1), 0)

    def norm_rows(rows, start, carry):
        normed, own_root = normalize(first[rows, :].astype(F32) + total[rows, :] + vec[DOWN_B : DOWN_B + 1, :])
        total[rows, :] = normed
        root[rows, :] = jnp.broadcast_to(own_root, (own_root.shape[0], LANES))
        valid = row_ids(start, own_root.shape[0]) < count
        block[rows, :] = jnp.where(valid, normed * gain + shift, 0.0).astype(BF)
        return carry

    row_loop(length, 64, norm_rows, 0)
    outs.append(begin(block, block_out, sems.at[5]))
    landed(pool, sems.at[4])
    head = (total[0:8, :] * gain + shift).astype(BF)
    pooled_wide = jnp.tanh(dot(head, pool[...]) + vec[POOL_B : POOL_B + 1, :])
    pooled = pooled_wide.astype(BF).astype(F32)
    class_rows = [vec[CLASS + c : CLASS + c + 1, :] for c in range(3)]
    logits = [
        jnp.sum(pooled * class_rows[c], -1, keepdims=True) + class_bias[c] for c in range(3)
    ]
    top = jnp.maximum(jnp.maximum(logits[0], logits[1]), logits[2])
    powers = [jnp.exp(l - top) for l in logits]
    power_sum = powers[0] + powers[1] + powers[2]
    deltas = [powers[c] / power_sum - jnp.where(label == c, 1.0, 0.0) for c in range(3)]
    pre = sum(deltas[c] * class_rows[c] for c in range(3)) * (1.0 - pooled_wide * pooled_wide)
    pre_high = pre.astype(BF)
    pre_low = (pre - pre_high.astype(F32)).astype(BF)
    head_delta = (dot(pre_high, pool[...], NT) + dot(pre_low, pool[...], NT))[0:1, :]
    lane = lax.broadcasted_iota(jnp.int32, (1, width), 1)
    tail = jnp.zeros((1, width), F32)
    for c in range(3):
        tail = jnp.where(lane == c, deltas[c][0:1], tail)
        tail = jnp.where(lane == LANES + c, logits[c][0:1], tail)
    ramp[0:1, :] = head[0:1, :].astype(F32)
    ramp[1:2, :] = pooled[0:1, :]
    ramp[2:3, :] = pre[0:1, :]
    ramp[3:4, :] = tail
    ramp[4:8, :] = jnp.zeros((4, width), F32)
    outs.append(begin(ramp, ramp_out, sems.at[6]))
    landed(cot, sems.at[2])

    def back_rows(rows, start, carry):
        ids = row_ids(start, 64)
        delta = jnp.where(ids < count, cot[rows, :].astype(F32), 0.0)
        delta = delta + jnp.where(ids == 0, head_delta, 0.0)
        normed = total[rows, :]
        dsecond = norm_backward(delta, normed, root[rows, 0:1], gain)
        second[rows, :] = dsecond
        feed[rows, :] = dsecond.astype(BF)
        return (
            carry[0] + column_sum(delta * normed),
            carry[1] + column_sum(delta),
            carry[2] + column_sum(dsecond),
        )

    zero = jnp.zeros((1, width), F32)
    sums = row_loop(length, 64, back_rows, (zero, zero, zero))
    for i in range(3):
        grads[i : i + 1, :] = sums[i]
    grads[3:8, :] = jnp.zeros((5, width), F32)
    outs.append(begin(grads, sums_out, sems.at[7]))
    outs.append(begin(second, second_out, sems.at[8]))
    outs.append(begin(feed, feed_out, sems.at[9]))
    feed_t[...] = feed[...].T
    outs.append(begin(feed_t, feed_t_out, sems.at[10]))
    for copy in outs:
        copy.wait()


def down_grad_kernel(grad_masks, info, feed_t_in, feed_t_other, act_in, act_other, *refs):
    lower, upper = refs[0:2]
    left, left_other, right, right_other, grad, sems = refs[2:]
    loads = ((feed_t_in, left), (act_in, right), (feed_t_other, left_other), (act_other, right_other))
    for i, (source, target) in enumerate(loads):
        begin(source, target, sems.at[i])
    for i, (_, target) in enumerate(loads):
        landed(target, sems.at[i])
    pair_product((left, left_other), (right, right_other), grad, grad_masks, info[0], lower, upper, sems.at[4])
    landed(grad, sems.at[4])


def up_grad_kernel(grad_masks, info, first_t_in, first_t_other, delta_in, delta_other, *refs):
    lower, upper, sums_out = refs[0:3]
    left, left_other, right, right_other, grad, sums, sems = refs[3:]
    loads = ((first_t_in, left), (delta_in, right), (first_t_other, left_other), (delta_other, right_other))
    for i, (source, target) in enumerate(loads):
        begin(source, target, sems.at[i])
    for i, (_, target) in enumerate(loads):
        landed(target, sems.at[i])
    pair_product((left, left_other), (right, right_other), grad, grad_masks, info[0], lower, upper, sems.at[4])
    sums[...] = column_sum(right[...].astype(F32)) + column_sum(right_other[...].astype(F32))
    begin(sums, sums_out, sems.at[5])
    landed(sums, sems.at[5])
    landed(grad, sems.at[4])


def hidden_kernel(down_masks, info, feed_in, slope_in, *refs):
    pieces = refs[0:4]
    own_out, other_out = refs[4:6]
    feed, slope, w, delta, sems = refs[6:]
    me = info[0]
    begin(feed_in, feed, sems.at[0])
    fetch(pieces, down_masks, me, w, sems.at[1])
    begin(slope_in, slope, sems.at[2])
    landed(feed, sems.at[0])
    landed(w, sems.at[1])
    landed(slope, sems.at[2])
    hidden_width = w.shape[1]
    cut = hidden_width // 2
    chunk = 512
    copies = []
    for c in reversed(range(hidden_width // chunk)):
        cols = slice(c * chunk, (c + 1) * chunk)
        delta[:, cols] = (dot(feed[...], w[:, cols]) * slope[:, cols].astype(F32)).astype(BF)
        if c * chunk == cut:
            copies.append(begin(delta.at[:, pl.ds(cut, cut)], other_out, sems.at[3]))
    copies.append(begin(delta.at[:, pl.ds(0, cut)], own_out, sems.at[4]))
    for copy in copies:
        copy.wait()


def branch_kernel(
    up_masks, masks_b, info, vec, sums_in, own_in, other_in, second_in, normed_in, root_in, *refs
):
    up, vo = refs[0:4], refs[4:8]
    total_out, datt_out, branch_t_out, sums_out = refs[8:12]
    delta, wu, wo, second, normed, root, branch, branch_t, datt, grads, sems = refs[12:]
    me = info[0]
    length, width = normed.shape
    half = width // 2
    cut = delta.shape[1] // 2
    begin(own_in, delta.at[:, pl.ds(0, cut)], sems.at[0])
    begin(other_in, delta.at[:, pl.ds(cut, cut)], sems.at[0])
    fetch(up, up_masks, me, wu, sems.at[1])
    begin(second_in, second, sems.at[2])
    begin(normed_in, normed, sems.at[3])
    begin(root_in, root, sems.at[4])
    fetch(vo, masks_b, me, wo, sems.at[5], (half, half))
    landed(delta, sems.at[0])
    landed(wu, sems.at[1])
    landed(second, sems.at[2])
    second[...] = second[...] + dot(delta[...], wu[...], NT)
    landed(normed, sems.at[3])
    landed(root, sems.at[4])
    gain = vec[GAIN_1 : GAIN_1 + 1, :]

    def back_rows(rows, _, carry):
        dfirst = second[rows, :]
        own_normed = normed[rows, :]
        total = norm_backward(dfirst, own_normed, root[rows, 0:1], gain)
        second[rows, :] = total
        branch[rows, :] = total.astype(BF)
        return (
            carry[0] + column_sum(total),
            carry[1] + column_sum(dfirst * own_normed),
            carry[2] + column_sum(dfirst),
        )

    zero = jnp.zeros((1, width), F32)
    sums = row_loop(length, 64, back_rows, (zero, zero, zero))
    for i in range(3):
        grads[i : i + 1, :] = sums[i]
    grads[3:6, :] = sums_in[0:3, :]
    grads[6:8, :] = jnp.zeros((2, width), F32)
    outs = [begin(second, total_out, sems.at[7]), begin(grads, sums_out, sems.at[8])]
    landed(wo, sems.at[5])
    datt[...] = dot(branch[...], wo[...]).astype(BF)
    outs.append(begin(datt, datt_out, sems.at[9]))
    branch_t[...] = branch[...].T
    outs.append(begin(branch_t, branch_t_out, sems.at[10]))
    for copy in outs:
        copy.wait()


def back_kernel(q_in, k_in, v_in, att_own_in, att_other_in, datt_in, p_in, *refs):
    own_out, other_out = refs[0:2]
    q, k, v, att, datt, p, dq, dk, dv, sems = refs[2:]
    length, width = q.shape
    half = width // 2
    for slot in range(2):
        begin(p_in.at[slot], p.at[slot], sems.at[11 + slot])
    loads = (
        (q_in, q),
        (k_in, k),
        (v_in, v),
        (att_own_in, att.at[:, pl.ds(0, half)]),
        (att_other_in, att.at[:, pl.ds(half, half)]),
        (datt_in, datt),
    )
    for i, (source, target) in enumerate(loads):
        begin(source, target, sems.at[i])
    for i, (_, target) in enumerate(loads):
        landed(target, sems.at[i])
    lane = lax.broadcasted_iota(jnp.int32, (1, LANES), 1)
    pairs = width // LANES

    def pair_step(pair, _):
        cols = pl.ds(pl.multiple_of(pair * LANES, LANES), LANES)
        slot = pair % 2
        pltpu.make_async_copy(p.at[slot], p.at[slot], sems.at[11 + slot]).wait()
        do = datt[:, cols]
        product = do.astype(F32) * att[:, cols].astype(F32)
        k_pair, v_pair = k[:, cols], v[:, cols]
        q_t = q[:, cols].T
        do_t = do.T
        dq_sum = None
        dk_parts, dv_parts = [], []
        for a in range(2):
            mine = (lane < HD) if a == 0 else (lane >= HD)
            shift = jnp.sum(jnp.where(mine, product, 0.0), -1, keepdims=True)
            dprobs = dot(jnp.where(mine, do, 0.0).astype(BF), v_pair, NT)
            probs = p[slot, a]
            dscores = (probs.astype(F32) * (dprobs - shift)).astype(BF)
            term = dot(dscores, jnp.where(mine, k_pair, 0.0).astype(BF))
            dq_sum = term if dq_sum is None else dq_sum + term
            own = slice(a * HD, (a + 1) * HD)
            dk_parts.append(dot(q_t[own], dscores))
            dv_parts.append(dot(do_t[own], probs))
        dq[:, cols] = (dq_sum * (1.0 / math.sqrt(HD))).astype(BF)
        dk[:, cols] = jnp.concatenate(dk_parts, 0).T.astype(BF)
        dv[:, cols] = jnp.concatenate(dv_parts, 0).T.astype(BF)

        @pl.when(pair + 2 < pairs)
        def _():
            begin(p_in.at[pair + 2], p.at[slot], sems.at[11 + slot])

        return 0

    lax.fori_loop(0, pairs, pair_step, 0)
    for h, out in ((1, other_out), (0, own_out)):
        for i, source in enumerate((dq, dk, dv)):
            begin(source.at[:, pl.ds(h * half, half)], out.at[:, pl.ds(i * half, half)], sems.at[i])
    for i, target in enumerate((dq, dk, dv)):
        landed(target, sems.at[i])


def input_grad_kernel(
    masks_a, masks_b, info, sums_in, sums_other, up_sums, x_t_in, x_t_other, delta_in, delta_other,
    branch_t_in, branch_t_other, att_in, att_other, *refs
):
    qk_pieces, vo_pieces = refs[0:2], refs[2:4]
    (
        x_t, other_x_t, delta, other_delta, branch_t, other_branch_t, att, other_att, grad_a, grad_b, extra, sems,
    ) = refs[4:]
    me = info[0]
    loads = (
        (x_t_in, x_t),
        (delta_in, delta),
        (x_t_other, other_x_t),
        (delta_other, other_delta),
        (branch_t_in, branch_t),
        (att_in, att),
        (branch_t_other, other_branch_t),
        (att_other, other_att),
    )
    for i, (source, target) in enumerate(loads):
        begin(source, target, sems.at[i])
    for i, (_, target) in enumerate(loads):
        landed(target, sems.at[i])
    width = x_t.shape[0]
    half = width // 2
    columns = column_sum(delta[...].astype(F32)) + column_sum(other_delta[...].astype(F32))
    pack_vectors(sums_in[...] + sums_other[...], columns[:, :half], columns[:, width:], up_sums[...], extra)
    grad_b[:, width:] = extra[...].astype(BF)
    step = 4
    rows = width // BLOCKS
    for c in range(BLOCKS // step):
        span = slice(c * step * rows, (c + 1) * step * rows)
        blocks = range(c * step, (c + 1) * step)
        both = dot(x_t[span, :], delta[...]) + dot(other_x_t[span, :], other_delta[...])
        grad_a[span, :] = both[:, :width].astype(BF)
        grad_b[span, :half] = both[:, width:].astype(BF)
        out = dot(branch_t[span, :], att[...]) + dot(other_branch_t[span, :], other_att[...])
        grad_b[span, half:width] = out.astype(BF)
        hand_out(grad_a, blocks, masks_a, me, *qk_pieces, sems.at[8])
        hand_out(grad_b, blocks, masks_b, me, *vo_pieces, sems.at[9])
    landed(grad_a, sems.at[8])
    landed(grad_b, sems.at[9])


def input_kernel(masks_a, masks_b, info, own_in, other_in, total_in, *refs):
    qk, vo = refs[0:4], refs[4:8]
    (out,) = refs[8:9]
    own, other, total, wa, wv, low, sems = refs[9:]
    me = info[0]
    length, width = total.shape
    half = width // 2
    fetch(qk, masks_a, me, wa, sems.at[0], (0, width))
    fetch(vo, masks_b, me, wv, sems.at[1], (0, half))
    loads = ((own_in, own), (other_in, other), (total_in, total))
    for i, (source, target) in enumerate(loads):
        begin(source, target, sems.at[2 + i])
    for i, (_, target) in enumerate(loads):
        landed(target, sems.at[2 + i])
    landed(wa, sems.at[0])
    landed(wv, sems.at[1])
    acc = total[...]
    for h, delta in enumerate((own, other)):
        acc = acc + dot(delta[:, :width], wa[:, h * width : (h + 1) * width], NT)
        acc = acc + dot(delta[:, width:], wv[:, h * half : (h + 1) * half], NT)
    low[...] = acc.astype(BF)
    begin(low, out, sems.at[6])
    landed(low, sems.at[6])


def call(body, name, in_specs, out_shapes, scratch, sems, args):
    return pl.pallas_call(
        body,
        name=name,
        in_specs=in_specs,
        out_specs=[HBM] * len(out_shapes),
        out_shape=out_shapes,
        scratch_shapes=[pltpu.VMEM(s, d) for s, d in scratch] + [pltpu.SemaphoreType.DMA((sems,))],
        compiler_params=pltpu.CompilerParams(vmem_limit_bytes=VMEM_BYTES),
        cost_estimate=pl.CostEstimate(flops=COST, bytes_accessed=COST, transcendentals=0),
    )(*args)


def orders(size):
    bits = [1 << k for k in range(size.bit_length() - 1)]
    high = bits[2:][::-1]
    return high + [1, 2], high + [2, 1], [2] + high + [1], [1] + high + [2]


def block_mask(index, order):
    mask = 0
    for k, bit in enumerate(order):
        if (index >> k) & 1:
            mask ^= bit
    return mask


def swap(array, mask):
    size = lax.axis_size("dp")
    return lax.ppermute(array, "dp", [(i, i ^ mask) for i in range(size)])


def swap_core(array):
    return lax.ppermute(array, "tensor", [(0, 1), (1, 0)])


def after(array, *others):
    return lax.optimization_barrier((array, *others))[0]


def join(left, right):
    return jnp.concatenate([left, right], 0)


def gather_blocks(shard, order):
    held = shard[None]
    for mask in order:
        held = join(held, swap(held, mask))
    return held


def scatter_blocks(blocks, order):
    for mask in order[::-1]:
        half = blocks.shape[0] // 2
        blocks = blocks[:half] + swap(blocks[half:], mask)
    return blocks[0]


def in_order(blocks, order, me):
    size = len(blocks)
    place = [0] * size
    for j in range(size):
        place[block_mask(j, order)] = j
    chosen = jnp.array(place)[jnp.arange(size) ^ me]
    return jnp.take(blocks, chosen, axis=0)


def out_of_order(blocks, order, me):
    owners = jnp.array([block_mask(j, order) for j in range(len(blocks))]) ^ me
    return jnp.take(blocks, owners, axis=0)


def extra_columns(shared, pair, up, rows):
    def lanes(array):
        return jnp.pad(array, ((0, 0), (0, 0), (0, LANES - array.shape[2])))

    columns = jnp.concatenate([lanes(shared), lanes(pair), lanes(up)], 1)
    return jnp.pad(columns, ((0, 0), (0, rows - columns.shape[1]), (0, 0)))


def per_device(
    hidden_in,
    lengths,
    labels,
    out_cot,
    input_weight,
    input_bias,
    out_weight,
    out_bias,
    first_gain,
    first_shift,
    up_weight,
    up_bias,
    down_weight,
    down_bias,
    second_gain,
    second_shift,
    pool_weight,
    pool_bias,
    class_weight,
    class_bias,
):
    size = lax.axis_size("dp")
    me = lax.axis_index("dp")
    core = lax.axis_index("tensor")
    length, width = hidden_in.shape[2:]
    rows = width // size
    half = input_weight.shape[2]
    hidden_half = up_weight.shape[1]
    hidden_width = 2 * hidden_half
    classes = class_bias.shape[0]
    pairs = width // LANES
    block = width // BLOCKS
    lower = BLOCKS // 2
    direct = size == BLOCKS
    order_a, order_b, order_u, order_d = orders(size)

    def kernel_masks(order):
        return [block_mask(j, order) if direct else j for j in range(BLOCKS)]

    a_masks, b_masks, u_masks, d_masks = [kernel_masks(o) for o in orders(size)]

    inputs = hidden_in.reshape(2, length, width)
    cotangents = out_cot.reshape(2, length, width)
    info = jnp.concatenate(
        [
            jnp.stack([me if direct else jnp.zeros_like(me), core]).astype(jnp.int32),
            lengths.reshape(-1),
            labels.reshape(-1),
        ]
    )

    pool_half = lax.dynamic_slice_in_dim(pool_weight, core * half, half, 1)
    a_shard = jnp.concatenate([input_weight[0], input_weight[1], pool_half], 1)
    vo_shard = jnp.concatenate([input_weight[2], out_weight.T], 1)
    u_shard = up_weight
    d_shard = down_weight.T
    shared = jnp.concatenate(
        [
            jnp.stack(
                [out_bias, first_gain, first_shift, down_bias, second_gain, second_shift, pool_bias]
            ),
            class_weight.T,
        ],
        0,
    )
    if direct:
        extra = extra_columns(
            shared[None], input_bias.reshape(1, 1, rows), up_bias.reshape(1, 1, 2 * rows), rows
        )
        b_shard = jnp.concatenate([vo_shard, extra[0]], 1)
        a0, b0, u0, d0 = a_shard[None], b_shard[None], u_shard[None], d_shard[None]
        z1, z0 = order_a[0], order_a[1]
        a1, b1, u1, d1 = swap(a0, z1), swap(b0, z1), swap(u0, 2), swap(d0, 1)
        a2, b2 = join(a0, a1), join(b0, b1)
        a2_in, b2_in = swap(a2, z0), swap(b2, z0)
        u2 = after(join(u0, u1), a2, b2)
        u2_in = swap(u2, z1)
        a4, b4 = join(a2, a2_in), join(b2, b2_in)
        a4_in, b4_in = swap(a4, 1), swap(b4, 2)
        d2 = after(join(d0, d1), a4, b4)
        u4 = after(join(u2, u2_in), a4, b4)
        d2_in, u4_in = swap(d2, z1), swap(u4, z0)
        a8, b8 = join(a4, a4_in), join(b4, b4_in)
        a8_in, b8_in = swap(a8, 2), swap(b8, 1)
        d4 = after(join(d2, d2_in), a8, b8)
        u8 = after(join(u4, u4_in), a8, b8)
        d4_in, u8_in = swap(d4, z0), swap(u8, 1)
        d8 = after(join(d4, d4_in), a8_in, b8_in)
        d8_in = swap(d8, 2)
        info = after(info, d8)
        pieces = [(a8, a8_in), (b8, b8_in), (u8, u8_in), (d8, d8_in)]
    else:

        def whole(shard, order):
            return in_order(gather_blocks(shard, order), order, me)

        def cut(array):
            blocks = array.reshape(BLOCKS, block, -1)
            return blocks[:lower], blocks[lower:]

        shared = whole(shared, order_a).transpose(1, 0, 2).reshape(-1, BLOCKS, block)
        pair = whole(input_bias, order_a).transpose(1, 0, 2).reshape(2, BLOCKS, block // 2)
        extra = extra_columns(
            shared.transpose(1, 0, 2),
            pair.transpose(1, 0, 2).reshape(BLOCKS, 1, block),
            whole(up_bias, order_a).reshape(BLOCKS, 1, 2 * block),
            block,
        )
        vo = cut(whole(vo_shard, order_b))
        vo = jnp.concatenate([vo[0], extra[:lower]], 2), jnp.concatenate([vo[1], extra[lower:]], 2)
        pieces = [
            cut(whole(a_shard, order_a)),
            vo,
            cut(whole(u_shard, order_u)),
            cut(whole(d_shard, order_d)),
        ]
    def with_other(lo, hi):
        return lo, hi, swap_core(lo), swap_core(hi)

    qk, vo = with_other(*pieces[0]), with_other(*pieces[1])

    def shape(*dims, dtype=BF):
        return jax.ShapeDtypeStruct(dims, dtype)

    row = shape(length, width)
    wide = shape(length, hidden_width)
    norm = shape(length, width, dtype=F32)
    flat = shape(width, length)
    roots = shape(length, LANES, dtype=F32)
    eight = shape(8, width, dtype=F32)
    vectors = shape(16, width, dtype=F32)
    probs = shape(pairs, 2, length, length)

    def grad(columns):
        return [shape(lower, block, columns)] * 2

    def of(s):
        return (s.shape, s.dtype)

    vmem = pl.BlockSpec(memory_space=pltpu.VMEM)
    part = width + LANES
    slim = shape(length, half)
    halved = shape(length, hidden_half)
    thirds = shape(length, 3 * half)
    q, k, v, att, att_other, p, first, first_t, x_t, x_t_other, normed, root, vec = call(
        functools.partial(attend_kernel, a_masks, b_masks),
        "attend",
        [SCALARS, HBM] + [HBM] * 8,
        [row, row, row, slim, slim, probs, row, flat, flat, flat, norm, roots, vectors],
        [of(row), of(row), ((width, 2 * width), BF), ((width, 2 * part), BF), of(row), of(row), of(row), of(row)]
        + [((2, 2, length, length), BF), of(row), of(flat), of(flat), of(norm), of(roots), of(vectors)]
        + [((width, LANES), F32)],
        17,
        (info, inputs, *qk, *vo),
    )
    (up_lo, up_hi), (down_lo, down_hi) = pieces[2:]
    up_hi, down_hi = after(up_hi, first), after(down_hi, first)
    up = with_other(up_lo, up_hi)
    down = with_other(down_lo, down_hi)
    first_t_in, att_in = swap_core(first_t), swap_core(att_other)
    act, act_other, slope = call(
        functools.partial(up_kernel, u_masks),
        "up",
        [SCALARS, vmem, HBM] + [HBM] * 4,
        [halved, halved, wide],
        [of(row), ((width, hidden_width), BF), of(wide), of(wide)],
        5,
        (info, vec, first, *up),
    )
    act_in = swap_core(act_other)
    block_out, ramp, feed, feed_t, second, sums_two = call(
        functools.partial(ramp_kernel, d_masks, a_masks),
        "ramp",
        [SCALARS, SCALARS, vmem] + [HBM] * 12,
        [row, eight, row, flat, norm, eight],
        [of(wide), of(row), of(row), ((width, hidden_width), BF), ((width, width), BF), of(norm), of(roots)]
        + [of(row), of(row), of(flat), of(norm), of(eight), of(eight)],
        11,
        (info, class_bias.astype(F32), vec, cotangents, act, act_other, first, *down, *qk),
    )
    feed_t_in = swap_core(feed_t)
    delta, delta_other = call(
        functools.partial(hidden_kernel, d_masks),
        "hidden",
        [SCALARS] + [HBM] * 6,
        [halved, halved],
        [of(row), of(wide), ((width, hidden_width), BF), of(wide)],
        5,
        (info, feed, slope, *down),
    )
    delta_in = swap_core(delta_other)
    down_grad = call(
        functools.partial(down_grad_kernel, d_masks),
        "down_grad",
        [SCALARS] + [HBM] * 4,
        grad(hidden_half),
        [of(flat), of(flat), of(halved), of(halved), ((width, hidden_half), BF)],
        5,
        (info, feed_t, feed_t_in, act, act_in),
    )
    *up_grad, up_sums = call(
        functools.partial(up_grad_kernel, b_masks),
        "up_grad",
        [SCALARS] + [HBM] * 4,
        grad(hidden_half) + [shape(1, hidden_half, dtype=F32)],
        [of(flat), of(flat), of(halved), of(halved), ((width, hidden_half), BF), ((1, hidden_half), F32)],
        6,
        (after(info, down_grad[0]), first_t, first_t_in, delta, delta_in),
    )

    def first_hop(pieces, order):
        if direct:
            return swap(pieces[1], order[-1])

    def spread(pieces, arrived, order):
        if direct:
            return scatter_blocks(pieces[0] + arrived, order[:-1])
        return scatter_blocks(out_of_order(join(*pieces).reshape(size, rows, -1), order, me), order)

    down_arrived = first_hop(down_grad, order_d)
    pair = jnp.stack([ramp[:4], swap_core(ramp[:4])])
    total, datt, branch_t, sums_one = call(
        functools.partial(branch_kernel, u_masks, b_masks),
        "branch",
        [SCALARS, vmem, vmem] + [HBM] * 13,
        [norm, row, flat, eight],
        [of(wide), ((width, hidden_width), BF), ((width, width), BF), of(norm), of(norm), of(roots)]
        + [of(row), of(flat), of(row), of(eight)],
        11,
        (after(info, up_grad[0], pair), vec, sums_two, delta, delta_other, second, normed, root, *up, *vo),
    )
    up_arrived = first_hop(up_grad, order_b)
    branch_t_in, sums_in = swap_core(branch_t), swap_core(sums_one)
    dqkv, dqkv_other = call(
        back_kernel,
        "back",
        [HBM] * 7,
        [thirds, thirds],
        [of(row), of(row), of(row), of(row), of(row)]
        + [((2, 2, length, length), BF), of(row), of(row), of(row)],
        13,
        (q, k, v, att, att_other, datt, p),
    )
    dqkv_in = swap_core(dqkv_other)
    (input_delta,) = call(
        functools.partial(input_kernel, a_masks, b_masks),
        "input",
        [SCALARS] + [HBM] * 11,
        [row],
        [of(thirds), of(thirds), of(norm), ((width, 2 * width), BF), ((width, width), BF), of(row)],
        7,
        (info, dqkv, dqkv_other, total, *qk, *vo),
    )
    if direct:
        down_arrived, up_arrived = lax.optimization_barrier((down_arrived, up_arrived))
    input_grads = call(
        functools.partial(input_grad_kernel, a_masks, b_masks),
        "input_grad",
        [SCALARS, vmem, vmem, vmem] + [HBM] * 8,
        grad(width) + grad(part),
        [of(flat), of(flat), of(thirds), of(thirds), of(flat), of(flat), of(slim), of(slim)]
        + [((width, width), BF), ((width, part), BF), ((width, LANES), F32)],
        10,
        (after(info, input_delta), sums_one, sums_in, up_sums, x_t, x_t_other, dqkv, dqkv_in)
        + (branch_t, branch_t_in, att, att_in),
    )
    qk_grad, vo_grad = input_grads[:2], input_grads[2:]
    qk_arrived, vo_arrived = first_hop(qk_grad, order_a), first_hop(vo_grad, order_b)
    down_share = spread(down_grad, down_arrived, order_d)
    up_share = spread(up_grad, up_arrived, order_b)
    qk_share = spread(qk_grad, qk_arrived, order_a)
    if direct:
        vo_share = spread(vo_grad, vo_arrived, order_b)
        extra_share = vo_share[:, width:]
        vector_grads = extra_share[:6, :rows]
        pair_share = extra_share[PAIR_ROW, :rows].reshape(2, rows // 2)
        up_bias_share = extra_share[UP_ROW, : 2 * rows]
    else:
        vo_share = spread([piece[:, :, :width] for piece in vo_grad], None, order_b)
        extra_sum = lax.psum(join(*[piece[:, :, width:] for piece in vo_grad]).astype(F32), "dp")

        def own(array, count):
            return lax.dynamic_slice_in_dim(array, me * count, count, array.ndim - 1)

        vector_grads = own(extra_sum[:, :6, :block].transpose(1, 0, 2).reshape(6, width), rows)
        pair_sums = extra_sum[:, PAIR_ROW, :block].reshape(BLOCKS, 2, block // 2)
        pair_share = own(pair_sums.transpose(1, 0, 2).reshape(2, half), rows // 2)
        up_bias_share = own(extra_sum[:, UP_ROW, : 2 * block].reshape(-1), 2 * rows)

    pair_logits = pair[:, 3, LANES : LANES + classes]
    logits_out = jnp.where(core == 0, pair_logits, pair_logits[::-1])
    if direct:
        ramps = pair
        for mask, previous in zip(order_a, (up_sums, datt, dqkv, input_delta)):
            ramps = join(ramps, swap(after(ramps, previous), mask))
    else:
        ramps = lax.all_gather(pair, "dp", axis=0, tiled=True)
    logit_deltas = ramps[:, 3, :classes]
    own_columns = lax.dynamic_slice_in_dim(ramps[:, :3], me * rows, rows, 2)
    pool_grad = dot(own_columns[:, 0].astype(BF), ramps[:, 2].astype(BF), TN)
    pool_bias_grad = jnp.sum(own_columns[:, 2], 0)
    class_grad = lax.dot_general(
        own_columns[:, 1], logit_deltas, (TN, ((), ())), precision=lax.Precision.HIGHEST
    )
    class_bias_grad = jnp.sum(logit_deltas, 0)

    blocks_out = lax.all_gather(block_out, "tensor", axis=0)[:, None]
    input_grad = lax.all_gather(input_delta, "tensor", axis=0)[:, None]
    vector_grads = vector_grads.astype(F32)
    return (
        blocks_out,
        logits_out[:, None],
        input_grad,
        jnp.stack([qk_share[:, :half], qk_share[:, half:], vo_share[:, :half]]).astype(F32),
        pair_share.astype(F32),
        vo_share[:, half:width].T.astype(F32),
        vector_grads[0],
        vector_grads[1],
        vector_grads[2],
        up_share.astype(F32),
        up_bias_share.astype(F32),
        down_share.T.astype(F32),
        vector_grads[5],
        vector_grads[3],
        vector_grads[4],
        pool_grad,
        pool_bias_grad,
        class_grad,
        class_bias_grad,
    )


def solution(mesh):
    placed = (
        P(None, "dp", None, None),
        P(None, "dp"),
        P(None, "dp"),
        P(None, "dp", None, None),
        P(None, "dp", "tensor"),
        P(None, ("tensor", "dp")),
        P("tensor", "dp"),
        P("dp"),
        P("dp"),
        P("dp"),
        P("dp", "tensor"),
        P(("tensor", "dp")),
        P("tensor", "dp"),
        P("dp"),
        P("dp"),
        P("dp"),
        P("dp", None),
        P("dp"),
        P("dp", None),
        P(),
    )
    return jax.shard_map(
        per_device,
        mesh=mesh,
        in_specs=placed,
        out_specs=(
            P(None, "dp", None, None),
            P(None, "dp", None),
            P(None, "dp", None, None),
            P(None, "dp", "tensor"),
            P(None, ("tensor", "dp")),
            P("tensor", "dp"),
            P("dp"),
            P("dp"),
            P("dp"),
            P("dp", "tensor"),
            P(("tensor", "dp")),
            P("tensor", "dp"),
            P("dp"),
            P("dp"),
            P("dp"),
            P("dp", None),
            P("dp"),
            P("dp", None),
            P(),
        ),
        check_vma=False,
    )
```

```python
import functools
import math

import jax
import jax.numpy as jnp
from jax import lax
from jax.experimental import pallas as pl
from jax.experimental.pallas import tpu as pltpu
from jax.sharding import PartitionSpec as P

HD = 64
LANES = 128
BLOCKS = 16
EPS = 1e-06
BF = jnp.bfloat16
F32 = jnp.float32
NN = ((1,), (0,))
NT = ((1,), (1,))
TN = ((0,), (0,))
HBM = pl.BlockSpec(memory_space=pltpu.HBM)
SCALARS = pl.BlockSpec(memory_space=pltpu.SMEM)
VMEM = pl.BlockSpec(memory_space=pltpu.VMEM)
MIB = 1024 * 1024
FLOPS_PER_MICROSECOND = 1_150_000_000

OUT_B, GAIN_1, SHIFT_1, DOWN_B, GAIN_2, SHIFT_2, POOL_B, CLASS, QUERY_B, VALUE_B, UP_B = (
    0, 1, 2, 3, 4, 5, 6, 7, 10, 11, 12,
)
SHARED, PAIR_ROW, UP_ROW, CLASS_ROW = 10, 10, 11, 12


def dot(left, right, dims=NN):
    return lax.dot_general(left, right, (dims, ((), ())), preferred_element_type=F32)


def begin(source, target, sem):
    copy = pltpu.make_async_copy(source, target, sem)
    copy.start()
    return copy


def row_block(me, mask, rows):
    return pl.ds(pl.multiple_of((me ^ mask) * rows, 16), rows)


def load(pieces, target, sems, columns=None):
    cut, width = pieces[0].shape
    start, width = columns or (0, width)
    for i, piece in enumerate(pieces):
        begin(piece.at[:, pl.ds(start, width)], target.at[i // 2, pl.ds(i % 2 * cut, cut), :], sems.at[i])


def landed(target, sem):
    pltpu.make_async_copy(target, target, sem).wait()


def loaded(target, h, sems):
    cut = target.shape[1] // 2
    for i in range(2):
        landed(target.at[h, pl.ds(i * cut, cut), :], sems.at[2 * h + i])


def to_blocks(source, target, masks, me):
    rows = source.shape[0] // BLOCKS
    for j in range(BLOCKS):
        target[j * rows : (j + 1) * rows, :] = source[row_block(me, masks[j], rows), :]


def to_rows(source, target, masks, me):
    rows = target.shape[0] // BLOCKS
    for j in range(BLOCKS):
        target[row_block(me, masks[j], rows), :] = source[j * rows : (j + 1) * rows, :]


def row_product(matrices, rights):
    return sum(dot(matrices[h], rights[h], NT) for h in range(2))


def pair_product(lefts, rights, lower, upper):
    cut = lefts[0].shape[0] // 2
    columns = rights[0].shape[1]
    for i, target in enumerate((lower, upper)):
        span = slice(i * cut, (i + 1) * cut)
        total = dot(lefts[0][span, :], rights[0][...]) + dot(lefts[1][span, :], rights[1][...])
        target[:, 0:columns] = total.astype(BF)


def mean(array):
    return jnp.mean(array, -1, keepdims=True)


def normalize(total):
    centered = total - mean(total)
    root = lax.rsqrt(mean(centered * centered) + EPS)
    return centered * root, root


def norm_backward(delta, normed, root, gain):
    scaled = delta * gain
    return root * (scaled - mean(scaled) - normed * mean(scaled * normed))


def column_sum(array):
    return jnp.sum(array, 0, keepdims=True)


def unpack_vectors(extra, vec, h):
    width = vec.shape[1]
    rows, part = width // BLOCKS, width // BLOCKS // 2
    for b in range(BLOCKS):
        own = extra[b * rows : b * rows + 16, :]
        if h == 0:
            vec[0:SHARED, b * rows : (b + 1) * rows] = own[0:SHARED, 0:rows]
        at = h * width // 2 + b * part
        vec[QUERY_B : QUERY_B + 1, at : at + part] = own[PAIR_ROW : PAIR_ROW + 1, 0:part]
        vec[VALUE_B : VALUE_B + 1, at : at + part] = own[PAIR_ROW : PAIR_ROW + 1, part:rows]
        row, at = UP_B + 2 * h + b // (BLOCKS // 2), b % (BLOCKS // 2) * 2 * rows
        vec[row : row + 1, at : at + 2 * rows] = own[UP_ROW : UP_ROW + 1, 0 : 2 * rows]


def pack_vectors(sums, query, value, up, extra):
    width = sums.shape[1]
    rows, part = width // BLOCKS, width // BLOCKS // 2
    extra[...] = jnp.zeros(extra.shape, F32)
    for b in range(BLOCKS):
        top = b * rows
        extra[top : top + SHARED, 0:rows] = sums[0:SHARED, b * rows : (b + 1) * rows]
        at = b * part
        extra[top + PAIR_ROW : top + PAIR_ROW + 1, 0:part] = query[:, at : at + part]
        extra[top + PAIR_ROW : top + PAIR_ROW + 1, part:rows] = value[:, at : at + part]
        at = b * 2 * rows
        extra[top + UP_ROW : top + UP_ROW + 1, 0 : 2 * rows] = up[:, at : at + 2 * rows]
        extra[top + CLASS_ROW : top + CLASS_ROW + 1, :] = sums[SHARED : SHARED + 1, 0:LANES]


def prepare_kernel(masks_p, masks_q, info, hidden, *refs):
    outs, (rows_p, rows_q, x, other_x, flip, held, sems) = refs[0:4], refs[4:]
    me, core = info[0], info[1]
    begin(hidden.at[core], x, sems.at[0])
    begin(hidden.at[1 - core], other_x, sems.at[1])
    for i, source in enumerate((x, other_x)):
        landed(source, sems.at[i])
        flip[...] = source[...].T
        for n, masks in enumerate((masks_p, masks_q)):
            to_blocks(flip, held.at[2 * i + n], masks, me)
            begin(held.at[2 * i + n], outs[2 * i + n], sems.at[2 + 2 * i + n])
    rows_p[...] = held[0].T
    rows_q[...] = held[1].T
    for i in range(4):
        landed(held.at[i], sems.at[2 + i])


def attend_kernel(masks_p, masks_q, info, hidden, rows_p, rows_q, *refs):
    qk, vo = refs[0:4], refs[4:8]
    q, k, v, att_own, att_other, p, first, first_p = refs[8:16]
    normed, root, vec = refs[16:19]
    x, wa, wb, att, flip, wide, extra, sems = refs[19:]
    me, core = info[0], info[1]
    count = info[2 + core]
    length, width = x.shape
    half = width // 2
    load(vo, wb, sems.at[pl.ds(2, 4)])
    load(qk, wa, sems.at[pl.ds(6, 4)])
    begin(hidden.at[core], x, sems.at[0])
    rows = width // BLOCKS
    for h in range(2):
        loaded(wb, h, sems.at[pl.ds(2, 4)])
        for j in range(BLOCKS):
            piece = wb[h, j * rows : (j + 1) * rows, width:]
            extra[row_block(me, masks_q[j], rows), :] = piece.astype(F32)
        unpack_vectors(extra, vec, h)
    for h in range(2):
        own = slice(h * half, (h + 1) * half)
        loaded(wa, h, sems.at[pl.ds(6, 4)])
        both = dot(rows_p[...], wa[h])
        q[:, own] = (both[:, :half] + vec[QUERY_B : QUERY_B + 1, own]).astype(BF) * (1.0 / math.sqrt(HD))
        k[:, own] = both[:, half:].astype(BF)
        v[:, own] = (dot(rows_q[...], wb[h, :, 0:half]) + vec[VALUE_B : VALUE_B + 1, own]).astype(BF)
    keys = lax.broadcasted_iota(jnp.int32, (1, length), 1)
    bias = jnp.where(keys < count, 0.0, -1e30).astype(F32)
    lane = lax.broadcasted_iota(jnp.int32, (1, LANES), 1)
    for pair in range(width // LANES):
        cols = slice(pair * LANES, (pair + 1) * LANES)
        q_pair, k_pair, v_pair = q[:, cols], k[:, cols], v[:, cols]
        acc = None
        for a in range(2):
            mine = (lane < HD) if a == 0 else (lane >= HD)
            scores = dot(jnp.where(mine, q_pair, 0.0).astype(BF), k_pair, NT) + bias
            weights = jnp.exp(scores - jnp.max(scores, -1, keepdims=True))
            probs = (weights * (1.0 / jnp.sum(weights, -1, keepdims=True))).astype(BF)
            p[pair, a] = probs
            term = dot(probs, jnp.where(mine, v_pair, 0.0).astype(BF))
            acc = term if acc is None else acc + term
        att[:, cols] = acc.astype(BF)
    att_own[...] = att[:, :half]
    att_other[...] = att[:, half:]
    to_rows(row_product([wb[h, :, half:width] for h in range(2)], (att[:, :half], att[:, half:])), wide, masks_q, me)
    landed(x, sems.at[0])
    own_normed, own_root = normalize(x[...].astype(F32) + wide[...].T + vec[OUT_B : OUT_B + 1, :])
    normed[...] = own_normed
    root[...] = jnp.broadcast_to(own_root, root.shape)
    low = (own_normed * vec[GAIN_1 : GAIN_1 + 1, :] + vec[SHIFT_1 : SHIFT_1 + 1, :]).astype(BF)
    first[...] = low
    flip[...] = low.T
    to_blocks(flip, first_p, masks_p, me)


def up_kernel(vec, first_p, *refs):
    pieces = refs[0:4]
    active, other_active, slope, w, sems = refs[4:]
    width = first_p.shape[0]
    half = active.shape[1]
    load(pieces, w, sems, (0, half))
    left = first_p[...].T
    chunk = 256
    for h, target in enumerate((active, other_active)):
        loaded(w, h, sems)
        for c in range(half // chunk):
            cols = slice(c * chunk, (c + 1) * chunk)
            at = h * half + c * chunk
            row, lane = UP_B + at // width, at % width
            hidden = dot(left, w[h, :, cols]) + vec[row : row + 1, lane : lane + chunk]
            cdf = 0.5 + 0.5 * lax.erf(hidden * math.sqrt(0.5))
            density = jnp.exp(hidden * hidden * -0.5) * (1.0 / math.sqrt(2.0 * math.pi))
            target[:, cols] = (hidden * cdf).astype(BF)
            slope[:, at : at + chunk] = (cdf + hidden * density).astype(BF)


def ramp_kernel(masks, pool_masks, info, class_bias, vec, cotangent, active, other_active, first, *refs):
    pieces, pool_pieces = refs[0:4], refs[4:8]
    block, ramp, feed_r, second, grads, w = refs[8:14]
    cot, right, pool, flip, wide, slim, z, sems = refs[14:]
    me, core = info[0], info[1]
    count, label = info[2 + core], info[4 + core]
    length, width = first.shape
    half = width // 2
    cut = w.shape[2]
    load(pieces, w, sems.at[pl.ds(0, 4)])
    begin(other_active, right, sems.at[8])
    load(pool_pieces, pool, sems.at[pl.ds(4, 4)], (cut, half))
    begin(cotangent.at[core], cot, sems.at[9])
    loaded(w, 0, sems)
    part = dot(w[0], active[...], NT)
    landed(right, sems.at[8])
    loaded(w, 1, sems)
    to_rows(part + dot(w[1], right[...], NT), wide, masks, me)
    total = first[...].astype(F32) + wide[...].T + vec[DOWN_B : DOWN_B + 1, :]
    gain, shift = vec[GAIN_2 : GAIN_2 + 1, :], vec[SHIFT_2 : SHIFT_2 + 1, :]
    normed, root = normalize(total)
    ids = lax.broadcasted_iota(jnp.int32, (length, 1), 0)
    block[...] = jnp.where(ids < count, normed * gain + shift, 0.0).astype(BF)
    for h in range(2):
        loaded(pool, h, sems.at[pl.ds(4, 4)])
    head = (normed[0:8, :] * gain + shift).astype(BF)
    sides = [pl.ds(pl.multiple_of(side * half, LANES), half) for side in (core, 1 - core)]
    slim[:, 0:8] = head.astype(F32).T
    for j in range(BLOCKS):
        at = slice(j * (width // BLOCKS), (j + 1) * (width // BLOCKS))
        slim[at, LANES : LANES + 8] = slim[row_block(me, pool_masks[j], width // BLOCKS), 0:8]
    head_t = slim[:, LANES : LANES + 8].astype(BF)
    for h in range(2):
        z[:, sides[h]] = dot(head_t, pool[h], TN)
    pooled_wide = jnp.tanh(z[...] + vec[POOL_B : POOL_B + 1, :])
    pooled = pooled_wide.astype(BF).astype(F32)
    class_rows = [vec[CLASS + c : CLASS + c + 1, :] for c in range(3)]
    logits = [
        jnp.sum(pooled * class_rows[c], -1, keepdims=True) + class_bias[c] for c in range(3)
    ]
    top = jnp.maximum(jnp.maximum(logits[0], logits[1]), logits[2])
    powers = [jnp.exp(l - top) for l in logits]
    power_sum = powers[0] + powers[1] + powers[2]
    deltas = [powers[c] / power_sum - jnp.where(label == c, 1.0, 0.0) for c in range(3)]
    pre = sum(deltas[c] * class_rows[c] for c in range(3)) * (1.0 - pooled_wide * pooled_wide)
    pre_high = pre.astype(BF)
    z[0:8, :] = pre_high.astype(F32)
    high = [z[:, side].astype(BF) for side in sides]
    z[0:8, :] = pre - pre_high.astype(F32)
    low = [z[:, side].astype(BF) for side in sides]
    slim[:, 0:8] = row_product(pool, high) + row_product(pool, low)
    for j in range(BLOCKS):
        at = slice(j * (width // BLOCKS), (j + 1) * (width // BLOCKS))
        slim[row_block(me, pool_masks[j], width // BLOCKS), LANES : LANES + 8] = slim[at, 0:8]
    head_delta = slim[:, LANES : LANES + 8].T[0:1, :]
    lane = lax.broadcasted_iota(jnp.int32, (1, width), 1)
    tail = jnp.zeros((1, width), F32)
    for c in range(3):
        tail = jnp.where(lane == c, deltas[c][0:1], tail)
        tail = jnp.where(lane == LANES + c, logits[c][0:1], tail)
    ramp[0:1, :] = head[0:1, :].astype(F32)
    ramp[1:2, :] = pooled[0:1, :]
    ramp[2:3, :] = pre[0:1, :]
    ramp[3:4, :] = tail
    ramp[4:8, :] = jnp.zeros((4, width), F32)
    landed(cot, sems.at[9])
    delta = jnp.where(ids < count, cot[...].astype(F32), 0.0) + jnp.where(ids == 0, head_delta, 0.0)
    grads[0:1, :] = column_sum(delta * normed)
    grads[1:2, :] = column_sum(delta)
    dsecond = norm_backward(delta, normed, root, gain)
    grads[2:3, :] = column_sum(dsecond)
    grads[3:4, :] = pre[0:1, :]
    for c in range(3):
        grads[4 + c : 5 + c, :] = deltas[c][0:1] * pooled[0:1, :]
    grads[7:8, :] = tail
    second[...] = dsecond
    flip[...] = dsecond.astype(BF).T
    to_blocks(flip, feed_r, masks, me)


def hidden_kernel(feed_r, slope, w, delta, other_delta):
    half = delta.shape[1]
    left = feed_r[...].T
    chunk = 512
    for h, target in ((1, other_delta), (0, delta)):
        for c in range(half // chunk):
            cols = slice(c * chunk, (c + 1) * chunk)
            at = h * half + c * chunk
            target[:, cols] = (dot(left, w[h, :, cols]) * slope[:, at : at + chunk].astype(F32)).astype(BF)


def down_grad_kernel(masks, info, ramp, ramp_other, left_in, left_other_in, right, right_other_in, *refs):
    lower, upper, logits, left, left_other, right_other, wide, slim, sems = refs
    loads = ((left_in, left), (left_other_in, left_other), (right_other_in, right_other))
    for i, (source, target) in enumerate(loads):
        begin(source, target, sems.at[i])
    width, columns = left.shape[0], right.shape[1]
    half = width // 2
    own = pl.ds(pl.multiple_of(info[1] * half, LANES), half)
    classes = logits.shape[1]
    pair = [r[3:4, LANES : LANES + classes] for r in (ramp, ramp_other)]
    logits[0:1, :] = jnp.where(info[1] == 0, pair[0], pair[1])
    logits[1:2, :] = jnp.where(info[1] == 0, pair[1], pair[0])
    none = jnp.zeros((14, width), F32)
    wide[...] = jnp.concatenate([ramp[0:1, :], ramp_other[0:1, :], none], 0).T
    to_blocks(wide, slim, masks, info[0])
    heads = slim[...].astype(BF)
    pres = jnp.concatenate([ramp[2:3, own], ramp_other[2:3, own], none[:, :half]], 0).astype(BF)
    for i, target in enumerate((lower, upper)):
        target[:, columns:] = dot(heads[i * half : (i + 1) * half], pres).astype(BF)
    for i, (_, target) in enumerate(loads):
        landed(target, sems.at[i])
    pair_product((left, left_other), (right, right_other), lower, upper)


def up_grad_kernel(left, left_other, right, right_other_in, *refs):
    lower, upper, sums, right_other, sems = refs
    begin(right_other_in, right_other, sems.at[0])
    own_sum = column_sum(right[...].astype(F32))
    landed(right_other, sems.at[0])
    sums[...] = own_sum + column_sum(right_other[...].astype(F32))
    pair_product((left, left_other), (right, right_other), lower, upper)


def branch_kernel(masks_p, masks_q, info, vec, sums_in, delta, other_delta, second, normed, root, wu, *refs):
    vo = refs[0:4]
    total_out, datt, branch_p, grads = refs[4:8]
    wo, right, flip, rows_q, wide, sems = refs[8:]
    me = info[0]
    width = normed.shape[1]
    half = width // 2
    begin(other_delta, right, sems.at[4])
    load(vo, wo, sems.at[pl.ds(0, 4)], (half, half))
    gain = vec[GAIN_1 : GAIN_1 + 1, :]
    part = dot(wu[0], delta[...], NT)
    landed(right, sems.at[4])
    to_rows(part + dot(wu[1], right[...], NT), wide, masks_p, me)
    dfirst = second[...] + wide[...].T
    own_normed = normed[...]
    total = norm_backward(dfirst, own_normed, root[:, 0:1], gain)
    total_out[...] = total
    flip[...] = total.astype(BF).T
    to_blocks(flip, branch_p, masks_p, me)
    to_blocks(flip, rows_q, masks_q, me)
    grads[0:1, :] = column_sum(total)
    grads[1:2, :] = column_sum(dfirst * own_normed)
    grads[2:3, :] = column_sum(dfirst)
    grads[3 : SHARED + 1, :] = sums_in[...]
    grads[SHARED + 1 :, :] = jnp.zeros((grads.shape[0] - SHARED - 1, width), F32)
    left = rows_q[...].T
    for h in range(2):
        loaded(wo, h, sems)
        datt[:, h * half : (h + 1) * half] = dot(left, wo[h]).astype(BF)


def back_kernel(q, k, v, att_own, att_other, datt, p, *refs):
    own_out, other_out = refs[0:2]
    att, dq, dk, dv = refs[2:]
    length, width = q.shape
    half = width // 2
    att[:, :half] = att_own[...]
    att[:, half:] = att_other[...]
    lane = lax.broadcasted_iota(jnp.int32, (1, LANES), 1)
    pairs = width // LANES

    for pair in range(pairs):
        cols = slice(pair * LANES, (pair + 1) * LANES)
        do = datt[:, cols]
        product = do.astype(F32) * att[:, cols].astype(F32)
        k_pair, v_pair = k[:, cols], v[:, cols]
        q_t = q[:, cols].T
        do_t = do.T
        dq_sum = None
        dk_parts, dv_parts = [], []
        for a in range(2):
            mine = (lane < HD) if a == 0 else (lane >= HD)
            shift = jnp.sum(jnp.where(mine, product, 0.0), -1, keepdims=True)
            dprobs = dot(jnp.where(mine, do, 0.0).astype(BF), v_pair, NT)
            probs = p[pair, a]
            dscores = (probs.astype(F32) * (dprobs - shift)).astype(BF)
            term = dot(dscores, jnp.where(mine, k_pair, 0.0).astype(BF))
            dq_sum = term if dq_sum is None else dq_sum + term
            own = slice(a * HD, (a + 1) * HD)
            dk_parts.append(dot(q_t[own], dscores))
            dv_parts.append(dot(do_t[own], probs))
        dq[:, cols] = (dq_sum * (1.0 / math.sqrt(HD))).astype(BF)
        dk[:, cols] = jnp.concatenate(dk_parts, 0).T.astype(BF)
        dv[:, cols] = jnp.concatenate(dv_parts, 0).T.astype(BF)
    for h, out in ((1, other_out), (0, own_out)):
        for i, source in enumerate((dq, dk, dv)):
            out[:, i * half : (i + 1) * half] = source[:, h * half : (h + 1) * half]


def out_grad_kernel(branch_t, other_branch_t, att, other_att, grad):
    grad[...] = (dot(branch_t[...], att[...]) + dot(other_branch_t[...], other_att[...])).astype(BF)


def input_grad_kernel(
    masks_p, info, sums_in, sums_other, up_sums, x_p, x_q, other_p, other_q, delta, other_delta, out_grad, *refs
):
    qk_pieces, vo_pieces = refs[0:2], refs[2:4]
    extra = refs[4]
    me = info[0]
    width = x_p.shape[0]
    half = width // 2
    rows = width // BLOCKS
    columns = column_sum(delta[...].astype(F32)) + column_sum(other_delta[...].astype(F32))
    pack_vectors(sums_in[...] + sums_other[...], columns[:, :half], columns[:, width:], up_sums[...], extra)
    for i, target in enumerate(vo_pieces):
        span = slice(i * half, (i + 1) * half)
        total = dot(x_p[span, :], delta[:, width:]) + dot(other_p[span, :], other_delta[:, width:])
        target[:, 0:half] = total.astype(BF)
        target[:, half:width] = out_grad[span, :]
        for j in range(BLOCKS // 2):
            at = row_block(me, masks_p[i * (BLOCKS // 2) + j], rows)
            target[j * rows : (j + 1) * rows, width:] = extra[at, :].astype(BF)
    pair_product((x_q, other_q), (delta.at[:, pl.ds(0, width)], other_delta.at[:, pl.ds(0, width)]), *qk_pieces)


def hop_kernel(*refs):
    sent, kept = refs[-2:]
    at = 0
    for own, arrived in zip(refs[0:-2:2], refs[1:-2:2]):
        half, _, width = sent.shape[0], 0, own.shape[2]
        cols = slice(at, at + width)
        sent[:, :, cols] = own[half:] + arrived[half:]
        kept[:, :, cols] = own[:half] + arrived[:half]
        at += width


def finish_kernel(kept, arrived, input_out, out_out, pair_out, up_out, class_bias_out, class_out, *vectors):
    share = kept[0].astype(F32) + arrived[0].astype(F32)
    rows, half = input_out.shape[1:]
    for i in range(3):
        input_out[i] = share[:, i * half : (i + 1) * half]
    out_out[...] = share[:, 3 * half : 4 * half].T
    extra = share[:, 4 * half :]
    for i, target in enumerate(vectors):
        target[...] = extra[i : i + 1, 0:rows]
    pair_out[0:1, :] = extra[PAIR_ROW : PAIR_ROW + 1, 0 : rows // 2]
    pair_out[1:2, :] = extra[PAIR_ROW : PAIR_ROW + 1, rows // 2 : rows]
    up_out[...] = extra[UP_ROW : UP_ROW + 1, 0 : 2 * rows]
    class_bias_out[...] = extra[CLASS_ROW : CLASS_ROW + 1, 0 : class_bias_out.shape[1]]
    class_out[...] = extra[:, 0:rows].T[:, len(vectors) : SHARED]


def arrange_kernel(info, block_own, block_other, grad_own, grad_other, block_out, grad_out, held, sems):
    core = info[1]
    moves = (
        (block_own, block_out, core),
        (block_other, block_out, 1 - core),
        (grad_own, grad_out, core),
        (grad_other, grad_out, 1 - core),
    )
    for i, (source, _, _) in enumerate(moves):
        begin(source, held.at[i], sems.at[i])
    for i, (_, target, side) in enumerate(moves):
        landed(held.at[i], sems.at[i])
        begin(held.at[i], target.at[side], sems.at[4 + i])
    for i in range(4):
        landed(held.at[i], sems.at[4 + i])


def input_kernel(masks_p, masks_q, info, own, other, total, *refs):
    qk, vo = refs[0:4], refs[4:8]
    out, wa, wv, wide, wide_v, sems = refs[8:]
    me = info[0]
    width = total.shape[1]
    half = width // 2
    load(vo, wv, sems.at[pl.ds(0, 4)], (0, half))
    load(qk, wa, sems.at[pl.ds(4, 4)])
    for h in range(2):
        loaded(wv, h, sems.at[pl.ds(0, 4)])
    to_rows(row_product(wv, (own[:, width:], other[:, width:])), wide_v, masks_q, me)
    for h in range(2):
        loaded(wa, h, sems.at[pl.ds(4, 4)])
    to_rows(row_product(wa, (own[:, :width], other[:, :width])), wide, masks_p, me)
    out[...] = (total[...] + (wide[...] + wide_v[...]).T).astype(BF)


def costing(micros):
    return pl.CostEstimate(flops=micros * FLOPS_PER_MICROSECOND, bytes_accessed=1024, transcendentals=0)


def call(body, name, micros, mib, in_specs, outs, scratch, sems, args):
    return pl.pallas_call(
        body,
        name=name,
        in_specs=in_specs,
        out_specs=[spec for _, spec in outs],
        out_shape=[shape for shape, _ in outs],
        scratch_shapes=[pltpu.VMEM(s, d) for s, d in scratch] + [pltpu.SemaphoreType.DMA((sems,))] * (sems > 0),
        compiler_params=pltpu.CompilerParams(vmem_limit_bytes=mib * MIB),
        cost_estimate=costing(micros),
    )(*args)


def orders(size):
    bits = [1 << k for k in range(size.bit_length() - 1)]
    high = bits[2:][::-1]
    x_last, y_last = high + [2, 1], high + [1, 2]
    return (x_last, y_last, x_last, [1] + high + [2]), (y_last, x_last, x_last, [1] + high + [2])


def block_mask(index, order):
    mask = 0
    for k, bit in enumerate(order):
        if (index >> k) & 1:
            mask ^= bit
    return mask


def swap(array, mask):
    size = lax.axis_size("dp")
    return lax.ppermute(array, "dp", [(i, i ^ mask) for i in range(size)])


def swap_core(array):
    return lax.ppermute(array, "tensor", [(0, 1), (1, 0)])


def after(array, *others):
    return lax.optimization_barrier((array, *others))[0]


def join(left, right):
    return jnp.concatenate([left, right], 0)


def gather_blocks(shard, order):
    held = shard[None]
    for mask in order:
        held = join(held, swap(held, mask))
    return held


def hop(blocks, arrived):
    half = blocks.shape[0] // 2
    return blocks[half:] + arrived[half:], blocks[:half] + arrived[:half]


def scatter_blocks(blocks, order):
    for mask in order[::-1]:
        half = blocks.shape[0] // 2
        blocks = blocks[:half] + swap(blocks[half:], mask)
    return blocks[0]


def in_order(blocks, order, me):
    size = len(blocks)
    place = [0] * size
    for j in range(size):
        place[block_mask(j, order)] = j
    chosen = jnp.array(place)[jnp.arange(size) ^ me]
    return jnp.take(blocks, chosen, axis=0)


def out_of_order(blocks, order, me):
    owners = jnp.array([block_mask(j, order) for j in range(len(blocks))]) ^ me
    return jnp.take(blocks, owners, axis=0)


def extra_columns(shared, pair, up, rows):
    def lanes(array):
        return jnp.pad(array, ((0, 0), (0, 0), (0, LANES - array.shape[2])))

    columns = jnp.concatenate([lanes(shared), lanes(pair), lanes(up)], 1)
    return jnp.pad(columns, ((0, 0), (0, rows - columns.shape[1]), (0, 0)))


def per_device(
    hidden_in,
    lengths,
    labels,
    out_cot,
    input_weight,
    input_bias,
    out_weight,
    out_bias,
    first_gain,
    first_shift,
    up_weight,
    up_bias,
    down_weight,
    down_bias,
    second_gain,
    second_shift,
    pool_weight,
    pool_bias,
    class_weight,
    class_bias,
):
    size = lax.axis_size("dp")
    me = lax.axis_index("dp")
    core = lax.axis_index("tensor")
    length, width = hidden_in.shape[2:]
    rows = width // size
    half = input_weight.shape[2]
    hidden_half = up_weight.shape[1]
    hidden_width = 2 * hidden_half
    classes = class_bias.shape[0]
    pairs = width // LANES
    block = width // BLOCKS
    lower = BLOCKS // 2
    direct = size == BLOCKS
    (order_a, order_b, order_u, order_d), (back_a, back_b, back_u, back_d) = orders(size)

    def kernel_masks(order):
        return [block_mask(j, order) if direct else j for j in range(BLOCKS)]

    (a_masks, b_masks, u_masks, d_masks), back_masks = [[kernel_masks(o) for o in part] for part in orders(size)]

    inputs = hidden_in.reshape(2, length, width)
    cotangents = out_cot.reshape(2, length, width)
    info = jnp.concatenate(
        [
            jnp.stack([me if direct else jnp.zeros_like(me), core]).astype(jnp.int32),
            lengths.reshape(-1),
            labels.reshape(-1),
        ]
    )

    def shape(*dims, dtype=BF):
        return jax.ShapeDtypeStruct(dims, dtype)

    def of(s):
        return (s.shape, s.dtype)

    def in_vmem(*shapes):
        return [(s, VMEM) for s in shapes]

    def in_hbm(*shapes):
        return [(s, HBM) for s in shapes]

    row = shape(length, width)
    flat = shape(width, length)
    x_p, x_q, other_p, other_q, rows_p, rows_q = call(
        functools.partial(prepare_kernel, a_masks, b_masks),
        "prepare",
        0,
        8,
        [SCALARS, HBM],
        in_hbm(flat, flat, flat, flat) + in_vmem(row, row),
        [of(row), of(row), of(flat), ((4, width, length), BF)],
        6,
        (info, inputs),
    )

    pool_half = lax.dynamic_slice_in_dim(pool_weight, core * half, half, 1)
    a_shard = jnp.concatenate([input_weight[0], input_weight[1]], 1)
    vo_shard = jnp.concatenate([input_weight[2], out_weight.T], 1)
    u_shard = jnp.concatenate([up_weight, pool_half], 1)
    d_shard = down_weight.T
    shared = jnp.concatenate(
        [
            jnp.stack(
                [out_bias, first_gain, first_shift, down_bias, second_gain, second_shift, pool_bias]
            ),
            class_weight.T,
        ],
        0,
    )
    def with_other(lo, hi):
        return flat_rows(lo, hi, swap_core(lo), swap_core(hi))

    def flat_rows(*arrays):
        return tuple(array.reshape(-1, array.shape[2]) for array in arrays)

    def by_block(arrays):
        return [array.reshape(lower, block, array.shape[1]) for array in arrays]

    if direct:
        extra = extra_columns(
            shared[None], input_bias.reshape(1, 1, rows), up_bias.reshape(1, 1, 2 * rows), rows
        )
        b_shard = jnp.concatenate([vo_shard, after(extra, a_shard, d_shard)[0]], 1)
        a0, b0, u0, d0 = a_shard[None], b_shard[None], u_shard[None], d_shard[None]
        z1, z0 = order_a[0], order_a[1]
        a1, b1, d1 = swap(a0, z1), swap(b0, z1), swap(d0, 1)
        a2, b2 = join(a0, a1), join(b0, b1)
        a2_in, b2_in = swap(a2, z0), swap(b2, z0)
        u1 = swap(after(u0, a2, b2), z1)
        a4, b4 = join(a2, a2_in), join(b2, b2_in)
        a4_in, b4_in = swap(a4, 2), swap(b4, 1)
        u2 = after(join(u0, u1), a4, b4)
        d2 = after(join(d0, d1), a4, b4)
        u2_in, d2_in = swap(u2, z0), swap(d2, z1)
        u4 = join(u2, u2_in)
        u4_in = swap(u4, 2)
        a8, b8 = join(a4, a4_in), join(b4, b4_in)
        a8_in, b8_in = swap(a8, 1), swap(b8, 2)
        a8_other, b8_other = swap_core(a8), swap_core(b8)
        d4 = after(join(d2, d2_in), a8, b8)
        d4_in = swap(d4, z0)
        u8 = after(join(u4, u4_in), a8_in, b8, rows_q)
        u8_in = swap(u8, 1)
        d8 = after(join(d4, d4_in), b8_in, u8)
        d8_in = swap(d8, 2)
        info = after(info, u8, d8)
        qk = flat_rows(a8, a8_in, a8_other, swap_core(a8_in))
        vo = flat_rows(b8, b8_in, b8_other, swap_core(b8_in))
        pieces = [(u8, u8_in), (d8, d8_in)]
    else:

        def whole(shard, order):
            return in_order(gather_blocks(shard, order), order, me)

        def cut(array):
            blocks = array.reshape(BLOCKS, block, -1)
            return blocks[:lower], blocks[lower:]

        shared = whole(shared, order_a).transpose(1, 0, 2).reshape(-1, BLOCKS, block)
        pair = whole(input_bias, order_a).transpose(1, 0, 2).reshape(2, BLOCKS, block // 2)
        extra = extra_columns(
            shared.transpose(1, 0, 2),
            pair.transpose(1, 0, 2).reshape(BLOCKS, 1, block),
            whole(up_bias, order_a).reshape(BLOCKS, 1, 2 * block),
            block,
        )
        vo = cut(whole(vo_shard, order_b))
        vo = jnp.concatenate([vo[0], extra[:lower]], 2), jnp.concatenate([vo[1], extra[lower:]], 2)
        qk, vo = with_other(*cut(whole(a_shard, order_a))), with_other(*vo)
        pieces = [cut(whole(u_shard, order_u)), cut(whole(d_shard, order_d))]

    wide = shape(length, hidden_width)
    norm = shape(length, width, dtype=F32)
    roots = shape(length, LANES, dtype=F32)
    eight = shape(8, width, dtype=F32)
    vectors = shape(16, width, dtype=F32)
    probs = shape(pairs, 2, length, length)

    def grad(columns):
        return [shape(half, columns)] * 2

    part = width + LANES
    slim = shape(length, half)
    halved = shape(length, hidden_half)
    thirds = shape(length, 3 * half)
    matrix = shape(width, hidden_width)

    def blocks_of(columns):
        return shape(2, width, columns)

    q, k, v, att, att_other, p, first, first_p, normed, root, vec = call(
        functools.partial(attend_kernel, a_masks, b_masks),
        "attend",
        0,
        18,
        [SCALARS, HBM, VMEM, VMEM] + [HBM] * 8,
        in_vmem(row, row, row, slim, slim, probs, row, flat, norm, roots, vectors),
        [of(row), of(blocks_of(width)), of(blocks_of(part)), of(row), of(flat), ((width, length), F32)]
        + [((width, LANES), F32)],
        10,
        (info, inputs, rows_p, rows_q, *qk, *vo),
    )
    (up_lo, up_hi), (down_lo, down_hi) = pieces
    up_hi, down_hi = after(up_hi, first), after(down_hi, first)
    up = with_other(up_lo, up_hi)
    down = with_other(down_lo, down_hi)
    first_in, att_in = swap_core(first_p), swap_core(att_other)
    act, act_other, slope, up_matrix = call(
        up_kernel,
        "up",
        0,
        4,
        [VMEM, VMEM] + [HBM] * 4,
        in_vmem(halved, halved, wide, blocks_of(hidden_half)),
        [],
        4,
        (vec, first_p, *up),
    )
    act_in = swap_core(act_other)
    block_out, ramp, feed, second, sums_two, down_matrix = call(
        functools.partial(ramp_kernel, d_masks, u_masks),
        "ramp",
        15,
        14,
        [SCALARS, SCALARS, VMEM, HBM, VMEM, HBM, VMEM] + [HBM] * 8,
        in_vmem(row, eight, flat, norm, eight, blocks_of(hidden_half)),
        [of(row), of(halved), of(blocks_of(half)), of(flat), ((width, length), F32), ((width, 2 * LANES), F32)]
        + [of(eight)],
        10,
        (info, class_bias.astype(F32), vec, cotangents, act, act_other, first, *down, *up),
    )
    feed_in, ramp_in = swap_core(feed), swap_core(ramp)
    delta, delta_other = call(
        hidden_kernel,
        "hidden",
        400,
        5,
        [VMEM] * 3,
        in_vmem(halved, halved),
        [],
        0,
        (after(feed, act_in, first_in, att_in), slope, down_matrix),
    )
    delta_in = swap_core(delta_other)
    *down_grad, logits_out = call(
        functools.partial(down_grad_kernel, back_masks[3]),
        "down_grad",
        400,
        6,
        [SCALARS, VMEM, VMEM, HBM, HBM, VMEM, HBM],
        in_vmem(*grad(hidden_half + half), shape(2, classes, dtype=F32)),
        [of(flat), of(flat), of(halved), ((width, 16), F32), ((width, 16), F32)],
        3,
        (after(info, delta), ramp, ramp_in, feed, feed_in, act, act_in),
    )

    def first_hop(pieces, order):
        return swap(pieces[1], order[-1]) if direct else None

    def add(*streams):
        columns = sum(own.shape[2] for own, _ in streams)
        return call(
            hop_kernel,
            "hop",
            0,
            2,
            [VMEM] * (2 * len(streams)),
            in_vmem(*[shape(streams[0][0].shape[0] // 2, block, columns)] * 2),
            [],
            0,
            tuple(array for stream in streams for array in stream),
        )

    def next_hop(kept, arrived, mask, start):
        if not direct:
            return kept, None
        sent, kept = add((after(kept, start), arrived))
        return kept, swap(sent, mask)

    down_grad = by_block(down_grad)
    down_arrived = first_hop(down_grad, back_d)
    *up_grad, up_sums = call(
        up_grad_kernel,
        "up_grad",
        0,
        6,
        [VMEM] * 3 + [HBM],
        in_vmem(*grad(hidden_half), shape(1, hidden_half, dtype=F32)),
        [of(halved)],
        1,
        (after(first_p, down_grad[0]), first_in, delta, delta_in),
    )
    up_grad = by_block(up_grad)
    up_arrived = first_hop(up_grad, back_u)
    block_in = swap_core(after(block_out, up_sums))
    total, datt, branch, sums_one = call(
        functools.partial(branch_kernel, u_masks, b_masks),
        "branch",
        0,
        11,
        [SCALARS] + [VMEM] * 3 + [HBM] + [VMEM] * 4 + [HBM] * 4,
        in_vmem(norm, row, flat, vectors),
        [of(blocks_of(half)), of(halved), of(flat), of(flat), ((width, length), F32)],
        5,
        (after(info, up_grad[0]), vec, sums_two, delta, delta_other, second, normed, root, up_matrix, *vo),
    )
    branch_in, sums_in = swap_core(branch), swap_core(sums_one)
    dqkv, dqkv_other = call(
        back_kernel,
        "back",
        0,
        10,
        [VMEM] * 7,
        in_vmem(thirds, thirds),
        [of(row)] * 4,
        0,
        (q, k, v, att, att_other, after(datt, block_in), p),
    )
    dqkv_in = swap_core(dqkv_other)
    (input_delta,) = call(
        functools.partial(input_kernel, a_masks, b_masks),
        "input",
        0,
        9,
        [SCALARS] + [VMEM] * 3 + [HBM] * 8,
        in_vmem(row),
        [of(blocks_of(width)), of(blocks_of(half)), ((width, length), F32), ((width, length), F32)],
        8,
        (info, dqkv, dqkv_other, total, *qk, *vo),
    )
    up_kept, up_arrived = next_hop(up_grad[0], up_arrived, back_u[2], input_delta)
    (out_grad,) = call(
        out_grad_kernel,
        "out_grad",
        0,
        3,
        [VMEM] * 4,
        in_vmem(shape(width, half)),
        [],
        0,
        (after(branch, dqkv, sums_in, up_kept), branch_in, att, att_in),
    )
    input_grads = call(
        functools.partial(input_grad_kernel, back_masks[1]),
        "input_grad",
        0,
        4,
        [SCALARS] + [VMEM] * 10,
        in_vmem(*grad(width), *grad(part)),
        [((width, LANES), F32)],
        0,
        (info, sums_one, sums_in, up_sums, x_p, x_q, other_p, other_q, dqkv, dqkv_in, out_grad),
    )
    qk_grad, vo_grad = by_block(input_grads[:2]), by_block(input_grads[2:])
    qk_arrived, vo_arrived = first_hop(qk_grad, back_a), first_hop(vo_grad, back_b)
    input_delta_in = swap_core(input_delta)
    down_kept, down_arrived = next_hop(down_grad[0], down_arrived, back_d[2], qk_grad[0])
    up_kept, up_arrived = next_hop(up_kept, up_arrived, back_u[1], down_kept)
    qk_kept, qk_arrived = next_hop(qk_grad[0], qk_arrived, back_a[2], down_kept)
    vo_kept, vo_arrived = next_hop(vo_grad[0], vo_arrived, back_b[2], down_kept)
    down_kept, down_arrived = next_hop(down_kept, down_arrived, back_d[1], vo_kept)
    blocks_out, input_grad = call(
        arrange_kernel,
        "arrange",
        0,
        4,
        [SCALARS] + [HBM] * 4,
        in_hbm(*[shape(2, length, width)] * 2),
        [((4, length, width), BF)],
        8,
        (after(info, qk_kept, vo_kept), block_out, block_in, input_delta, input_delta_in),
    )
    if direct:
        sent, kept = add((after(qk_kept, blocks_out), qk_arrived), (vo_kept, vo_arrived))
        arrived = swap(sent, back_a[1])
        down_kept, down_arrived = next_hop(down_kept, down_arrived, back_d[0], kept)
        up_kept, up_arrived = next_hop(up_kept, up_arrived, back_u[0], kept)
        sent, kept = add((after(kept, down_kept, up_kept), arrived))
        arrived = swap(sent, back_a[0])
        down_kept, up_kept = after(down_kept, kept), after(up_kept, kept)
        down_share, up_share = (down_kept + down_arrived)[0], (up_kept + up_arrived)[0]
        kept = after(kept, down_share, up_share)
    else:

        def spread(pieces, order):
            return scatter_blocks(out_of_order(join(*pieces).reshape(size, rows, -1), order, me), order)

        down_share, up_share = spread(down_grad, back_d), spread(up_grad, back_u)
        qk_share = spread(qk_grad, back_a)
    down_share, pool_share = down_share[:, :hidden_half], down_share[:, hidden_half:]
    pool_shares = pool_share, swap_core(pool_share)
    pool_grad = jnp.where(
        core == 0, jnp.concatenate(pool_shares, 1), jnp.concatenate(pool_shares[::-1], 1)
    ).astype(F32)
    if direct:
        input_share, out_share, pair_share, up_bias_share, class_bias_grad, class_grad, *vector_grads = call(
            finish_kernel,
            "finish",
            0,
            2,
            [VMEM] * 2,
            in_vmem(
                shape(3, rows, half, dtype=F32),
                shape(half, rows, dtype=F32),
                shape(2, rows // 2, dtype=F32),
                shape(1, 2 * rows, dtype=F32),
                shape(1, classes, dtype=F32),
                shape(rows, classes, dtype=F32),
                *[shape(1, rows, dtype=F32)] * 7,
            ),
            [],
            0,
            (kept, arrived),
        )
        up_bias_share, class_bias_grad = up_bias_share.reshape(-1), class_bias_grad.reshape(-1)
        vector_grads = [array.reshape(-1) for array in vector_grads]
    else:
        vo_share = spread([piece[:, :, :width] for piece in vo_grad], back_b)
        extra_sum = lax.psum(join(*[piece[:, :, width:] for piece in vo_grad]).astype(F32), "dp")

        def own(array, count):
            return lax.dynamic_slice_in_dim(array, me * count, count, array.ndim - 1)

        vector_grads = own(extra_sum[:, :SHARED, :block].transpose(1, 0, 2).reshape(SHARED, width), rows)
        pair_sums = extra_sum[:, PAIR_ROW, :block].reshape(BLOCKS, 2, block // 2)
        pair_share = own(pair_sums.transpose(1, 0, 2).reshape(2, half), rows // 2)
        up_bias_share = own(extra_sum[:, UP_ROW, : 2 * block].reshape(-1), 2 * rows)
        class_bias_grad = extra_sum[0, CLASS_ROW, :classes]
        vector_grads, class_grad = vector_grads[:7], vector_grads[7:].T
        input_share = jnp.stack([qk_share[:, :half], qk_share[:, half:], vo_share[:, :half]])
        out_share = vo_share[:, half:width].T
    return (
        blocks_out[:, None],
        logits_out[:, None],
        input_grad[:, None],
        input_share.astype(F32),
        pair_share.astype(F32),
        out_share.astype(F32),
        vector_grads[0],
        vector_grads[1],
        vector_grads[2],
        up_share.astype(F32),
        up_bias_share.astype(F32),
        down_share.T.astype(F32),
        vector_grads[5],
        vector_grads[3],
        vector_grads[4],
        pool_grad,
        vector_grads[6],
        class_grad,
        class_bias_grad.astype(F32),
    )


def solution(mesh):
    placed = (
        P(None, "dp", None, None),
        P(None, "dp"),
        P(None, "dp"),
        P(None, "dp", None, None),
        P(None, "dp", "tensor"),
        P(None, ("tensor", "dp")),
        P("tensor", "dp"),
        P("dp"),
        P("dp"),
        P("dp"),
        P("dp", "tensor"),
        P(("tensor", "dp")),
        P("tensor", "dp"),
        P("dp"),
        P("dp"),
        P("dp"),
        P("dp", None),
        P("dp"),
        P("dp", None),
        P(),
    )
    return jax.shard_map(
        per_device,
        mesh=mesh,
        in_specs=placed,
        out_specs=(
            P(None, "dp", None, None),
            P(None, "dp", None),
            P(None, "dp", None, None),
            P(None, "dp", "tensor"),
            P(None, ("tensor", "dp")),
            P("tensor", "dp"),
            P("dp"),
            P("dp"),
            P("dp"),
            P("dp", "tensor"),
            P(("tensor", "dp")),
            P("tensor", "dp"),
            P("dp"),
            P("dp"),
            P("dp"),
            P("dp", None),
            P("dp"),
            P("dp", None),
            P(),
        ),
        check_vma=False,
    )
```

```python
import functools
import math

import jax
import jax.numpy as jnp
from jax import lax
from jax.experimental import pallas as pl
from jax.experimental.pallas import tpu as pltpu
from jax.sharding import PartitionSpec as P

HD = 64
LANES = 128
BLOCKS = 16
EPS = 1e-06
BF = jnp.bfloat16
F32 = jnp.float32
NN = ((1,), (0,))
NT = ((1,), (1,))
TN = ((0,), (0,))
HBM = pl.BlockSpec(memory_space=pltpu.HBM)
SCALARS = pl.BlockSpec(memory_space=pltpu.SMEM)
VMEM = pl.BlockSpec(memory_space=pltpu.VMEM)
MIB = 1024 * 1024
FLOPS_PER_MICROSECOND = 1_150_000_000

OUT_B, GAIN_1, SHIFT_1, DOWN_B, GAIN_2, SHIFT_2, POOL_B, CLASS, QUERY_B, VALUE_B, UP_B = (
    0, 1, 2, 3, 4, 5, 6, 7, 10, 11, 12,
)
SHARED, PAIR_ROW, UP_ROW, CLASS_ROW = 10, 10, 11, 12
NOTES = 16


def dot(left, right, dims=NN):
    return lax.dot_general(left, right, (dims, ((), ())), preferred_element_type=F32)


def begin(source, target, sem):
    copy = pltpu.make_async_copy(source, target, sem)
    copy.start()
    return copy


def row_block(me, mask, rows):
    return pl.ds(pl.multiple_of((me ^ mask) * rows, 16), rows)


def load(pieces, target, sems, columns=None):
    cut, width = pieces[0].shape
    start, width = columns or (0, width)
    for i, piece in enumerate(pieces):
        begin(piece.at[:, pl.ds(start, width)], target.at[i // 2, pl.ds(i % 2 * cut, cut), :], sems.at[i])


def landed(target, sem):
    pltpu.make_async_copy(target, target, sem).wait()


def loaded(target, h, sems):
    cut = target.shape[1] // 2
    for i in range(2):
        landed(target.at[h, pl.ds(i * cut, cut), :], sems.at[2 * h + i])


def to_blocks(source, target, masks, me):
    rows = source.shape[0] // BLOCKS
    for j in range(BLOCKS):
        target[j * rows : (j + 1) * rows, :] = source[row_block(me, masks[j], rows), :]


def to_rows(source, target, masks, me):
    rows = target.shape[0] // BLOCKS
    for j in range(BLOCKS):
        target[row_block(me, masks[j], rows), :] = source[j * rows : (j + 1) * rows, :]


def row_product(matrices, rights):
    return sum(dot(matrices[h], rights[h], NT) for h in range(2))


def pair_product(lefts, rights, lower, upper):
    cut = lefts[0].shape[0] // 2
    columns = rights[0].shape[1]
    for i, target in enumerate((lower, upper)):
        span = slice(i * cut, (i + 1) * cut)
        total = dot(lefts[0][span, :], rights[0][...]) + dot(lefts[1][span, :], rights[1][...])
        target[:, 0:columns] = total.astype(BF)


def mean(array):
    return jnp.mean(array, -1, keepdims=True)


def normalize(total):
    centered = total - mean(total)
    root = lax.rsqrt(mean(centered * centered) + EPS)
    return centered * root, root


def norm_backward(delta, normed, root, gain):
    scaled = delta * gain
    return root * (scaled - mean(scaled) - normed * mean(scaled * normed))


def column_sum(array):
    return jnp.sum(array, 0, keepdims=True)


def unpack_vectors(extra, vec, h):
    width = vec.shape[1]
    rows, part = width // BLOCKS, width // BLOCKS // 2
    for b in range(BLOCKS):
        own = extra[b * rows : b * rows + 16, :]
        if h == 0:
            vec[0:SHARED, b * rows : (b + 1) * rows] = own[0:SHARED, 0:rows]
        at = h * width // 2 + b * part
        vec[QUERY_B : QUERY_B + 1, at : at + part] = own[PAIR_ROW : PAIR_ROW + 1, 0:part]
        vec[VALUE_B : VALUE_B + 1, at : at + part] = own[PAIR_ROW : PAIR_ROW + 1, part:rows]
        row, at = UP_B + 2 * h + b // (BLOCKS // 2), b % (BLOCKS // 2) * 2 * rows
        vec[row : row + 1, at : at + 2 * rows] = own[UP_ROW : UP_ROW + 1, 0 : 2 * rows]


def pack_vectors(sums, query, value, up, extra):
    width = sums.shape[1]
    rows, part = width // BLOCKS, width // BLOCKS // 2
    extra[...] = jnp.zeros(extra.shape, F32)
    for b in range(BLOCKS):
        top = b * rows
        extra[top : top + SHARED, 0:rows] = sums[0:SHARED, b * rows : (b + 1) * rows]
        at = b * part
        extra[top + PAIR_ROW : top + PAIR_ROW + 1, 0:part] = query[:, at : at + part]
        extra[top + PAIR_ROW : top + PAIR_ROW + 1, part:rows] = value[:, at : at + part]
        at = b * 2 * rows
        extra[top + UP_ROW : top + UP_ROW + 1, 0 : 2 * rows] = up[:, at : at + 2 * rows]
        extra[top + CLASS_ROW : top + CLASS_ROW + 1, :] = sums[SHARED : SHARED + 1, 0:LANES]


def prepare_kernel(masks_p, masks_q, info, hidden, *refs):
    outs, (x_rows, x, other_x, flip, held, sems) = refs[0:4], refs[4:]
    me, core = info[0], info[1]
    begin(hidden.at[core], x, sems.at[0])
    begin(hidden.at[1 - core], other_x, sems.at[1])
    for i, source in enumerate((x, other_x)):
        landed(source, sems.at[i])
        flip[...] = source[...].T
        for n, masks in enumerate((masks_p, masks_q)):
            to_blocks(flip, held.at[2 * i + n], masks, me)
            begin(held.at[2 * i + n], outs[2 * i + n], sems.at[2 + 2 * i + n])
    x_rows[...] = held[0].T
    for i in range(4):
        landed(held.at[i], sems.at[2 + i])


def attend_kernel(masks, info, hidden, x_rows, *refs):
    qk, vo = refs[0:4], refs[4:8]
    q, k, v, att_own, att_other, p, first, first_p = refs[8:16]
    normed, root, vec = refs[16:19]
    x, wa, wb, att, flip, wide, extra, sems = refs[19:]
    me, core = info[0], info[1]
    count = info[2 + core]
    length, width = x.shape
    half = width // 2
    load(vo, wb, sems.at[pl.ds(2, 4)])
    load(qk, wa, sems.at[pl.ds(6, 4)])
    begin(hidden.at[core], x, sems.at[0])
    rows = width // BLOCKS
    for h in range(2):
        loaded(wb, h, sems.at[pl.ds(2, 4)])
        for j in range(BLOCKS):
            piece = wb[h, j * rows : (j + 1) * rows, width:]
            extra[row_block(me, masks[j], rows), :] = piece.astype(F32)
        unpack_vectors(extra, vec, h)
    for h in range(2):
        own = slice(h * half, (h + 1) * half)
        loaded(wa, h, sems.at[pl.ds(6, 4)])
        both = dot(x_rows[...], wa[h])
        q[:, own] = (both[:, :half] + vec[QUERY_B : QUERY_B + 1, own]).astype(BF) * (1.0 / math.sqrt(HD))
        k[:, own] = both[:, half:].astype(BF)
        v[:, own] = (dot(x_rows[...], wb[h, :, 0:half]) + vec[VALUE_B : VALUE_B + 1, own]).astype(BF)
    keys = lax.broadcasted_iota(jnp.int32, (1, length), 1)
    bias = jnp.where(keys < count, 0.0, -1e30).astype(F32)
    lane = lax.broadcasted_iota(jnp.int32, (1, LANES), 1)
    for pair in range(width // LANES):
        cols = slice(pair * LANES, (pair + 1) * LANES)
        q_pair, k_pair, v_pair = q[:, cols], k[:, cols], v[:, cols]
        acc = None
        for a in range(2):
            mine = (lane < HD) if a == 0 else (lane >= HD)
            scores = dot(jnp.where(mine, q_pair, 0.0).astype(BF), k_pair, NT) + bias
            weights = jnp.exp(scores - jnp.max(scores, -1, keepdims=True))
            probs = (weights * (1.0 / jnp.sum(weights, -1, keepdims=True))).astype(BF)
            p[pair, a] = probs
            term = dot(probs, jnp.where(mine, v_pair, 0.0).astype(BF))
            acc = term if acc is None else acc + term
        att[:, cols] = acc.astype(BF)
    att_own[...] = att[:, :half]
    att_other[...] = att[:, half:]
    to_rows(row_product([wb[h, :, half:width] for h in range(2)], (att[:, :half], att[:, half:])), wide, masks, me)
    landed(x, sems.at[0])
    own_normed, own_root = normalize(x[...].astype(F32) + wide[...].T + vec[OUT_B : OUT_B + 1, :])
    normed[...] = own_normed
    root[...] = jnp.broadcast_to(own_root, root.shape)
    low = (own_normed * vec[GAIN_1 : GAIN_1 + 1, :] + vec[SHIFT_1 : SHIFT_1 + 1, :]).astype(BF)
    first[...] = low
    flip[...] = low.T
    to_blocks(flip, first_p, masks, me)


def up_kernel(vec, first_p, *refs):
    pieces = refs[0:4]
    active, other_active, slope, w, sems = refs[4:]
    width = first_p.shape[0]
    half = active.shape[1]
    load(pieces, w, sems, (0, half))
    left = first_p[...].T
    chunk = 256
    for h, target in enumerate((active, other_active)):
        loaded(w, h, sems)
        for c in range(half // chunk):
            cols = slice(c * chunk, (c + 1) * chunk)
            at = h * half + c * chunk
            row, lane = UP_B + at // width, at % width
            hidden = dot(left, w[h, :, cols]) + vec[row : row + 1, lane : lane + chunk]
            cdf = 0.5 + 0.5 * lax.erf(hidden * math.sqrt(0.5))
            density = jnp.exp(hidden * hidden * -0.5) * (1.0 / math.sqrt(2.0 * math.pi))
            target[:, cols] = (hidden * cdf).astype(BF)
            slope[:, at : at + chunk] = (cdf + hidden * density).astype(BF)


def ramp_kernel(masks, pool_masks, back_masks, info, class_bias, vec, cotangent, active, other_active, first, *refs):
    pieces, pool_pieces = refs[0:4], refs[4:8]
    block, ramp, feed_r, feed_back, second, grads = refs[8:14]
    w, cot, right, pool, flip, wide, slim, z, sems = refs[14:]
    me, core = info[0], info[1]
    count, label = info[2 + core], info[4 + core]
    length, width = first.shape
    half = width // 2
    cut = w.shape[2]
    load(pieces, w, sems.at[pl.ds(0, 4)], (0, cut))
    begin(other_active, right, sems.at[8])
    load(pool_pieces, pool, sems.at[pl.ds(4, 4)], (cut, half))
    begin(cotangent.at[core], cot, sems.at[9])
    parts = []
    for i in range(2):
        span = slice(i * half, (i + 1) * half)
        landed(w.at[0, pl.ds(i * half, half), :], sems.at[i])
        parts.append(dot(w[0, span, :], active[...], NT))
    landed(right, sems.at[8])
    for i in range(2):
        span = slice(i * half, (i + 1) * half)
        landed(w.at[1, pl.ds(i * half, half), :], sems.at[2 + i])
        parts[i] = parts[i] + dot(w[1, span, :], right[...], NT)
    to_rows(jnp.concatenate(parts, 0), wide, masks, me)
    total = first[...].astype(F32) + wide[...].T + vec[DOWN_B : DOWN_B + 1, :]
    gain, shift = vec[GAIN_2 : GAIN_2 + 1, :], vec[SHIFT_2 : SHIFT_2 + 1, :]
    normed, root = normalize(total)
    ids = lax.broadcasted_iota(jnp.int32, (length, 1), 0)
    block[...] = jnp.where(ids < count, normed * gain + shift, 0.0).astype(BF)
    for h in range(2):
        loaded(pool, h, sems.at[pl.ds(4, 4)])
    head = (normed[0:8, :] * gain + shift).astype(BF)
    sides = [pl.ds(pl.multiple_of(side * half, LANES), half) for side in (core, 1 - core)]
    slim[:, 0:8] = head.astype(F32).T
    for j in range(BLOCKS):
        at = slice(j * (width // BLOCKS), (j + 1) * (width // BLOCKS))
        slim[at, LANES : LANES + 8] = slim[row_block(me, pool_masks[j], width // BLOCKS), 0:8]
    head_t = slim[:, LANES : LANES + 8].astype(BF)
    for h in range(2):
        z[:, sides[h]] = dot(head_t, pool[h], TN)
    pooled_wide = jnp.tanh(z[...] + vec[POOL_B : POOL_B + 1, :])
    pooled = pooled_wide.astype(BF).astype(F32)
    class_rows = [vec[CLASS + c : CLASS + c + 1, :] for c in range(3)]
    logits = [
        jnp.sum(pooled * class_rows[c], -1, keepdims=True) + class_bias[c] for c in range(3)
    ]
    top = jnp.maximum(jnp.maximum(logits[0], logits[1]), logits[2])
    powers = [jnp.exp(l - top) for l in logits]
    power_sum = powers[0] + powers[1] + powers[2]
    deltas = [powers[c] / power_sum - jnp.where(label == c, 1.0, 0.0) for c in range(3)]
    pre = sum(deltas[c] * class_rows[c] for c in range(3)) * (1.0 - pooled_wide * pooled_wide)
    pre_high = pre.astype(BF)
    z[0:8, :] = pre_high.astype(F32)
    high = [z[:, side].astype(BF) for side in sides]
    z[0:8, :] = pre - pre_high.astype(F32)
    low = [z[:, side].astype(BF) for side in sides]
    slim[:, 0:8] = row_product(pool, high) + row_product(pool, low)
    for j in range(BLOCKS):
        at = slice(j * (width // BLOCKS), (j + 1) * (width // BLOCKS))
        slim[row_block(me, pool_masks[j], width // BLOCKS), LANES : LANES + 8] = slim[at, 0:8]
    head_delta = slim[:, LANES : LANES + 8].T[0:1, :]
    lane = lax.broadcasted_iota(jnp.int32, (1, width), 1)
    tail = jnp.zeros((1, width), F32)
    for c in range(3):
        tail = jnp.where(lane == c, deltas[c][0:1], tail)
        tail = jnp.where(lane == LANES + c, logits[c][0:1], tail)
    ramp[0:1, :] = head[0:1, :].astype(F32)
    ramp[1:2, :] = pooled[0:1, :]
    ramp[2:3, :] = pre[0:1, :]
    ramp[3:4, :] = tail
    ramp[4:8, :] = jnp.zeros((4, width), F32)
    landed(cot, sems.at[9])
    delta = jnp.where(ids < count, cot[...].astype(F32), 0.0) + jnp.where(ids == 0, head_delta, 0.0)
    grads[0:1, :] = column_sum(delta * normed)
    grads[1:2, :] = column_sum(delta)
    dsecond = norm_backward(delta, normed, root, gain)
    grads[2:3, :] = column_sum(dsecond)
    grads[3:4, :] = pre[0:1, :]
    for c in range(3):
        grads[4 + c : 5 + c, :] = deltas[c][0:1] * pooled[0:1, :]
    grads[7:8, :] = tail
    second[...] = dsecond
    flip[...] = dsecond.astype(BF).T
    to_blocks(flip, feed_r, masks, me)
    to_blocks(flip, feed_back, back_masks, me)


def hidden_kernel(feed_r, slope, *refs):
    pieces = refs[0:4]
    delta, other_delta, w, sems = refs[4:]
    half = delta.shape[1]
    load(pieces[2:] + pieces[:2], w, sems, (0, half))
    left = feed_r[...].T
    chunk = 512
    for n, (h, target) in enumerate(((1, other_delta), (0, delta))):
        loaded(w, n, sems)
        for c in range(half // chunk):
            cols = slice(c * chunk, (c + 1) * chunk)
            at = h * half + c * chunk
            target[:, cols] = (dot(left, w[n, :, cols]) * slope[:, at : at + chunk].astype(F32)).astype(BF)


def down_grad_kernel(info, ramp, ramp_other, left_in, left_other_in, right, right_other_in, *refs):
    lower, upper, logits, left, left_other, right_other, sems = refs
    loads = ((left_in, left), (left_other_in, left_other), (right_other_in, right_other))
    for i, (source, target) in enumerate(loads):
        begin(source, target, sems.at[i])
    width, columns = left.shape[0], right.shape[1]
    half = width // 2
    classes = logits.shape[1]
    pair = [r[3:4, LANES : LANES + classes] for r in (ramp, ramp_other)]
    logits[0:1, :] = jnp.where(info[1] == 0, pair[0], pair[1])
    logits[1:2, :] = jnp.where(info[1] == 0, pair[1], pair[0])
    heads = jnp.concatenate([ramp[0:1, :], ramp_other[0:1, :], jnp.zeros((NOTES - 2, width), F32)], 0)
    pres = jnp.concatenate([ramp[2:3, :], ramp_other[2:3, :], jnp.zeros((NOTES - 2, width), F32)], 0)
    upper[half:, :width] = heads.astype(BF)
    upper[half:, width:] = pres.astype(BF)
    for i, (_, target) in enumerate(loads):
        landed(target, sems.at[i])
    for target, span in ((lower, slice(0, half)), (upper, slice(half, width))):
        total = dot(left[span, :], right[...]) + dot(left_other[span, :], right_other[...])
        target[0:half, :] = total.astype(BF)


def up_grad_kernel(left, left_other, right, right_other_in, *refs):
    lower, upper, sums, right_other, sems = refs
    begin(right_other_in, right_other, sems.at[0])
    own_sum = column_sum(right[...].astype(F32))
    landed(right_other, sems.at[0])
    sums[...] = own_sum + column_sum(right_other[...].astype(F32))
    pair_product((left, left_other), (right, right_other), lower, upper)


def branch_kernel(masks_p, masks_q, info, vec, sums_in, delta, other_delta, second, normed, root, *refs):
    up, vo = refs[0:4], refs[4:8]
    total_out, datt, branch_p, grads = refs[8:12]
    wu, wo, right, flip, rows_q, wide, sems = refs[12:]
    me = info[0]
    width = normed.shape[1]
    half = width // 2
    load(up, wu, sems.at[pl.ds(5, 4)], (0, delta.shape[1]))
    begin(other_delta, right, sems.at[4])
    load(vo, wo, sems.at[pl.ds(0, 4)], (half, half))
    gain = vec[GAIN_1 : GAIN_1 + 1, :]
    parts = []
    for i in range(2):
        span = slice(i * half, (i + 1) * half)
        landed(wu.at[0, pl.ds(i * half, half), :], sems.at[5 + i])
        parts.append(dot(wu[0, span, :], delta[...], NT))
    landed(right, sems.at[4])
    for i in range(2):
        span = slice(i * half, (i + 1) * half)
        landed(wu.at[1, pl.ds(i * half, half), :], sems.at[7 + i])
        parts[i] = parts[i] + dot(wu[1, span, :], right[...], NT)
    to_rows(jnp.concatenate(parts, 0), wide, masks_p, me)
    dfirst = second[...] + wide[...].T
    own_normed = normed[...]
    total = norm_backward(dfirst, own_normed, root[:, 0:1], gain)
    total_out[...] = total
    flip[...] = total.astype(BF).T
    to_blocks(flip, branch_p, masks_p, me)
    to_blocks(flip, rows_q, masks_q, me)
    grads[0:1, :] = column_sum(total)
    grads[1:2, :] = column_sum(dfirst * own_normed)
    grads[2:3, :] = column_sum(dfirst)
    grads[3 : SHARED + 1, :] = sums_in[...]
    grads[SHARED + 1 :, :] = jnp.zeros((grads.shape[0] - SHARED - 1, width), F32)
    left = rows_q[...].T
    for h in range(2):
        loaded(wo, h, sems)
        datt[:, h * half : (h + 1) * half] = dot(left, wo[h]).astype(BF)


def back_kernel(q, k, v, att_own, att_other, datt, p, *refs):
    qk_own, v_own, qk_other, v_other = refs[0:4]
    att, dq, dk, dv = refs[4:]
    length, width = q.shape
    half = width // 2
    att[:, :half] = att_own[...]
    att[:, half:] = att_other[...]
    lane = lax.broadcasted_iota(jnp.int32, (1, LANES), 1)
    pairs = width // LANES

    for pair in range(pairs):
        cols = slice(pair * LANES, (pair + 1) * LANES)
        do = datt[:, cols]
        product = do.astype(F32) * att[:, cols].astype(F32)
        k_pair, v_pair = k[:, cols], v[:, cols]
        q_t = q[:, cols].T
        do_t = do.T
        dq_sum = None
        dk_parts, dv_parts = [], []
        for a in range(2):
            mine = (lane < HD) if a == 0 else (lane >= HD)
            shift = jnp.sum(jnp.where(mine, product, 0.0), -1, keepdims=True)
            dprobs = dot(jnp.where(mine, do, 0.0).astype(BF), v_pair, NT)
            probs = p[pair, a]
            dscores = (probs.astype(F32) * (dprobs - shift)).astype(BF)
            term = dot(dscores, jnp.where(mine, k_pair, 0.0).astype(BF))
            dq_sum = term if dq_sum is None else dq_sum + term
            own = slice(a * HD, (a + 1) * HD)
            dk_parts.append(dot(q_t[own], dscores))
            dv_parts.append(dot(do_t[own], probs))
        dq[:, cols] = (dq_sum * (1.0 / math.sqrt(HD))).astype(BF)
        dk[:, cols] = jnp.concatenate(dk_parts, 0).T.astype(BF)
        dv[:, cols] = jnp.concatenate(dv_parts, 0).T.astype(BF)
    for h, (qk, values) in enumerate(((qk_own, v_own), (qk_other, v_other))):
        own = slice(h * half, (h + 1) * half)
        qk[:, :half] = dq[:, own]
        qk[:, half:] = dk[:, own]
        values[...] = dv[:, own]


def out_grad_kernel(branch_t, other_branch_t, att, other_att, grad):
    grad[...] = (dot(branch_t[...], att[...]) + dot(other_branch_t[...], other_att[...])).astype(BF)


def input_grad_kernel(
    masks_p, info, sums_in, sums_other, up_sums, x_p, x_q, other_p, other_q, qk, qk_in, values, values_in, out_grad,
    *refs
):
    qk_pieces, vo_pieces = refs[0:2], refs[2:4]
    extra = refs[4]
    me = info[0]
    width = x_p.shape[0]
    half = width // 2
    rows = width // BLOCKS
    query_sum = column_sum(qk[:, :half].astype(F32)) + column_sum(qk_in[:, :half].astype(F32))
    value_sum = column_sum(values[...].astype(F32)) + column_sum(values_in[...].astype(F32))
    pack_vectors(sums_in[...] + sums_other[...], query_sum, value_sum, up_sums[...], extra)
    for i, target in enumerate(vo_pieces):
        span = slice(i * half, (i + 1) * half)
        total = dot(x_p[span, :], values[...]) + dot(other_p[span, :], values_in[...])
        target[:, 0:half] = total.astype(BF)
        target[:, half:width] = out_grad[span, :]
        for j in range(BLOCKS // 2):
            at = row_block(me, masks_p[i * (BLOCKS // 2) + j], rows)
            target[j * rows : (j + 1) * rows, width:] = extra[at, :].astype(BF)
    pair_product((x_q, other_q), (qk, qk_in), *qk_pieces)


def hop_kernel(*refs):
    sent, kept = refs[-2:]
    at = 0
    for own, arrived in zip(refs[0:-2:2], refs[1:-2:2]):
        half, _, width = sent.shape[0], 0, own.shape[2]
        cols = slice(at, at + width)
        sent[:, :, cols] = own[half:] + arrived[half:]
        kept[:, :, cols] = own[:half] + arrived[:half]
        at += width


def noted_hop_kernel(count, notes, own, arrived, sent, kept):
    cut = sent.shape[0] - NOTES
    sent[0:cut, :] = own[cut:, :] + arrived[cut : 2 * cut, :]
    kept[...] = own[0:cut, :] + arrived[0:cut, :]
    low, high = notes[0:NOTES, :].astype(F32), arrived[2 * cut :, :].astype(F32)
    rows = lax.broadcasted_iota(jnp.int32, (NOTES, 1), 0)
    sent[cut:, :] = jnp.where(rows < count, low, jnp.where(rows < 2 * count, pltpu.roll(high, count, 0), 0.0)).astype(BF)


def ramp_grad_kernel(info, notes, arrived, out, flip):
    rows, width = out.shape
    both = jnp.concatenate([notes[...], arrived[...]], 0).astype(F32)
    flip[...] = both[:, :width].T
    own = flip[pl.ds(pl.multiple_of(info[0] * rows, 16), rows), :].astype(BF)
    out[...] = dot(own, both[:, width:].astype(BF))


def finish_kernel(kept, arrived, input_out, out_out, pair_out, up_out, class_bias_out, class_out, *vectors):
    share = kept[0].astype(F32) + arrived[0].astype(F32)
    rows, half = input_out.shape[1:]
    for i in range(3):
        input_out[i] = share[:, i * half : (i + 1) * half]
    out_out[...] = share[:, 3 * half : 4 * half].T
    extra = share[:, 4 * half :]
    for i, target in enumerate(vectors):
        target[...] = extra[i : i + 1, 0:rows]
    pair_out[0:1, :] = extra[PAIR_ROW : PAIR_ROW + 1, 0 : rows // 2]
    pair_out[1:2, :] = extra[PAIR_ROW : PAIR_ROW + 1, rows // 2 : rows]
    up_out[...] = extra[UP_ROW : UP_ROW + 1, 0 : 2 * rows]
    class_bias_out[...] = extra[CLASS_ROW : CLASS_ROW + 1, 0 : class_bias_out.shape[1]]
    class_out[...] = extra[:, 0:rows].T[:, len(vectors) : SHARED]


def arrange_kernel(info, block_own, block_other, grad_own, grad_other, block_out, grad_out, held, sems):
    core = info[1]
    moves = (
        (block_own, block_out, core),
        (block_other, block_out, 1 - core),
        (grad_own, grad_out, core),
        (grad_other, grad_out, 1 - core),
    )
    for i, (source, _, _) in enumerate(moves):
        begin(source, held.at[i], sems.at[i])
    for i, (_, target, side) in enumerate(moves):
        landed(held.at[i], sems.at[i])
        begin(held.at[i], target.at[side], sems.at[4 + i])
    for i in range(4):
        landed(held.at[i], sems.at[4 + i])


def input_kernel(masks_p, masks_q, info, qk_own, v_own, qk_other, v_other, total, *refs):
    qk, vo = refs[0:4], refs[4:8]
    out, wa, wv, wide, wide_v, sems = refs[8:]
    me = info[0]
    width = total.shape[1]
    half = width // 2
    load(vo, wv, sems.at[pl.ds(0, 4)], (0, half))
    load(qk, wa, sems.at[pl.ds(4, 4)])
    for h in range(2):
        loaded(wv, h, sems.at[pl.ds(0, 4)])
    to_rows(row_product(wv, (v_own[...], v_other[...])), wide_v, masks_q, me)
    for h in range(2):
        loaded(wa, h, sems.at[pl.ds(4, 4)])
    to_rows(row_product(wa, (qk_own[...], qk_other[...])), wide, masks_p, me)
    out[...] = (total[...] + (wide[...] + wide_v[...]).T).astype(BF)


def costing(micros):
    return pl.CostEstimate(flops=micros * FLOPS_PER_MICROSECOND, bytes_accessed=1024, transcendentals=0)


def call(body, name, micros, mib, in_specs, outs, scratch, sems, args):
    return pl.pallas_call(
        body,
        name=name,
        in_specs=in_specs,
        out_specs=[spec for _, spec in outs],
        out_shape=[shape for shape, _ in outs],
        scratch_shapes=[pltpu.VMEM(s, d) for s, d in scratch] + [pltpu.SemaphoreType.DMA((sems,))] * (sems > 0),
        compiler_params=pltpu.CompilerParams(vmem_limit_bytes=mib * MIB),
        cost_estimate=costing(micros),
    )(*args)


def orders(size):
    bits = [1 << k for k in range(size.bit_length() - 1)]
    high = bits[2:][::-1]
    x_last, y_last = high + [2, 1], high + [1, 2]
    return (x_last, x_last, x_last, [1] + high + [2]), (y_last, x_last, x_last, [1] + high + [2])


def block_mask(index, order):
    mask = 0
    for k, bit in enumerate(order):
        if (index >> k) & 1:
            mask ^= bit
    return mask


def swap(array, mask):
    size = lax.axis_size("dp")
    return lax.ppermute(array, "dp", [(i, i ^ mask) for i in range(size)])


def swap_core(array):
    return lax.ppermute(array, "tensor", [(0, 1), (1, 0)])


def after(array, *others):
    return lax.optimization_barrier((array, *others))[0]


def join(left, right):
    return jnp.concatenate([left, right], 0)


def gather_blocks(shard, order):
    held = shard[None]
    for mask in order:
        held = join(held, swap(held, mask))
    return held


def hop(blocks, arrived):
    half = blocks.shape[0] // 2
    return blocks[half:] + arrived[half:], blocks[:half] + arrived[:half]


def scatter_blocks(blocks, order):
    for mask in order[::-1]:
        half = blocks.shape[0] // 2
        blocks = blocks[:half] + swap(blocks[half:], mask)
    return blocks[0]


def in_order(blocks, order, me):
    size = len(blocks)
    place = [0] * size
    for j in range(size):
        place[block_mask(j, order)] = j
    chosen = jnp.array(place)[jnp.arange(size) ^ me]
    return jnp.take(blocks, chosen, axis=0)


def out_of_order(blocks, order, me):
    owners = jnp.array([block_mask(j, order) for j in range(len(blocks))]) ^ me
    return jnp.take(blocks, owners, axis=0)


def extra_columns(shared, pair, up, rows):
    def lanes(array):
        return jnp.pad(array, ((0, 0), (0, 0), (0, LANES - array.shape[2])))

    columns = jnp.concatenate([lanes(shared), lanes(pair), lanes(up)], 1)
    return jnp.pad(columns, ((0, 0), (0, rows - columns.shape[1]), (0, 0)))


def per_device(
    hidden_in,
    lengths,
    labels,
    out_cot,
    input_weight,
    input_bias,
    out_weight,
    out_bias,
    first_gain,
    first_shift,
    up_weight,
    up_bias,
    down_weight,
    down_bias,
    second_gain,
    second_shift,
    pool_weight,
    pool_bias,
    class_weight,
    class_bias,
):
    size = lax.axis_size("dp")
    me = lax.axis_index("dp")
    core = lax.axis_index("tensor")
    length, width = hidden_in.shape[2:]
    rows = width // size
    half = input_weight.shape[2]
    hidden_half = up_weight.shape[1]
    hidden_width = 2 * hidden_half
    classes = class_bias.shape[0]
    pairs = width // LANES
    block = width // BLOCKS
    lower = BLOCKS // 2
    direct = size == BLOCKS
    (order_a, order_b, order_u, order_d), (back_a, back_b, back_u, back_d) = orders(size)

    def kernel_masks(order):
        return [block_mask(j, order) if direct else j for j in range(BLOCKS)]

    (a_masks, b_masks, u_masks, d_masks), back_masks = [[kernel_masks(o) for o in part] for part in orders(size)]

    inputs = hidden_in.reshape(2, length, width)
    cotangents = out_cot.reshape(2, length, width)
    info = jnp.concatenate(
        [
            jnp.stack([me if direct else jnp.zeros_like(me), core]).astype(jnp.int32),
            lengths.reshape(-1),
            labels.reshape(-1),
        ]
    )

    def shape(*dims, dtype=BF):
        return jax.ShapeDtypeStruct(dims, dtype)

    def of(s):
        return (s.shape, s.dtype)

    def in_vmem(*shapes):
        return [(s, VMEM) for s in shapes]

    def in_hbm(*shapes):
        return [(s, HBM) for s in shapes]

    row = shape(length, width)
    flat = shape(width, length)
    x_p, x_q, other_p, other_q, x_rows = call(
        functools.partial(prepare_kernel, back_masks[1], back_masks[0]),
        "prepare",
        0,
        8,
        [SCALARS, HBM],
        in_hbm(flat, flat, flat, flat) + in_vmem(row),
        [of(row), of(row), of(flat), ((4, width, length), BF)],
        6,
        (info, inputs),
    )

    pool_half = lax.dynamic_slice_in_dim(pool_weight, core * half, half, 1)
    a_shard = jnp.concatenate([input_weight[0], input_weight[1]], 1)
    vo_shard = jnp.concatenate([input_weight[2], out_weight.T], 1)
    u_shard = up_weight
    d_shard = jnp.concatenate([down_weight.T, pool_half], 1)
    shared = jnp.concatenate(
        [
            jnp.stack(
                [out_bias, first_gain, first_shift, down_bias, second_gain, second_shift, pool_bias]
            ),
            class_weight.T,
        ],
        0,
    )
    def with_other(lo, hi):
        return flat_rows(lo, hi, swap_core(lo), swap_core(hi))

    def flat_rows(*arrays):
        return tuple(array.reshape(-1, array.shape[2]) for array in arrays)

    def by_block(arrays):
        return [array.reshape(lower, block, array.shape[1]) for array in arrays]

    if direct:
        extra = extra_columns(
            shared[None], input_bias.reshape(1, 1, rows), up_bias.reshape(1, 1, 2 * rows), rows
        )
        b_shard = jnp.concatenate([vo_shard, after(extra, a_shard, d_shard)[0]], 1)
        a0, b0, u0, d0 = a_shard[None], b_shard[None], u_shard[None], d_shard[None]
        z1, z0 = order_a[0], order_a[1]
        a1, b1, d1 = swap(a0, z1), swap(b0, z1), swap(d0, 1)
        a2, b2 = join(a0, a1), join(b0, b1)
        a2_in, b2_in = swap(a2, z0), swap(b2, z0)
        u1 = swap(after(u0, a2, b2), z1)
        a4, b4 = join(a2, a2_in), join(b2, b2_in)
        a4_in, b4_in = swap(a4, 2), swap(b4, 2)
        u2 = after(join(u0, u1), a4, b4)
        u2_in = swap(u2, z0)
        a8, b8 = join(a4, a4_in), join(b4, b4_in)
        a8_in, b8_in = swap(a8, 1), swap(b8, 1)
        u4 = after(join(u2, u2_in), a8, b8)
        d2 = after(join(d0, d1), a4, b4)
        u4_in, d2_in = swap(u4, 2), swap(d2, z1)
        d4 = after(join(d2, d2_in), u4, a8_in, x_rows)
        d4_in = swap(d4, z0)
        a8_other, b8_other = swap_core(a8), swap_core(b8)
        u8 = after(join(u4, u4_in), a8_in, b8_in, d4)
        u8_in = swap(u8, 1)
        d8 = after(join(d4, d4_in), u8)
        d8_in = swap(d8, 2)
        info = after(info, u8, d8)
        qk = flat_rows(a8, a8_in, a8_other, swap_core(a8_in))
        vo = flat_rows(b8, b8_in, b8_other, swap_core(b8_in))
        pieces = [(u8, u8_in), (d8, d8_in)]
    else:

        def whole(shard, order):
            return in_order(gather_blocks(shard, order), order, me)

        def cut(array):
            blocks = array.reshape(BLOCKS, block, -1)
            return blocks[:lower], blocks[lower:]

        shared = whole(shared, order_a).transpose(1, 0, 2).reshape(-1, BLOCKS, block)
        pair = whole(input_bias, order_a).transpose(1, 0, 2).reshape(2, BLOCKS, block // 2)
        extra = extra_columns(
            shared.transpose(1, 0, 2),
            pair.transpose(1, 0, 2).reshape(BLOCKS, 1, block),
            whole(up_bias, order_a).reshape(BLOCKS, 1, 2 * block),
            block,
        )
        vo = cut(whole(vo_shard, order_b))
        vo = jnp.concatenate([vo[0], extra[:lower]], 2), jnp.concatenate([vo[1], extra[lower:]], 2)
        qk, vo = with_other(*cut(whole(a_shard, order_a))), with_other(*vo)
        pieces = [cut(whole(u_shard, order_u)), cut(whole(d_shard, order_d))]

    wide = shape(length, hidden_width)
    norm = shape(length, width, dtype=F32)
    roots = shape(length, LANES, dtype=F32)
    eight = shape(8, width, dtype=F32)
    vectors = shape(16, width, dtype=F32)
    probs = shape(pairs, 2, length, length)

    def grad(columns):
        return [shape(half, columns)] * 2

    part = width + LANES
    slim = shape(length, half)
    halved = shape(length, hidden_half)
    thirds = shape(length, 3 * half)
    matrix = shape(width, hidden_width)

    def blocks_of(columns):
        return shape(2, width, columns)

    q, k, v, att, att_other, p, first, first_p, normed, root, vec = call(
        functools.partial(attend_kernel, a_masks),
        "attend",
        0,
        18,
        [SCALARS, HBM, VMEM] + [HBM] * 8,
        in_vmem(row, row, row, slim, slim, probs, row, flat, norm, roots, vectors),
        [of(row), of(blocks_of(width)), of(blocks_of(part)), of(row), of(flat), ((width, length), F32)]
        + [((width, LANES), F32)],
        10,
        (info, inputs, x_rows, *qk, *vo),
    )
    (up_lo, up_hi), (down_lo, down_hi) = pieces
    up = with_other(up_lo, after(up_hi, first))
    first_in, att_in = swap_core(first_p), swap_core(att_other)
    act, act_other, slope = call(
        up_kernel,
        "up",
        0,
        8,
        [VMEM, VMEM] + [HBM] * 4,
        in_vmem(halved, halved, wide),
        [of(blocks_of(hidden_half))],
        4,
        (vec, first_p, *up),
    )
    act_in = swap_core(act_other)
    down = with_other(down_lo, after(down_hi, act))
    block_out, ramp, feed, feed_back, second, sums_two = call(
        functools.partial(ramp_kernel, d_masks, d_masks, back_masks[3]),
        "ramp",
        15,
        18,
        [SCALARS, SCALARS, VMEM, HBM, VMEM, HBM, VMEM] + [HBM] * 8,
        in_vmem(row, eight, flat, flat, norm, eight),
        [of(blocks_of(hidden_half)), of(row), of(halved), of(blocks_of(half)), of(flat), ((width, length), F32), ((width, 2 * LANES), F32)]
        + [of(eight)],
        10,
        (info, class_bias.astype(F32), vec, cotangents, act, act_other, first, *down, *down),
    )
    feed_in, ramp_in = swap_core(feed_back), swap_core(ramp)
    delta, delta_other = call(
        hidden_kernel,
        "hidden",
        400,
        9,
        [VMEM] * 2 + [HBM] * 4,
        in_vmem(halved, halved),
        [of(blocks_of(hidden_half))],
        4,
        (after(feed, act_in, first_in, att_in), slope, *down),
    )
    delta_in = swap_core(delta_other)
    *down_grad, logits_out = call(
        down_grad_kernel,
        "down_grad",
        400,
        6,
        [SCALARS, VMEM, VMEM, HBM, HBM, VMEM, HBM],
        in_vmem(shape(half, hidden_half), shape(half + NOTES, hidden_half), shape(2, classes, dtype=F32)),
        [of(flat), of(flat), of(halved)],
        3,
        (after(info, delta), ramp, ramp_in, feed_back, feed_in, act, act_in),
    )

    def first_hop(pieces, order):
        return swap(pieces[1], order[-1]) if direct else None

    def add(*streams):
        columns = sum(own.shape[2] for own, _ in streams)
        return call(
            hop_kernel,
            "hop",
            0,
            2,
            [VMEM] * (2 * len(streams)),
            in_vmem(*[shape(streams[0][0].shape[0] // 2, block, columns)] * 2),
            [],
            0,
            tuple(array for stream in streams for array in stream),
        )

    def next_hop(kept, arrived, mask, start):
        if not direct:
            return kept, None
        sent, kept = add((after(kept, start), arrived))
        return kept, swap(sent, mask)

    down_arrived = swap(down_grad[1], back_d[-1]) if direct else None

    def noted_hop(kept, notes, arrived, k, start):
        if not direct:
            return kept, notes, None
        cut = kept.shape[0] // 2
        sent, kept = call(
            functools.partial(noted_hop_kernel, 2 << (2 - k)),
            "noted_hop",
            0,
            4,
            [VMEM] * 3,
            in_vmem(shape(cut + NOTES, hidden_half), shape(cut, hidden_half)),
            [],
            0,
            (notes, after(kept, start), arrived),
        )
        return kept, sent[cut:], swap(sent, back_d[k])

    *up_grad, up_sums = call(
        up_grad_kernel,
        "up_grad",
        0,
        6,
        [VMEM] * 3 + [HBM],
        in_vmem(*grad(hidden_half), shape(1, hidden_half, dtype=F32)),
        [of(halved)],
        1,
        (after(first_p, down_grad[0]), first_in, delta, delta_in),
    )
    up_grad = by_block(up_grad)
    up_arrived = first_hop(up_grad, back_u)
    block_in = swap_core(after(block_out, up_sums))
    total, datt, branch, sums_one = call(
        functools.partial(branch_kernel, u_masks, b_masks),
        "branch",
        0,
        16,
        [SCALARS] + [VMEM] * 3 + [HBM] + [VMEM] * 3 + [HBM] * 8,
        in_vmem(norm, row, flat, vectors),
        [of(blocks_of(hidden_half)), of(blocks_of(half)), of(halved), of(flat), of(flat), ((width, length), F32)],
        9,
        (after(info, up_grad[0]), vec, sums_two, delta, delta_other, second, normed, root, *up, *vo),
    )
    branch_in, sums_in = swap_core(branch), swap_core(sums_one)
    dqk, dv, dqk_other, dv_other = call(
        back_kernel,
        "back",
        0,
        10,
        [VMEM] * 7,
        in_vmem(row, slim, row, slim),
        [of(row)] * 4,
        0,
        (q, k, v, att, att_other, after(datt, block_in), p),
    )
    dqk_in, dv_in = swap_core(dqk_other), swap_core(dv_other)
    (input_delta,) = call(
        functools.partial(input_kernel, a_masks, b_masks),
        "input",
        0,
        9,
        [SCALARS] + [VMEM] * 5 + [HBM] * 8,
        in_vmem(row),
        [of(blocks_of(width)), of(blocks_of(half)), ((width, length), F32), ((width, length), F32)],
        8,
        (info, dqk, dv, dqk_other, dv_other, total, *qk, *vo),
    )
    (out_grad,) = call(
        out_grad_kernel,
        "out_grad",
        0,
        3,
        [VMEM] * 4,
        in_vmem(shape(width, half)),
        [],
        0,
        (after(branch, dqk, sums_in, input_delta), branch_in, att, att_in),
    )
    up_sent, up_kept = add((after(up_grad[0], out_grad), up_arrived)) if direct else (None, up_grad[0])
    input_grads = call(
        functools.partial(input_grad_kernel, back_masks[1]),
        "input_grad",
        0,
        4,
        [SCALARS] + [VMEM] * 12,
        in_vmem(*grad(width), *grad(part)),
        [((width, LANES), F32)],
        0,
        (after(info, up_kept), sums_one, sums_in, up_sums, x_p, x_q, other_p, other_q, dqk, dqk_in, dv, dv_in, out_grad),
    )
    qk_grad, vo_grad = by_block(input_grads[:2]), by_block(input_grads[2:])
    qk_arrived, vo_arrived = first_hop(qk_grad, back_a), first_hop(vo_grad, back_b)
    input_delta_in = swap_core(input_delta)
    down_kept, notes, down_arrived = noted_hop(down_grad[0], down_grad[1][half:], down_arrived, 2, qk_grad[0])
    vo_kept, vo_arrived = next_hop(vo_grad[0], vo_arrived, back_b[2], down_kept)
    qk_kept, qk_arrived = next_hop(qk_grad[0], qk_arrived, back_a[2], vo_kept)
    up_arrived = swap(after(up_sent, qk_kept), back_u[2]) if direct else None
    down_kept, notes, down_arrived = noted_hop(down_kept, notes, down_arrived, 1, qk_kept)
    blocks_out, input_grad = call(
        arrange_kernel,
        "arrange",
        0,
        4,
        [SCALARS] + [HBM] * 4,
        in_hbm(*[shape(2, length, width)] * 2),
        [((4, length, width), BF)],
        8,
        (after(info, qk_kept), block_out, block_in, input_delta, input_delta_in),
    )
    if direct:
        sent, kept = add((after(qk_kept, blocks_out), qk_arrived), (vo_kept, vo_arrived))
        arrived = swap(sent, back_a[1])
        up_kept, up_arrived = next_hop(up_kept, up_arrived, back_u[1], kept)
        down_kept, notes, down_arrived = noted_hop(down_kept, notes, down_arrived, 0, up_kept)
        sent, kept = add((after(kept, down_kept), arrived))
        arrived = swap(sent, back_a[0])
        up_kept, up_arrived = next_hop(up_kept, up_arrived, back_u[0], kept)
        down_kept, up_kept = after(down_kept, kept), after(up_kept, kept)
        down_share, up_share = down_kept + down_arrived[:rows], (up_kept + up_arrived)[0]
        (pool_grad,) = call(
            ramp_grad_kernel,
            "ramp_grad",
            0,
            2,
            [SCALARS, VMEM, VMEM],
            in_vmem(shape(rows, width, dtype=F32)),
            [((width, 2 * NOTES), F32)],
            0,
            (info, notes, after(down_arrived[rows:], kept)),
        )
        kept = after(kept, down_share, up_share)
    else:

        def spread(pieces, order):
            return scatter_blocks(out_of_order(join(*pieces).reshape(size, rows, -1), order, me), order)

        down_halves = by_block([down_grad[0], down_grad[1][:half]])
        down_share, up_share = spread(down_halves, back_d), spread(up_grad, back_u)
        notes = lax.all_gather(down_grad[1][half : half + 2], "dp", axis=0, tiled=True)
        own_heads = lax.dynamic_slice_in_dim(notes[:, :width], me * rows, rows, 1)
        pool_grad = dot(own_heads, notes[:, width:], TN)
        qk_share = spread(qk_grad, back_a)
    if direct:
        input_share, out_share, pair_share, up_bias_share, class_bias_grad, class_grad, *vector_grads = call(
            finish_kernel,
            "finish",
            0,
            2,
            [VMEM] * 2,
            in_vmem(
                shape(3, rows, half, dtype=F32),
                shape(half, rows, dtype=F32),
                shape(2, rows // 2, dtype=F32),
                shape(1, 2 * rows, dtype=F32),
                shape(1, classes, dtype=F32),
                shape(rows, classes, dtype=F32),
                *[shape(1, rows, dtype=F32)] * 7,
            ),
            [],
            0,
            (kept, arrived),
        )
        up_bias_share, class_bias_grad = up_bias_share.reshape(-1), class_bias_grad.reshape(-1)
        vector_grads = [array.reshape(-1) for array in vector_grads]
    else:
        vo_share = spread([piece[:, :, :width] for piece in vo_grad], back_b)
        extra_sum = lax.psum(join(*[piece[:, :, width:] for piece in vo_grad]).astype(F32), "dp")

        def own(array, count):
            return lax.dynamic_slice_in_dim(array, me * count, count, array.ndim - 1)

        vector_grads = own(extra_sum[:, :SHARED, :block].transpose(1, 0, 2).reshape(SHARED, width), rows)
        pair_sums = extra_sum[:, PAIR_ROW, :block].reshape(BLOCKS, 2, block // 2)
        pair_share = own(pair_sums.transpose(1, 0, 2).reshape(2, half), rows // 2)
        up_bias_share = own(extra_sum[:, UP_ROW, : 2 * block].reshape(-1), 2 * rows)
        class_bias_grad = extra_sum[0, CLASS_ROW, :classes]
        vector_grads, class_grad = vector_grads[:7], vector_grads[7:].T
        input_share = jnp.stack([qk_share[:, :half], qk_share[:, half:], vo_share[:, :half]])
        out_share = vo_share[:, half:width].T
    return (
        blocks_out[:, None],
        logits_out[:, None],
        input_grad[:, None],
        input_share.astype(F32),
        pair_share.astype(F32),
        out_share.astype(F32),
        vector_grads[0],
        vector_grads[1],
        vector_grads[2],
        up_share.astype(F32),
        up_bias_share.astype(F32),
        down_share.T.astype(F32),
        vector_grads[5],
        vector_grads[3],
        vector_grads[4],
        pool_grad,
        vector_grads[6],
        class_grad,
        class_bias_grad.astype(F32),
    )


def solution(mesh):
    placed = (
        P(None, "dp", None, None),
        P(None, "dp"),
        P(None, "dp"),
        P(None, "dp", None, None),
        P(None, "dp", "tensor"),
        P(None, ("tensor", "dp")),
        P("tensor", "dp"),
        P("dp"),
        P("dp"),
        P("dp"),
        P("dp", "tensor"),
        P(("tensor", "dp")),
        P("tensor", "dp"),
        P("dp"),
        P("dp"),
        P("dp"),
        P("dp", None),
        P("dp"),
        P("dp", None),
        P(),
    )
    return jax.shard_map(
        per_device,
        mesh=mesh,
        in_specs=placed,
        out_specs=(
            P(None, "dp", None, None),
            P(None, "dp", None),
            P(None, "dp", None, None),
            P(None, "dp", "tensor"),
            P(None, ("tensor", "dp")),
            P("tensor", "dp"),
            P("dp"),
            P("dp"),
            P("dp"),
            P("dp", "tensor"),
            P(("tensor", "dp")),
            P("tensor", "dp"),
            P("dp"),
            P("dp"),
            P("dp"),
            P("dp", None),
            P("dp"),
            P("dp", None),
            P(),
        ),
        check_vma=False,
    )
```

```python
import functools
import math

import jax
import jax.numpy as jnp
from jax import lax
from jax.experimental import pallas as pl
from jax.experimental.pallas import tpu as pltpu
from jax.sharding import PartitionSpec as P

HD = 64
LANES = 128
BLOCKS = 16
EPS = 1e-06
BF = jnp.bfloat16
F32 = jnp.float32
NN = ((1,), (0,))
NT = ((1,), (1,))
TN = ((0,), (0,))
HBM = pl.BlockSpec(memory_space=pltpu.HBM)
SCALARS = pl.BlockSpec(memory_space=pltpu.SMEM)
VMEM = pl.BlockSpec(memory_space=pltpu.VMEM)
MIB = 1024 * 1024
FLOPS_PER_MICROSECOND = 1_150_000_000

OUT_B, GAIN_1, SHIFT_1, DOWN_B, GAIN_2, SHIFT_2, POOL_B, CLASS, QUERY_B, VALUE_B, UP_B = (
    0, 1, 2, 3, 4, 5, 6, 7, 10, 11, 12,
)
SHARED, PAIR_ROW, UP_ROW, CLASS_ROW = 10, 10, 11, 12
NOTES = 16


def dot(left, right, dims=NN):
    return lax.dot_general(left, right, (dims, ((), ())), preferred_element_type=F32)


def begin(source, target, sem):
    copy = pltpu.make_async_copy(source, target, sem)
    copy.start()
    return copy


def row_block(me, mask, rows):
    return pl.ds(pl.multiple_of((me ^ mask) * rows, 16), rows)


def load(pieces, target, sems, columns=None):
    cut, width = pieces[0].shape
    start, width = columns or (0, width)
    for i, piece in enumerate(pieces):
        begin(piece.at[:, pl.ds(start, width)], target.at[i // 2, pl.ds(i % 2 * cut, cut), :], sems.at[i])


def landed(target, sem):
    pltpu.make_async_copy(target, target, sem).wait()


def loaded(target, h, sems):
    cut = target.shape[1] // 2
    for i in range(2):
        landed(target.at[h, pl.ds(i * cut, cut), :], sems.at[2 * h + i])


def to_blocks(source, target, masks, me):
    rows = source.shape[0] // BLOCKS
    for j in range(BLOCKS):
        target[j * rows : (j + 1) * rows, :] = source[row_block(me, masks[j], rows), :]


def to_rows(source, target, masks, me):
    rows = target.shape[0] // BLOCKS
    for j in range(BLOCKS):
        target[row_block(me, masks[j], rows), :] = source[j * rows : (j + 1) * rows, :]


def row_product(matrices, rights):
    return sum(dot(matrices[h], rights[h], NT) for h in range(2))


def pair_product(lefts, rights, lower, upper):
    cut = lefts[0].shape[0] // 2
    columns = rights[0].shape[1]
    for i, target in enumerate((lower, upper)):
        span = slice(i * cut, (i + 1) * cut)
        total = dot(lefts[0][span, :], rights[0][...]) + dot(lefts[1][span, :], rights[1][...])
        target[:, 0:columns] = total.astype(BF)


def mean(array):
    return jnp.mean(array, -1, keepdims=True)


def normalize(total):
    centered = total - mean(total)
    root = lax.rsqrt(mean(centered * centered) + EPS)
    return centered * root, root


def norm_backward(delta, normed, root, gain):
    scaled = delta * gain
    return root * (scaled - mean(scaled) - normed * mean(scaled * normed))


def column_sum(array):
    return jnp.sum(array, 0, keepdims=True)


def unpack_vectors(extra, vec, h):
    width = vec.shape[1]
    rows, part = width // BLOCKS, width // BLOCKS // 2
    for b in range(BLOCKS):
        own = extra[b * rows : b * rows + 16, :]
        if h == 0:
            vec[0:SHARED, b * rows : (b + 1) * rows] = own[0:SHARED, 0:rows]
        at = h * width // 2 + b * part
        vec[QUERY_B : VALUE_B + 1, at : at + part] = own[SHARED : SHARED + 2, 0:part]
        row, at = UP_B + 2 * h + b // (BLOCKS // 2), b % (BLOCKS // 2) * 2 * rows
        vec[row : row + 1, at : at + 2 * rows] = own[SHARED + 2 : SHARED + 3, 0 : 2 * rows]


def pack_vectors(sums, query, value, up, extra):
    width = sums.shape[1]
    rows, part = width // BLOCKS, width // BLOCKS // 2
    extra[...] = jnp.zeros(extra.shape, F32)
    for b in range(BLOCKS):
        top = b * rows
        extra[top : top + SHARED, 0:rows] = sums[0:SHARED, b * rows : (b + 1) * rows]
        at = b * part
        extra[top + PAIR_ROW : top + PAIR_ROW + 1, 0:part] = query[:, at : at + part]
        extra[top + PAIR_ROW : top + PAIR_ROW + 1, part:rows] = value[:, at : at + part]
        at = b * 2 * rows
        extra[top + UP_ROW : top + UP_ROW + 1, 0 : 2 * rows] = up[:, at : at + 2 * rows]
        extra[top + CLASS_ROW : top + CLASS_ROW + 1, :] = sums[SHARED : SHARED + 1, 0:LANES]


def prepare_kernel(masks_p, masks_q, info, hidden, *refs):
    outs, (x_rows, x, other_x, flip, held, sems) = refs[0:4], refs[4:]
    me, core = info[0], info[1]
    begin(hidden.at[core], x, sems.at[0])
    begin(hidden.at[1 - core], other_x, sems.at[1])
    for i, source in enumerate((x, other_x)):
        landed(source, sems.at[i])
        flip[...] = source[...].T
        for n, masks in enumerate((masks_p, masks_q)):
            to_blocks(flip, held.at[2 * i + n], masks, me)
            begin(held.at[2 * i + n], outs[2 * i + n], sems.at[2 + 2 * i + n])
    x_rows[...] = held[0].T
    for i in range(4):
        landed(held.at[i], sems.at[2 + i])


def attend_kernel(masks, info, hidden, x_rows, *refs):
    qk, vo = refs[0:4], refs[4:8]
    q, k, v, att_own, att_other, p, first, first_p = refs[8:16]
    normed, root, vec = refs[16:19]
    x, wa, wb, att, flip, wide, extra, sems = refs[19:]
    me, core = info[0], info[1]
    count = info[2 + core]
    length, width = x.shape
    half = width // 2
    load(vo, wb, sems.at[pl.ds(2, 4)])
    load(qk, wa, sems.at[pl.ds(6, 4)])
    begin(hidden.at[core], x, sems.at[0])
    rows = width // BLOCKS
    for h in range(2):
        loaded(wb, h, sems.at[pl.ds(2, 4)])
        for j in range(BLOCKS):
            piece = wb[h, j * rows : (j + 1) * rows, width:]
            extra[row_block(me, masks[j], rows), :] = piece.astype(F32)
        unpack_vectors(extra, vec, h)
    for h in range(2):
        own = slice(h * half, (h + 1) * half)
        loaded(wa, h, sems.at[pl.ds(6, 4)])
        both = dot(x_rows[...], wa[h])
        q[:, own] = (both[:, :half] + vec[QUERY_B : QUERY_B + 1, own]).astype(BF) * (1.0 / math.sqrt(HD))
        k[:, own] = both[:, half:].astype(BF)
        v[:, own] = (dot(x_rows[...], wb[h, :, 0:half]) + vec[VALUE_B : VALUE_B + 1, own]).astype(BF)
    keys = lax.broadcasted_iota(jnp.int32, (1, length), 1)
    bias = jnp.where(keys < count, 0.0, -1e30).astype(F32)
    lane = lax.broadcasted_iota(jnp.int32, (1, LANES), 1)
    for pair in range(width // LANES):
        cols = slice(pair * LANES, (pair + 1) * LANES)
        q_pair, k_pair, v_pair = q[:, cols], k[:, cols], v[:, cols]
        acc = None
        for a in range(2):
            mine = (lane < HD) if a == 0 else (lane >= HD)
            scores = dot(jnp.where(mine, q_pair, 0.0).astype(BF), k_pair, NT) + bias
            weights = jnp.exp(scores - jnp.max(scores, -1, keepdims=True))
            probs = (weights * (1.0 / jnp.sum(weights, -1, keepdims=True))).astype(BF)
            p[pair, a] = probs
            term = dot(probs, jnp.where(mine, v_pair, 0.0).astype(BF))
            acc = term if acc is None else acc + term
        att[:, cols] = acc.astype(BF)
    att_own[...] = att[:, :half]
    att_other[...] = att[:, half:]
    to_rows(row_product([wb[h, :, half:width] for h in range(2)], (att[:, :half], att[:, half:])), wide, masks, me)
    landed(x, sems.at[0])
    own_normed, own_root = normalize(x[...].astype(F32) + wide[...].T + vec[OUT_B : OUT_B + 1, :])
    normed[...] = own_normed
    root[...] = jnp.broadcast_to(own_root, root.shape)
    low = (own_normed * vec[GAIN_1 : GAIN_1 + 1, :] + vec[SHIFT_1 : SHIFT_1 + 1, :]).astype(BF)
    first[...] = low
    flip[...] = low.T
    to_blocks(flip, first_p, masks, me)


def up_kernel(vec, first_p, *refs):
    pieces = refs[0:4]
    active, other_active, slope, w, sems = refs[4:]
    width = first_p.shape[0]
    half = active.shape[1]
    load(pieces, w, sems, (0, half))
    left = first_p[...].T
    chunk = 256
    for h, target in enumerate((active, other_active)):
        loaded(w, h, sems)
        for c in range(half // chunk):
            cols = slice(c * chunk, (c + 1) * chunk)
            at = h * half + c * chunk
            row, lane = UP_B + at // width, at % width
            hidden = dot(left, w[h, :, cols]) + vec[row : row + 1, lane : lane + chunk]
            cdf = 0.5 + 0.5 * lax.erf(hidden * math.sqrt(0.5))
            density = jnp.exp(hidden * hidden * -0.5) * (1.0 / math.sqrt(2.0 * math.pi))
            target[:, cols] = (hidden * cdf).astype(BF)
            slope[:, at : at + chunk] = (cdf + hidden * density).astype(BF)


def ramp_kernel(masks, pool_masks, back_masks, info, class_bias, vec, cotangent, active, other_active, first, *refs):
    pieces, pool_pieces = refs[0:4], refs[4:8]
    block, ramp, feed_r, feed_back, second, grads = refs[8:14]
    w, cot, right, pool, flip, wide, slim, z, sems = refs[14:]
    me, core = info[0], info[1]
    count, label = info[2 + core], info[4 + core]
    length, width = first.shape
    half = width // 2
    cut = w.shape[2]
    load(pieces, w, sems.at[pl.ds(0, 4)], (0, cut))
    begin(other_active, right, sems.at[8])
    load(pool_pieces, pool, sems.at[pl.ds(4, 4)], (cut, half))
    begin(cotangent.at[core], cot, sems.at[9])
    parts = []
    for i in range(2):
        span = slice(i * half, (i + 1) * half)
        landed(w.at[0, pl.ds(i * half, half), :], sems.at[i])
        parts.append(dot(w[0, span, :], active[...], NT))
    landed(right, sems.at[8])
    for i in range(2):
        span = slice(i * half, (i + 1) * half)
        landed(w.at[1, pl.ds(i * half, half), :], sems.at[2 + i])
        parts[i] = parts[i] + dot(w[1, span, :], right[...], NT)
    to_rows(jnp.concatenate(parts, 0), wide, masks, me)
    total = first[...].astype(F32) + wide[...].T + vec[DOWN_B : DOWN_B + 1, :]
    gain, shift = vec[GAIN_2 : GAIN_2 + 1, :], vec[SHIFT_2 : SHIFT_2 + 1, :]
    normed, root = normalize(total)
    ids = lax.broadcasted_iota(jnp.int32, (length, 1), 0)
    block[...] = jnp.where(ids < count, normed * gain + shift, 0.0).astype(BF)
    for h in range(2):
        loaded(pool, h, sems.at[pl.ds(4, 4)])
    head = (normed[0:8, :] * gain + shift).astype(BF)
    sides = [pl.ds(pl.multiple_of(side * half, LANES), half) for side in (core, 1 - core)]
    slim[:, 0:8] = head.astype(F32).T
    for j in range(BLOCKS):
        at = slice(j * (width // BLOCKS), (j + 1) * (width // BLOCKS))
        slim[at, LANES : LANES + 8] = slim[row_block(me, pool_masks[j], width // BLOCKS), 0:8]
    head_t = slim[:, LANES : LANES + 8].astype(BF)
    for h in range(2):
        z[:, sides[h]] = dot(head_t, pool[h], TN)
    pooled_wide = jnp.tanh(z[...] + vec[POOL_B : POOL_B + 1, :])
    pooled = pooled_wide.astype(BF).astype(F32)
    class_rows = [vec[CLASS + c : CLASS + c + 1, :] for c in range(3)]
    logits = [
        jnp.sum(pooled * class_rows[c], -1, keepdims=True) + class_bias[c] for c in range(3)
    ]
    top = jnp.maximum(jnp.maximum(logits[0], logits[1]), logits[2])
    powers = [jnp.exp(l - top) for l in logits]
    power_sum = powers[0] + powers[1] + powers[2]
    deltas = [powers[c] / power_sum - jnp.where(label == c, 1.0, 0.0) for c in range(3)]
    pre = sum(deltas[c] * class_rows[c] for c in range(3)) * (1.0 - pooled_wide * pooled_wide)
    pre_high = pre.astype(BF)
    z[0:8, :] = pre_high.astype(F32)
    high = [z[:, side].astype(BF) for side in sides]
    z[0:8, :] = pre - pre_high.astype(F32)
    low = [z[:, side].astype(BF) for side in sides]
    slim[:, 0:8] = row_product(pool, high) + row_product(pool, low)
    for j in range(BLOCKS):
        at = slice(j * (width // BLOCKS), (j + 1) * (width // BLOCKS))
        slim[row_block(me, pool_masks[j], width // BLOCKS), LANES : LANES + 8] = slim[at, 0:8]
    head_delta = slim[:, LANES : LANES + 8].T[0:1, :]
    lane = lax.broadcasted_iota(jnp.int32, (1, width), 1)
    tail = jnp.zeros((1, width), F32)
    for c in range(3):
        tail = jnp.where(lane == c, deltas[c][0:1], tail)
        tail = jnp.where(lane == LANES + c, logits[c][0:1], tail)
    ramp[0:1, :] = head[0:1, :].astype(F32)
    ramp[1:2, :] = pooled[0:1, :]
    ramp[2:3, :] = pre[0:1, :]
    ramp[3:4, :] = tail
    ramp[4:8, :] = jnp.zeros((4, width), F32)
    landed(cot, sems.at[9])
    delta = jnp.where(ids < count, cot[...].astype(F32), 0.0) + jnp.where(ids == 0, head_delta, 0.0)
    grads[0:1, :] = column_sum(delta * normed)
    grads[1:2, :] = column_sum(delta)
    dsecond = norm_backward(delta, normed, root, gain)
    grads[2:3, :] = column_sum(dsecond)
    grads[3:4, :] = pre[0:1, :]
    for c in range(3):
        grads[4 + c : 5 + c, :] = deltas[c][0:1] * pooled[0:1, :]
    grads[7:8, :] = tail
    second[...] = dsecond
    flip[...] = dsecond.astype(BF).T
    to_blocks(flip, feed_r, masks, me)
    to_blocks(flip, feed_back, back_masks, me)


def hidden_kernel(feed_r, slope, *refs):
    pieces = refs[0:4]
    delta, other_delta, w, sems = refs[4:]
    half = delta.shape[1]
    load(pieces[2:] + pieces[:2], w, sems, (0, half))
    left = feed_r[...].T
    chunk = 512
    for n, (h, target) in enumerate(((1, other_delta), (0, delta))):
        loaded(w, n, sems)
        for c in range(half // chunk):
            cols = slice(c * chunk, (c + 1) * chunk)
            at = h * half + c * chunk
            target[:, cols] = (dot(left, w[n, :, cols]) * slope[:, at : at + chunk].astype(F32)).astype(BF)


def down_grad_kernel(info, ramp, ramp_other, left_in, left_other_in, right, right_other_in, *refs):
    lower, upper, logits, left, left_other, right_other, sems = refs
    loads = ((left_in, left), (left_other_in, left_other), (right_other_in, right_other))
    for i, (source, target) in enumerate(loads):
        begin(source, target, sems.at[i])
    width, columns = left.shape[0], right.shape[1]
    half = width // 2
    classes = logits.shape[1]
    pair = [r[3:4, LANES : LANES + classes] for r in (ramp, ramp_other)]
    logits[0:1, :] = jnp.where(info[1] == 0, pair[0], pair[1])
    logits[1:2, :] = jnp.where(info[1] == 0, pair[1], pair[0])
    heads = jnp.concatenate([ramp[0:1, :], ramp_other[0:1, :], jnp.zeros((NOTES - 2, width), F32)], 0)
    pres = jnp.concatenate([ramp[2:3, :], ramp_other[2:3, :], jnp.zeros((NOTES - 2, width), F32)], 0)
    upper[half:, :width] = heads.astype(BF)
    upper[half:, width:] = pres.astype(BF)
    for i, (_, target) in enumerate(loads):
        landed(target, sems.at[i])
    for target, span in ((lower, slice(0, half)), (upper, slice(half, width))):
        total = dot(left[span, :], right[...]) + dot(left_other[span, :], right_other[...])
        target[0:half, :] = total.astype(BF)


def up_grad_kernel(left, left_other, right, right_other_in, *refs):
    lower, upper, sums, right_other, sems = refs
    begin(right_other_in, right_other, sems.at[0])
    own_sum = column_sum(right[...].astype(F32))
    landed(right_other, sems.at[0])
    sums[...] = own_sum + column_sum(right_other[...].astype(F32))
    pair_product((left, left_other), (right, right_other), lower, upper)


def branch_kernel(masks_p, masks_q, info, vec, sums_in, delta, other_delta, second, normed, root, *refs):
    up, vo = refs[0:4], refs[4:8]
    total_out, datt, branch_p, grads = refs[8:12]
    wu, wo, right, flip, rows_q, wide, sems = refs[12:]
    me = info[0]
    width = normed.shape[1]
    half = width // 2
    load(up, wu, sems.at[pl.ds(5, 4)], (0, delta.shape[1]))
    begin(other_delta, right, sems.at[4])
    load(vo, wo, sems.at[pl.ds(0, 4)], (half, half))
    gain = vec[GAIN_1 : GAIN_1 + 1, :]
    parts = []
    for i in range(2):
        span = slice(i * half, (i + 1) * half)
        landed(wu.at[0, pl.ds(i * half, half), :], sems.at[5 + i])
        parts.append(dot(wu[0, span, :], delta[...], NT))
    landed(right, sems.at[4])
    for i in range(2):
        span = slice(i * half, (i + 1) * half)
        landed(wu.at[1, pl.ds(i * half, half), :], sems.at[7 + i])
        parts[i] = parts[i] + dot(wu[1, span, :], right[...], NT)
    to_rows(jnp.concatenate(parts, 0), wide, masks_p, me)
    dfirst = second[...] + wide[...].T
    own_normed = normed[...]
    total = norm_backward(dfirst, own_normed, root[:, 0:1], gain)
    total_out[...] = total
    flip[...] = total.astype(BF).T
    to_blocks(flip, branch_p, masks_p, me)
    to_blocks(flip, rows_q, masks_q, me)
    grads[0:1, :] = column_sum(total)
    grads[1:2, :] = column_sum(dfirst * own_normed)
    grads[2:3, :] = column_sum(dfirst)
    grads[3 : SHARED + 1, :] = sums_in[...]
    grads[SHARED + 1 :, :] = jnp.zeros((grads.shape[0] - SHARED - 1, width), F32)
    left = rows_q[...].T
    for h in range(2):
        loaded(wo, h, sems)
        datt[:, h * half : (h + 1) * half] = dot(left, wo[h]).astype(BF)


def back_kernel(q, k, v, att_own, att_other, datt, p, *refs):
    qk_own, v_own, qk_other, v_other = refs[0:4]
    att, dq, dk, dv = refs[4:]
    length, width = q.shape
    half = width // 2
    att[:, :half] = att_own[...]
    att[:, half:] = att_other[...]
    lane = lax.broadcasted_iota(jnp.int32, (1, LANES), 1)
    pairs = width // LANES

    for pair in range(pairs):
        cols = slice(pair * LANES, (pair + 1) * LANES)
        do = datt[:, cols]
        product = do.astype(F32) * att[:, cols].astype(F32)
        k_pair, v_pair = k[:, cols], v[:, cols]
        q_t = q[:, cols].T
        do_t = do.T
        dq_sum = None
        dk_parts, dv_parts = [], []
        for a in range(2):
            mine = (lane < HD) if a == 0 else (lane >= HD)
            shift = jnp.sum(jnp.where(mine, product, 0.0), -1, keepdims=True)
            dprobs = dot(jnp.where(mine, do, 0.0).astype(BF), v_pair, NT)
            probs = p[pair, a]
            dscores = (probs.astype(F32) * (dprobs - shift)).astype(BF)
            term = dot(dscores, jnp.where(mine, k_pair, 0.0).astype(BF))
            dq_sum = term if dq_sum is None else dq_sum + term
            own = slice(a * HD, (a + 1) * HD)
            dk_parts.append(dot(q_t[own], dscores))
            dv_parts.append(dot(do_t[own], probs))
        dq[:, cols] = (dq_sum * (1.0 / math.sqrt(HD))).astype(BF)
        dk[:, cols] = jnp.concatenate(dk_parts, 0).T.astype(BF)
        dv[:, cols] = jnp.concatenate(dv_parts, 0).T.astype(BF)
    for h, (qk, values) in enumerate(((qk_own, v_own), (qk_other, v_other))):
        own = slice(h * half, (h + 1) * half)
        qk[:, :half] = dq[:, own]
        qk[:, half:] = dk[:, own]
        values[...] = dv[:, own]


def out_grad_kernel(branch_t, other_branch_t, att, other_att, grad):
    grad[...] = (dot(branch_t[...], att[...]) + dot(other_branch_t[...], other_att[...])).astype(BF)


def input_grad_kernel(
    masks_p, info, sums_in, sums_other, up_sums, x_p, x_q, other_p, other_q, qk, qk_in, values, values_in, out_grad,
    *refs
):
    qk_pieces, vo_pieces = refs[0:2], refs[2:4]
    extra = refs[4]
    me = info[0]
    width = x_p.shape[0]
    half = width // 2
    rows = width // BLOCKS
    query_sum = column_sum(qk[:, :half].astype(F32)) + column_sum(qk_in[:, :half].astype(F32))
    value_sum = column_sum(values[...].astype(F32)) + column_sum(values_in[...].astype(F32))
    pack_vectors(sums_in[...] + sums_other[...], query_sum, value_sum, up_sums[...], extra)
    for i, target in enumerate(vo_pieces):
        span = slice(i * half, (i + 1) * half)
        total = dot(x_p[span, :], values[...]) + dot(other_p[span, :], values_in[...])
        target[:, 0:half] = total.astype(BF)
        target[:, half:width] = out_grad[span, :]
        for j in range(BLOCKS // 2):
            at = row_block(me, masks_p[i * (BLOCKS // 2) + j], rows)
            target[j * rows : (j + 1) * rows, width:] = extra[at, :].astype(BF)
    pair_product((x_q, other_q), (qk, qk_in), *qk_pieces)


def hop_kernel(*refs):
    sent, kept = refs[-2:]
    at = 0
    for own, arrived in zip(refs[0:-2:2], refs[1:-2:2]):
        half, _, width = sent.shape[0], 0, own.shape[2]
        cols = slice(at, at + width)
        sent[:, :, cols] = own[half:] + arrived[half:]
        kept[:, :, cols] = own[:half] + arrived[:half]
        at += width


def noted_hop_kernel(count, notes, own, arrived, sent, kept):
    cut = sent.shape[0] - NOTES
    sent[0:cut, :] = own[cut:, :] + arrived[cut : 2 * cut, :]
    kept[...] = own[0:cut, :] + arrived[0:cut, :]
    low, high = notes[0:NOTES, :].astype(F32), arrived[2 * cut :, :].astype(F32)
    rows = lax.broadcasted_iota(jnp.int32, (NOTES, 1), 0)
    sent[cut:, :] = jnp.where(rows < count, low, jnp.where(rows < 2 * count, pltpu.roll(high, count, 0), 0.0)).astype(BF)


def ramp_grad_kernel(info, notes, arrived, out, flip):
    rows, width = out.shape
    both = jnp.concatenate([notes[...], arrived[...]], 0).astype(F32)
    flip[...] = both[:, :width].T
    own = flip[pl.ds(pl.multiple_of(info[0] * rows, 16), rows), :].astype(BF)
    out[...] = dot(own, both[:, width:].astype(BF))


def finish_kernel(kept, arrived, input_out, out_out, pair_out, up_out, class_bias_out, class_out, *vectors):
    share = kept[0].astype(F32) + arrived[0].astype(F32)
    rows, half = input_out.shape[1:]
    for i in range(3):
        input_out[i] = share[:, i * half : (i + 1) * half]
    out_out[...] = share[:, 3 * half : 4 * half]
    extra = share[:, 4 * half :]
    for i, target in enumerate(vectors):
        target[...] = extra[i : i + 1, 0:rows]
    pair_out[0:1, :] = extra[PAIR_ROW : PAIR_ROW + 1, 0 : rows // 2]
    pair_out[1:2, :] = extra[PAIR_ROW : PAIR_ROW + 1, rows // 2 : rows]
    up_out[...] = extra[UP_ROW : UP_ROW + 1, 0 : 2 * rows]
    class_bias_out[...] = extra[CLASS_ROW : CLASS_ROW + 1, 0 : class_bias_out.shape[1]]
    class_out[...] = extra[len(vectors) : SHARED, 0:rows]


def arrange_kernel(info, block_own, block_other, grad_own, grad_other, block_out, grad_out, held, sems):
    core = info[1]
    moves = (
        (block_own, block_out, core),
        (block_other, block_out, 1 - core),
        (grad_own, grad_out, core),
        (grad_other, grad_out, 1 - core),
    )
    for i, (source, _, _) in enumerate(moves):
        begin(source, held.at[i], sems.at[i])
    for i, (_, target, side) in enumerate(moves):
        landed(held.at[i], sems.at[i])
        begin(held.at[i], target.at[side], sems.at[4 + i])
    for i in range(4):
        landed(held.at[i], sems.at[4 + i])


def input_kernel(masks_p, masks_q, info, qk_own, v_own, qk_other, v_other, total, *refs):
    qk, vo = refs[0:4], refs[4:8]
    out, wa, wv, wide, wide_v, sems = refs[8:]
    me = info[0]
    width = total.shape[1]
    half = width // 2
    load(vo, wv, sems.at[pl.ds(0, 4)], (0, half))
    load(qk, wa, sems.at[pl.ds(4, 4)])
    for h in range(2):
        loaded(wv, h, sems.at[pl.ds(0, 4)])
    to_rows(row_product(wv, (v_own[...], v_other[...])), wide_v, masks_q, me)
    for h in range(2):
        loaded(wa, h, sems.at[pl.ds(4, 4)])
    to_rows(row_product(wa, (qk_own[...], qk_other[...])), wide, masks_p, me)
    out[...] = (total[...] + (wide[...] + wide_v[...]).T).astype(BF)


def costing(micros):
    return pl.CostEstimate(flops=micros * FLOPS_PER_MICROSECOND, bytes_accessed=1024, transcendentals=0)


def call(body, name, micros, mib, in_specs, outs, scratch, sems, args):
    return pl.pallas_call(
        body,
        name=name,
        in_specs=in_specs,
        out_specs=[spec for _, spec in outs],
        out_shape=[shape for shape, _ in outs],
        scratch_shapes=[pltpu.VMEM(s, d) for s, d in scratch] + [pltpu.SemaphoreType.DMA((sems,))] * (sems > 0),
        compiler_params=pltpu.CompilerParams(vmem_limit_bytes=mib * MIB),
        cost_estimate=costing(micros),
    )(*args)


def orders(size):
    bits = [1 << k for k in range(size.bit_length() - 1)]
    high = bits[2:][::-1]
    x_last, y_last = high + [2, 1], high + [1, 2]
    return (x_last, x_last, x_last, [1] + high + [2]), (y_last, x_last, x_last, [1] + high + [2])


def block_mask(index, order):
    mask = 0
    for k, bit in enumerate(order):
        if (index >> k) & 1:
            mask ^= bit
    return mask


def swap(array, mask):
    size = lax.axis_size("dp")
    return lax.ppermute(array, "dp", [(i, i ^ mask) for i in range(size)])


def swap_core(array):
    return lax.ppermute(array, "tensor", [(0, 1), (1, 0)])


def after(array, *others):
    return lax.optimization_barrier((array, *others))[0]


def join(left, right):
    return jnp.concatenate([left, right], 0)


def gather_blocks(shard, order):
    held = shard[None]
    for mask in order:
        held = join(held, swap(held, mask))
    return held


def hop(blocks, arrived):
    half = blocks.shape[0] // 2
    return blocks[half:] + arrived[half:], blocks[:half] + arrived[:half]


def scatter_blocks(blocks, order):
    for mask in order[::-1]:
        half = blocks.shape[0] // 2
        blocks = blocks[:half] + swap(blocks[half:], mask)
    return blocks[0]


def in_order(blocks, order, me):
    size = len(blocks)
    place = [0] * size
    for j in range(size):
        place[block_mask(j, order)] = j
    chosen = jnp.array(place)[jnp.arange(size) ^ me]
    return jnp.take(blocks, chosen, axis=0)


def out_of_order(blocks, order, me):
    owners = jnp.array([block_mask(j, order) for j in range(len(blocks))]) ^ me
    return jnp.take(blocks, owners, axis=0)


def extra_columns(shared, pair, up, rows):
    def lanes(array):
        return jnp.pad(array, ((0, 0), (0, 0), (0, LANES - array.shape[2])))

    columns = jnp.concatenate([lanes(shared), lanes(pair), lanes(up)], 1)
    return jnp.pad(columns, ((0, 0), (0, rows - columns.shape[1]), (0, 0)))


def per_device(
    hidden_in,
    lengths,
    labels,
    out_cot,
    input_weight,
    input_bias,
    out_weight,
    out_bias,
    first_gain,
    first_shift,
    up_weight,
    up_bias,
    down_weight,
    down_bias,
    second_gain,
    second_shift,
    pool_weight,
    pool_bias,
    class_weight,
    class_bias,
):
    size = lax.axis_size("dp")
    me = lax.axis_index("dp")
    core = lax.axis_index("tensor")
    length, width = hidden_in.shape[2:]
    rows = width // size
    half = input_weight.shape[2]
    hidden_half = up_weight.shape[1]
    hidden_width = 2 * hidden_half
    classes = class_bias.shape[0]
    pairs = width // LANES
    block = width // BLOCKS
    lower = BLOCKS // 2
    direct = size == BLOCKS
    (order_a, order_b, order_u, order_d), (back_a, back_b, back_u, back_d) = orders(size)

    def kernel_masks(order):
        return [block_mask(j, order) if direct else j for j in range(BLOCKS)]

    (a_masks, b_masks, u_masks, d_masks), back_masks = [[kernel_masks(o) for o in part] for part in orders(size)]

    inputs = hidden_in.reshape(2, length, width)
    cotangents = out_cot.reshape(2, length, width)
    info = jnp.concatenate(
        [
            jnp.stack([me if direct else jnp.zeros_like(me), core]).astype(jnp.int32),
            lengths.reshape(-1),
            labels.reshape(-1),
        ]
    )

    def shape(*dims, dtype=BF):
        return jax.ShapeDtypeStruct(dims, dtype)

    def of(s):
        return (s.shape, s.dtype)

    def in_vmem(*shapes):
        return [(s, VMEM) for s in shapes]

    def in_hbm(*shapes):
        return [(s, HBM) for s in shapes]

    row = shape(length, width)
    flat = shape(width, length)
    x_p, x_q, other_p, other_q, x_rows = call(
        functools.partial(prepare_kernel, back_masks[1], back_masks[0]),
        "prepare",
        0,
        8,
        [SCALARS, HBM],
        in_hbm(flat, flat, flat, flat) + in_vmem(row),
        [of(row), of(row), of(flat), ((4, width, length), BF)],
        6,
        (info, inputs),
    )

    pool_half = lax.dynamic_slice_in_dim(pool_weight, core * half, half, 1)
    a_shard = jnp.concatenate([input_weight[0], input_weight[1]], 1)
    vo_shard = jnp.concatenate([input_weight[2], out_weight.T], 1)
    u_shard = up_weight
    d_shard = jnp.concatenate([down_weight.T, pool_half], 1)
    shared = jnp.concatenate(
        [
            jnp.stack(
                [out_bias, first_gain, first_shift, down_bias, second_gain, second_shift, pool_bias]
            ),
            class_weight.T,
        ],
        0,
    )
    def with_other(lo, hi):
        return flat_rows(lo, hi, swap_core(lo), swap_core(hi))

    def flat_rows(*arrays):
        return tuple(array.reshape(-1, array.shape[2]) for array in arrays)

    def by_block(arrays):
        return [array.reshape(lower, block, array.shape[1]) for array in arrays]

    if direct:
        extra = extra_columns(
            shared[None], input_bias[None], up_bias.reshape(1, 1, 2 * rows), rows
        )
        b_shard = jnp.concatenate([vo_shard, after(extra, a_shard)[0]], 1)
        a0, b0, u0, d0 = a_shard[None], b_shard[None], u_shard[None], d_shard[None]
        z1, z0 = order_a[0], order_a[1]
        a1, b1, d1 = swap(a0, z1), swap(b0, z1), swap(d0, 1)
        a2, b2 = join(a0, a1), join(b0, b1)
        a2_in, b2_in = swap(a2, z0), swap(b2, z0)
        u1 = swap(after(u0, a2, b2), z1)
        a4, b4 = join(a2, a2_in), join(b2, b2_in)
        a4_in, b4_in = swap(a4, 2), swap(b4, 2)
        u2 = after(join(u0, u1), a4, b4)
        u2_in = swap(u2, z0)
        a8, b8 = join(a4, a4_in), join(b4, b4_in)
        a8_in, b8_in = swap(a8, 1), swap(b8, 1)
        u4 = after(join(u2, u2_in), a8, b8)
        d2 = after(join(d0, d1), a4, b4)
        u4_in, d2_in = swap(u4, 2), swap(d2, z1)
        d4 = after(join(d2, d2_in), u4, a8_in, x_rows)
        d4_in = swap(d4, z0)
        a8_other, b8_other = swap_core(a8), swap_core(b8)
        u8 = after(join(u4, u4_in), a8_in, b8_in, d4)
        u8_in = swap(u8, 1)
        d8 = after(join(d4, d4_in), u8)
        d8_in = swap(d8, 2)
        info = after(info, u8, d8)
        qk = flat_rows(a8, a8_in, a8_other, swap_core(a8_in))
        vo = flat_rows(b8, b8_in, b8_other, swap_core(b8_in))
        pieces = [(u8, u8_in), (d8, d8_in)]
    else:

        def whole(shard, order):
            return in_order(gather_blocks(shard, order), order, me)

        def cut(array):
            blocks = array.reshape(BLOCKS, block, -1)
            return blocks[:lower], blocks[lower:]

        shared = whole(shared, order_a).transpose(1, 0, 2).reshape(-1, BLOCKS, block)
        pair = whole(input_bias, order_a).transpose(1, 0, 2).reshape(2, BLOCKS, block // 2)
        extra = extra_columns(
            shared.transpose(1, 0, 2),
            pair.transpose(1, 0, 2),
            whole(up_bias, order_a).reshape(BLOCKS, 1, 2 * block),
            block,
        )
        vo = cut(whole(vo_shard, order_b))
        vo = jnp.concatenate([vo[0], extra[:lower]], 2), jnp.concatenate([vo[1], extra[lower:]], 2)
        qk, vo = with_other(*cut(whole(a_shard, order_a))), with_other(*vo)
        pieces = [cut(whole(u_shard, order_u)), cut(whole(d_shard, order_d))]

    wide = shape(length, hidden_width)
    norm = shape(length, width, dtype=F32)
    roots = shape(length, LANES, dtype=F32)
    eight = shape(8, width, dtype=F32)
    vectors = shape(16, width, dtype=F32)
    probs = shape(pairs, 2, length, length)

    def grad(columns):
        return [shape(half, columns)] * 2

    part = width + LANES
    slim = shape(length, half)
    halved = shape(length, hidden_half)
    thirds = shape(length, 3 * half)
    matrix = shape(width, hidden_width)

    def blocks_of(columns):
        return shape(2, width, columns)

    q, k, v, att, att_other, p, first, first_p, normed, root, vec = call(
        functools.partial(attend_kernel, a_masks),
        "attend",
        0,
        18,
        [SCALARS, HBM, VMEM] + [HBM] * 8,
        in_vmem(row, row, row, slim, slim, probs, row, flat, norm, roots, vectors),
        [of(row), of(blocks_of(width)), of(blocks_of(part)), of(row), of(flat), ((width, length), F32)]
        + [((width, LANES), F32)],
        10,
        (info, inputs, x_rows, *qk, *vo),
    )
    (up_lo, up_hi), (down_lo, down_hi) = pieces
    up = with_other(up_lo, after(up_hi, first))
    first_in, att_in = swap_core(first_p), swap_core(att_other)
    act, act_other, slope = call(
        up_kernel,
        "up",
        0,
        8,
        [VMEM, VMEM] + [HBM] * 4,
        in_vmem(halved, halved, wide),
        [of(blocks_of(hidden_half))],
        4,
        (vec, first_p, *up),
    )
    act_in = swap_core(act_other)
    down = with_other(down_lo, after(down_hi, act))
    block_out, ramp, feed, feed_back, second, sums_two = call(
        functools.partial(ramp_kernel, d_masks, d_masks, back_masks[3]),
        "ramp",
        15,
        18,
        [SCALARS, SCALARS, VMEM, HBM, VMEM, HBM, VMEM] + [HBM] * 8,
        in_vmem(row, eight, flat, flat, norm, eight),
        [of(blocks_of(hidden_half)), of(row), of(halved), of(blocks_of(half)), of(flat), ((width, length), F32), ((width, 2 * LANES), F32)]
        + [of(eight)],
        10,
        (info, class_bias.astype(F32), vec, cotangents, act, act_other, first, *down, *down),
    )
    feed_in, ramp_in = swap_core(feed_back), swap_core(ramp)
    delta, delta_other = call(
        hidden_kernel,
        "hidden",
        400,
        9,
        [VMEM] * 2 + [HBM] * 4,
        in_vmem(halved, halved),
        [of(blocks_of(hidden_half))],
        4,
        (after(feed, act_in, first_in, att_in), slope, *down),
    )
    delta_in = swap_core(delta_other)
    *down_grad, logits_out = call(
        down_grad_kernel,
        "down_grad",
        400,
        6,
        [SCALARS, VMEM, VMEM, HBM, HBM, VMEM, HBM],
        in_vmem(shape(half, hidden_half), shape(half + NOTES, hidden_half), shape(2, classes, dtype=F32)),
        [of(flat), of(flat), of(halved)],
        3,
        (after(info, delta), ramp, ramp_in, feed_back, feed_in, act, act_in),
    )

    def first_hop(pieces, order):
        return swap(pieces[1], order[-1]) if direct else None

    def add(*streams):
        columns = sum(own.shape[2] for own, _ in streams)
        return call(
            hop_kernel,
            "hop",
            0,
            2,
            [VMEM] * (2 * len(streams)),
            in_vmem(*[shape(streams[0][0].shape[0] // 2, block, columns)] * 2),
            [],
            0,
            tuple(array for stream in streams for array in stream),
        )

    def next_hop(kept, arrived, mask, start):
        if not direct:
            return kept, None
        sent, kept = add((after(kept, start), arrived))
        return kept, swap(sent, mask)

    down_arrived = swap(down_grad[1], back_d[-1]) if direct else None

    def noted_hop(kept, notes, arrived, k, start):
        if not direct:
            return kept, notes, None
        cut = kept.shape[0] // 2
        sent, kept = call(
            functools.partial(noted_hop_kernel, 2 << (2 - k)),
            "noted_hop",
            0,
            4,
            [VMEM] * 3,
            in_vmem(shape(cut + NOTES, hidden_half), shape(cut, hidden_half)),
            [],
            0,
            (notes, after(kept, start), arrived),
        )
        return kept, sent[cut:], swap(sent, back_d[k])

    *up_grad, up_sums = call(
        up_grad_kernel,
        "up_grad",
        0,
        6,
        [VMEM] * 3 + [HBM],
        in_vmem(*grad(hidden_half), shape(1, hidden_half, dtype=F32)),
        [of(halved)],
        1,
        (after(first_p, down_grad[0]), first_in, delta, delta_in),
    )
    up_grad = by_block(up_grad)
    up_arrived = first_hop(up_grad, back_u)
    block_in = swap_core(after(block_out, up_sums))
    total, datt, branch, sums_one = call(
        functools.partial(branch_kernel, u_masks, b_masks),
        "branch",
        0,
        16,
        [SCALARS] + [VMEM] * 3 + [HBM] + [VMEM] * 3 + [HBM] * 8,
        in_vmem(norm, row, flat, vectors),
        [of(blocks_of(hidden_half)), of(blocks_of(half)), of(halved), of(flat), of(flat), ((width, length), F32)],
        9,
        (after(info, up_grad[0]), vec, sums_two, delta, delta_other, second, normed, root, *up, *vo),
    )
    branch_in, sums_in = swap_core(branch), swap_core(sums_one)
    dqk, dv, dqk_other, dv_other = call(
        back_kernel,
        "back",
        0,
        10,
        [VMEM] * 7,
        in_vmem(row, slim, row, slim),
        [of(row)] * 4,
        0,
        (q, k, v, att, att_other, after(datt, block_in), p),
    )
    dqk_in, dv_in = swap_core(dqk_other), swap_core(dv_other)
    (input_delta,) = call(
        functools.partial(input_kernel, a_masks, b_masks),
        "input",
        0,
        9,
        [SCALARS] + [VMEM] * 5 + [HBM] * 8,
        in_vmem(row),
        [of(blocks_of(width)), of(blocks_of(half)), ((width, length), F32), ((width, length), F32)],
        8,
        (info, dqk, dv, dqk_other, dv_other, total, *qk, *vo),
    )
    (out_grad,) = call(
        out_grad_kernel,
        "out_grad",
        0,
        3,
        [VMEM] * 4,
        in_vmem(shape(width, half)),
        [],
        0,
        (after(branch, dqk, sums_in, input_delta), branch_in, att, att_in),
    )
    up_sent, up_kept = add((after(up_grad[0], out_grad), up_arrived)) if direct else (None, up_grad[0])
    input_grads = call(
        functools.partial(input_grad_kernel, back_masks[1]),
        "input_grad",
        0,
        4,
        [SCALARS] + [VMEM] * 12,
        in_vmem(*grad(width), *grad(part)),
        [((width, LANES), F32)],
        0,
        (after(info, up_kept), sums_one, sums_in, up_sums, x_p, x_q, other_p, other_q, dqk, dqk_in, dv, dv_in, out_grad),
    )
    qk_grad, vo_grad = by_block(input_grads[:2]), by_block(input_grads[2:])
    qk_arrived, vo_arrived = first_hop(qk_grad, back_a), first_hop(vo_grad, back_b)
    input_delta_in = swap_core(input_delta)
    down_kept, notes, down_arrived = noted_hop(down_grad[0], down_grad[1][half:], down_arrived, 2, qk_grad[0])
    vo_kept, vo_arrived = next_hop(vo_grad[0], vo_arrived, back_b[2], down_kept)
    qk_kept, qk_arrived = next_hop(qk_grad[0], qk_arrived, back_a[2], vo_kept)
    up_arrived = swap(after(up_sent, qk_kept), back_u[2]) if direct else None
    down_kept, notes, down_arrived = noted_hop(down_kept, notes, down_arrived, 1, qk_kept)
    blocks_out, input_grad = call(
        arrange_kernel,
        "arrange",
        0,
        4,
        [SCALARS] + [HBM] * 4,
        in_hbm(*[shape(2, length, width)] * 2),
        [((4, length, width), BF)],
        8,
        (after(info, qk_kept), block_out, block_in, input_delta, input_delta_in),
    )
    if direct:
        sent, kept = add((after(qk_kept, blocks_out), qk_arrived), (vo_kept, vo_arrived))
        arrived = swap(sent, back_a[1])
        up_kept, up_arrived = next_hop(up_kept, up_arrived, back_u[1], kept)
        down_kept, notes, down_arrived = noted_hop(down_kept, notes, down_arrived, 0, up_kept)
        sent, kept = add((after(kept, down_kept), arrived))
        arrived = swap(sent, back_a[0])
        up_kept, up_arrived = next_hop(up_kept, up_arrived, back_u[0], kept)
        down_kept, up_kept = after(down_kept, kept), after(up_kept, kept)
        down_share, up_share = down_kept + down_arrived[:rows], (up_kept + up_arrived)[0]
        (pool_grad,) = call(
            ramp_grad_kernel,
            "ramp_grad",
            0,
            2,
            [SCALARS, VMEM, VMEM],
            in_vmem(shape(rows, width, dtype=F32)),
            [((width, 2 * NOTES), F32)],
            0,
            (info, notes, after(down_arrived[rows:], kept)),
        )
        kept = after(kept, down_share, up_share)
    else:

        def spread(pieces, order):
            return scatter_blocks(out_of_order(join(*pieces).reshape(size, rows, -1), order, me), order)

        down_halves = by_block([down_grad[0], down_grad[1][:half]])
        down_share, up_share = spread(down_halves, back_d), spread(up_grad, back_u)
        notes = lax.all_gather(down_grad[1][half : half + 2], "dp", axis=0, tiled=True)
        own_heads = lax.dynamic_slice_in_dim(notes[:, :width], me * rows, rows, 1)
        pool_grad = dot(own_heads, notes[:, width:], TN)
        qk_share = spread(qk_grad, back_a)
    if direct:
        input_share, out_share, pair_share, up_bias_share, class_bias_grad, class_grad, *vector_grads = call(
            finish_kernel,
            "finish",
            0,
            2,
            [VMEM] * 2,
            in_vmem(
                shape(3, rows, half, dtype=F32),
                shape(rows, half, dtype=F32),
                shape(2, rows // 2, dtype=F32),
                shape(1, 2 * rows, dtype=F32),
                shape(1, classes, dtype=F32),
                shape(classes, rows, dtype=F32),
                *[shape(1, rows, dtype=F32)] * 7,
            ),
            [],
            0,
            (kept, arrived),
        )
        out_share, class_grad = out_share.T, class_grad.T
        up_bias_share, class_bias_grad = up_bias_share.reshape(-1), class_bias_grad.reshape(-1)
        vector_grads = [array.reshape(-1) for array in vector_grads]
    else:
        vo_share = spread([piece[:, :, :width] for piece in vo_grad], back_b)
        extra_sum = lax.psum(join(*[piece[:, :, width:] for piece in vo_grad]).astype(F32), "dp")

        def own(array, count):
            return lax.dynamic_slice_in_dim(array, me * count, count, array.ndim - 1)

        vector_grads = own(extra_sum[:, :SHARED, :block].transpose(1, 0, 2).reshape(SHARED, width), rows)
        pair_sums = extra_sum[:, PAIR_ROW, :block].reshape(BLOCKS, 2, block // 2)
        pair_share = own(pair_sums.transpose(1, 0, 2).reshape(2, half), rows // 2)
        up_bias_share = own(extra_sum[:, UP_ROW, : 2 * block].reshape(-1), 2 * rows)
        class_bias_grad = extra_sum[0, CLASS_ROW, :classes]
        vector_grads, class_grad = vector_grads[:7], vector_grads[7:].T
        input_share = jnp.stack([qk_share[:, :half], qk_share[:, half:], vo_share[:, :half]])
        out_share = vo_share[:, half:width].T
    return (
        blocks_out[:, None],
        logits_out[:, None],
        input_grad[:, None],
        input_share.astype(F32),
        pair_share.astype(F32),
        out_share.astype(F32),
        vector_grads[0],
        vector_grads[1],
        vector_grads[2],
        up_share.astype(F32),
        up_bias_share.astype(F32),
        down_share.T.astype(F32),
        vector_grads[5],
        vector_grads[3],
        vector_grads[4],
        pool_grad,
        vector_grads[6],
        class_grad,
        class_bias_grad.astype(F32),
    )


def solution(mesh):
    placed = (
        P(None, "dp", None, None),
        P(None, "dp"),
        P(None, "dp"),
        P(None, "dp", None, None),
        P(None, "dp", "tensor"),
        P(None, ("tensor", "dp")),
        P("tensor", "dp"),
        P("dp"),
        P("dp"),
        P("dp"),
        P("dp", "tensor"),
        P(("tensor", "dp")),
        P("tensor", "dp"),
        P("dp"),
        P("dp"),
        P("dp"),
        P("dp", None),
        P("dp"),
        P("dp", None),
        P(),
    )
    return jax.shard_map(
        per_device,
        mesh=mesh,
        in_specs=placed,
        out_specs=(
            P(None, "dp", None, None),
            P(None, "dp", None),
            P(None, "dp", None, None),
            P(None, "dp", "tensor"),
            P(None, ("tensor", "dp")),
            P("tensor", "dp"),
            P("dp"),
            P("dp"),
            P("dp"),
            P("dp", "tensor"),
            P(("tensor", "dp")),
            P("tensor", "dp"),
            P("dp"),
            P("dp"),
            P("dp"),
            P("dp", None),
            P("dp"),
            P("dp", None),
            P(),
        ),
        check_vma=False,
    )
```

```python
import functools
import math

import jax
import jax.numpy as jnp
from jax import lax
from jax.experimental import pallas as pl
from jax.experimental.pallas import tpu as pltpu
from jax.sharding import PartitionSpec as P

HD = 64
LANES = 128
BLOCKS = 16
EPS = 1e-06
BF = jnp.bfloat16
F32 = jnp.float32
NN = ((1,), (0,))
NT = ((1,), (1,))
TN = ((0,), (0,))
HBM = pl.BlockSpec(memory_space=pltpu.HBM)
SCALARS = pl.BlockSpec(memory_space=pltpu.SMEM)
VMEM = pl.BlockSpec(memory_space=pltpu.VMEM)
MIB = 1024 * 1024
FLOPS_PER_MICROSECOND = 1_150_000_000

OUT_B, GAIN_1, SHIFT_1, DOWN_B, GAIN_2, SHIFT_2, POOL_B, CLASS, QUERY_B, VALUE_B, UP_B = (
    0, 1, 2, 3, 4, 5, 6, 7, 10, 11, 12,
)
SHARED, PAIR_ROW, UP_ROW, CLASS_ROW = 10, 10, 11, 12
NOTES = 16


def dot(left, right, dims=NN):
    return lax.dot_general(left, right, (dims, ((), ())), preferred_element_type=F32)


def begin(source, target, sem):
    copy = pltpu.make_async_copy(source, target, sem)
    copy.start()
    return copy


def row_block(me, mask, rows):
    return pl.ds(pl.multiple_of((me ^ mask) * rows, 16), rows)


def load(pieces, target, sems, columns=None):
    cut, width = pieces[0].shape
    start, width = columns or (0, width)
    for i, piece in enumerate(pieces):
        begin(piece.at[:, pl.ds(start, width)], target.at[i // 2, pl.ds(i % 2 * cut, cut), :], sems.at[i])


def landed(target, sem):
    pltpu.make_async_copy(target, target, sem).wait()


def loaded(target, h, sems):
    cut = target.shape[1] // 2
    for i in range(2):
        landed(target.at[h, pl.ds(i * cut, cut), :], sems.at[2 * h + i])


def to_blocks(source, target, masks, me):
    rows = source.shape[0] // BLOCKS
    for j in range(BLOCKS):
        target[j * rows : (j + 1) * rows, :] = source[row_block(me, masks[j], rows), :]


def to_rows(source, target, masks, me):
    rows = target.shape[0] // BLOCKS
    for j in range(BLOCKS):
        target[row_block(me, masks[j], rows), :] = source[j * rows : (j + 1) * rows, :]


def row_product(matrices, rights):
    return sum(dot(matrices[h], rights[h], NT) for h in range(2))


def pair_product(lefts, rights, lower, upper):
    cut = lefts[0].shape[0] // 2
    columns = rights[0].shape[1]
    for i, target in enumerate((lower, upper)):
        span = slice(i * cut, (i + 1) * cut)
        total = dot(lefts[0][span, :], rights[0][...]) + dot(lefts[1][span, :], rights[1][...])
        target[:, 0:columns] = total.astype(BF)


def mean(array):
    return jnp.mean(array, -1, keepdims=True)


def normalize(total):
    centered = total - mean(total)
    root = lax.rsqrt(mean(centered * centered) + EPS)
    return centered * root, root


def norm_backward(delta, normed, root, gain):
    scaled = delta * gain
    return root * (scaled - mean(scaled) - normed * mean(scaled * normed))


def column_sum(array):
    return jnp.sum(array, 0, keepdims=True)


def unpack_vectors(extra, vec, h):
    width = vec.shape[1]
    rows, part = width // BLOCKS, width // BLOCKS // 2
    for b in range(BLOCKS):
        own = extra[b * rows : b * rows + 16, :]
        if h == 0:
            vec[0:SHARED, b * rows : (b + 1) * rows] = own[0:SHARED, 0:rows]
        at = h * width // 2 + b * part
        vec[QUERY_B : VALUE_B + 1, at : at + part] = own[SHARED : SHARED + 2, 0:part]
        row, at = UP_B + 2 * h + b // (BLOCKS // 2), b % (BLOCKS // 2) * 2 * rows
        vec[row : row + 1, at : at + 2 * rows] = own[SHARED + 2 : SHARED + 3, 0 : 2 * rows]


def pack_vectors(sums, query, value, up, extra):
    width = sums.shape[1]
    rows, part = width // BLOCKS, width // BLOCKS // 2
    extra[...] = jnp.zeros(extra.shape, F32)
    for b in range(BLOCKS):
        top = b * rows
        extra[top : top + SHARED, 0:rows] = sums[0:SHARED, b * rows : (b + 1) * rows]
        at = b * part
        extra[top + PAIR_ROW : top + PAIR_ROW + 1, 0:part] = query[:, at : at + part]
        extra[top + PAIR_ROW : top + PAIR_ROW + 1, part:rows] = value[:, at : at + part]
        at = b * 2 * rows
        extra[top + UP_ROW : top + UP_ROW + 1, 0 : 2 * rows] = up[:, at : at + 2 * rows]
        extra[top + CLASS_ROW : top + CLASS_ROW + 1, :] = sums[SHARED : SHARED + 1, 0:LANES]


def prepare_kernel(masks_p, masks_q, info, hidden, *refs):
    outs, (x_rows, x, other_x, flip, held, sems) = refs[0:4], refs[4:]
    me, core = info[0], info[1]
    begin(hidden.at[core], x, sems.at[0])
    begin(hidden.at[1 - core], other_x, sems.at[1])
    for i, source in enumerate((x, other_x)):
        landed(source, sems.at[i])
        flip[...] = source[...].T
        for n, masks in enumerate((masks_p, masks_q)):
            to_blocks(flip, held.at[2 * i + n], masks, me)
            begin(held.at[2 * i + n], outs[2 * i + n], sems.at[2 + 2 * i + n])
    x_rows[...] = held[0].T
    for i in range(4):
        landed(held.at[i], sems.at[2 + i])


def attend_kernel(masks, back_masks, info, hidden, x_rows, *refs):
    qk, vo = refs[0:4], refs[4:8]
    q, k, v, att_own, att_other, p, first, first_p, first_back = refs[8:17]
    normed, root, vec = refs[17:20]
    x, wa, wb, att, flip, wide, extra, sems = refs[20:]
    me, core = info[0], info[1]
    count = info[2 + core]
    length, width = x.shape
    half = width // 2
    load(vo, wb, sems.at[pl.ds(2, 4)])
    load(qk, wa, sems.at[pl.ds(6, 4)])
    begin(hidden.at[core], x, sems.at[0])
    rows = width // BLOCKS
    for h in range(2):
        loaded(wb, h, sems.at[pl.ds(2, 4)])
        for j in range(BLOCKS):
            piece = wb[h, j * rows : (j + 1) * rows, width:]
            extra[row_block(me, masks[j], rows), :] = piece.astype(F32)
        unpack_vectors(extra, vec, h)
    for h in range(2):
        own = slice(h * half, (h + 1) * half)
        loaded(wa, h, sems.at[pl.ds(6, 4)])
        both = dot(x_rows[...], wa[h])
        q[:, own] = (both[:, :half] + vec[QUERY_B : QUERY_B + 1, own]).astype(BF) * (1.0 / math.sqrt(HD))
        k[:, own] = both[:, half:].astype(BF)
        v[:, own] = (dot(x_rows[...], wb[h, :, 0:half]) + vec[VALUE_B : VALUE_B + 1, own]).astype(BF)
    keys = lax.broadcasted_iota(jnp.int32, (1, length), 1)
    bias = jnp.where(keys < count, 0.0, -1e30).astype(F32)
    lane = lax.broadcasted_iota(jnp.int32, (1, LANES), 1)
    for pair in range(width // LANES):
        cols = slice(pair * LANES, (pair + 1) * LANES)
        q_pair, k_pair, v_pair = q[:, cols], k[:, cols], v[:, cols]
        acc = None
        for a in range(2):
            mine = (lane < HD) if a == 0 else (lane >= HD)
            scores = dot(jnp.where(mine, q_pair, 0.0).astype(BF), k_pair, NT) + bias
            weights = jnp.exp(scores - jnp.max(scores, -1, keepdims=True))
            probs = (weights * (1.0 / jnp.sum(weights, -1, keepdims=True))).astype(BF)
            p[pair, a] = probs
            term = dot(probs, jnp.where(mine, v_pair, 0.0).astype(BF))
            acc = term if acc is None else acc + term
        att[:, cols] = acc.astype(BF)
    att_own[...] = att[:, :half]
    att_other[...] = att[:, half:]
    to_rows(row_product([wb[h, :, half:width] for h in range(2)], (att[:, :half], att[:, half:])), wide, masks, me)
    landed(x, sems.at[0])
    own_normed, own_root = normalize(x[...].astype(F32) + wide[...].T + vec[OUT_B : OUT_B + 1, :])
    normed[...] = own_normed
    root[...] = jnp.broadcast_to(own_root, root.shape)
    low = (own_normed * vec[GAIN_1 : GAIN_1 + 1, :] + vec[SHIFT_1 : SHIFT_1 + 1, :]).astype(BF)
    first[...] = low
    flip[...] = low.T
    to_blocks(flip, first_p, masks, me)
    to_blocks(flip, first_back, back_masks, me)


def up_kernel(vec, first_p, *refs):
    pieces = refs[0:4]
    active, other_active, slope, w, sems = refs[4:]
    width = first_p.shape[0]
    half = active.shape[1]
    load(pieces, w, sems, (0, half))
    left = first_p[...].T
    chunk = 256
    for h, target in enumerate((active, other_active)):
        loaded(w, h, sems)
        for c in range(half // chunk):
            cols = slice(c * chunk, (c + 1) * chunk)
            at = h * half + c * chunk
            row, lane = UP_B + at // width, at % width
            hidden = dot(left, w[h, :, cols]) + vec[row : row + 1, lane : lane + chunk]
            cdf = 0.5 + 0.5 * lax.erf(hidden * math.sqrt(0.5))
            density = jnp.exp(hidden * hidden * -0.5) * (1.0 / math.sqrt(2.0 * math.pi))
            target[:, cols] = (hidden * cdf).astype(BF)
            slope[:, at : at + chunk] = (cdf + hidden * density).astype(BF)


def ramp_kernel(masks, pool_masks, back_masks, info, class_bias, vec, cotangent, active, other_active, first, *refs):
    pieces, pool_pieces = refs[0:4], refs[4:8]
    block, ramp, feed_r, feed_back, second, grads = refs[8:14]
    w, cot, right, pool, flip, wide, slim, z, sems = refs[14:]
    me, core = info[0], info[1]
    count, label = info[2 + core], info[4 + core]
    length, width = first.shape
    half = width // 2
    cut = w.shape[2]
    load(pieces, w, sems.at[pl.ds(0, 4)], (0, cut))
    begin(other_active, right, sems.at[8])
    load(pool_pieces, pool, sems.at[pl.ds(4, 4)], (cut, half))
    begin(cotangent.at[core], cot, sems.at[9])
    parts = []
    for i in range(2):
        span = slice(i * half, (i + 1) * half)
        landed(w.at[0, pl.ds(i * half, half), :], sems.at[i])
        parts.append(dot(w[0, span, :], active[...], NT))
    landed(right, sems.at[8])
    for i in range(2):
        span = slice(i * half, (i + 1) * half)
        landed(w.at[1, pl.ds(i * half, half), :], sems.at[2 + i])
        parts[i] = parts[i] + dot(w[1, span, :], right[...], NT)
    to_rows(jnp.concatenate(parts, 0), wide, masks, me)
    total = first[...].astype(F32) + wide[...].T + vec[DOWN_B : DOWN_B + 1, :]
    gain, shift = vec[GAIN_2 : GAIN_2 + 1, :], vec[SHIFT_2 : SHIFT_2 + 1, :]
    normed, root = normalize(total)
    ids = lax.broadcasted_iota(jnp.int32, (length, 1), 0)
    block[...] = jnp.where(ids < count, normed * gain + shift, 0.0).astype(BF)
    for h in range(2):
        loaded(pool, h, sems.at[pl.ds(4, 4)])
    head = (normed[0:8, :] * gain + shift).astype(BF)
    sides = [pl.ds(pl.multiple_of(side * half, LANES), half) for side in (core, 1 - core)]
    slim[:, 0:8] = head.astype(F32).T
    for j in range(BLOCKS):
        at = slice(j * (width // BLOCKS), (j + 1) * (width // BLOCKS))
        slim[at, LANES : LANES + 8] = slim[row_block(me, pool_masks[j], width // BLOCKS), 0:8]
    head_t = slim[:, LANES : LANES + 8].astype(BF)
    for h in range(2):
        z[:, sides[h]] = dot(head_t, pool[h], TN)
    pooled_wide = jnp.tanh(z[...] + vec[POOL_B : POOL_B + 1, :])
    pooled = pooled_wide.astype(BF).astype(F32)
    class_rows = [vec[CLASS + c : CLASS + c + 1, :] for c in range(3)]
    logits = [
        jnp.sum(pooled * class_rows[c], -1, keepdims=True) + class_bias[c] for c in range(3)
    ]
    top = jnp.maximum(jnp.maximum(logits[0], logits[1]), logits[2])
    powers = [jnp.exp(l - top) for l in logits]
    power_sum = powers[0] + powers[1] + powers[2]
    deltas = [powers[c] / power_sum - jnp.where(label == c, 1.0, 0.0) for c in range(3)]
    pre = sum(deltas[c] * class_rows[c] for c in range(3)) * (1.0 - pooled_wide * pooled_wide)
    pre_high = pre.astype(BF)
    z[0:8, :] = pre_high.astype(F32)
    high = [z[:, side].astype(BF) for side in sides]
    z[0:8, :] = pre - pre_high.astype(F32)
    low = [z[:, side].astype(BF) for side in sides]
    slim[:, 0:8] = row_product(pool, high) + row_product(pool, low)
    for j in range(BLOCKS):
        at = slice(j * (width // BLOCKS), (j + 1) * (width // BLOCKS))
        slim[row_block(me, pool_masks[j], width // BLOCKS), LANES : LANES + 8] = slim[at, 0:8]
    head_delta = slim[:, LANES : LANES + 8].T[0:1, :]
    lane = lax.broadcasted_iota(jnp.int32, (1, width), 1)
    tail = jnp.zeros((1, width), F32)
    for c in range(3):
        tail = jnp.where(lane == c, deltas[c][0:1], tail)
        tail = jnp.where(lane == LANES + c, logits[c][0:1], tail)
    ramp[0:1, :] = head[0:1, :].astype(F32)
    ramp[1:2, :] = pooled[0:1, :]
    ramp[2:3, :] = pre[0:1, :]
    ramp[3:4, :] = tail
    ramp[4:8, :] = jnp.zeros((4, width), F32)
    landed(cot, sems.at[9])
    delta = jnp.where(ids < count, cot[...].astype(F32), 0.0) + jnp.where(ids == 0, head_delta, 0.0)
    grads[0:1, :] = column_sum(delta * normed)
    grads[1:2, :] = column_sum(delta)
    dsecond = norm_backward(delta, normed, root, gain)
    grads[2:3, :] = column_sum(dsecond)
    grads[3:4, :] = pre[0:1, :]
    for c in range(3):
        grads[4 + c : 5 + c, :] = deltas[c][0:1] * pooled[0:1, :]
    grads[7:8, :] = tail
    second[...] = dsecond
    flip[...] = dsecond.astype(BF).T
    to_blocks(flip, feed_r, masks, me)
    to_blocks(flip, feed_back, back_masks, me)


def hidden_kernel(h, feed_r, slope, lower, upper, target, w, sems):
    half = target.shape[1]
    load((lower, upper), w, sems, (0, half))
    left = feed_r[...].T
    chunk = 512
    loaded(w, 0, sems)
    for c in range(half // chunk):
        cols = slice(c * chunk, (c + 1) * chunk)
        at = h * half + c * chunk
        target[:, cols] = (dot(left, w[0, :, cols]) * slope[:, at : at + chunk].astype(F32)).astype(BF)


def down_grad_kernel(info, ramp, ramp_other, left_in, left_other_in, right, right_other_in, *refs):
    lower, upper, logits, left, left_other, right_other, sems = refs
    loads = ((left_in, left), (left_other_in, left_other), (right_other_in, right_other))
    for i, (source, target) in enumerate(loads):
        begin(source, target, sems.at[i])
    width, columns = left.shape[0], right.shape[1]
    half = width // 2
    classes = logits.shape[1]
    pair = [r[3:4, LANES : LANES + classes] for r in (ramp, ramp_other)]
    logits[0:1, :] = jnp.where(info[1] == 0, pair[0], pair[1])
    logits[1:2, :] = jnp.where(info[1] == 0, pair[1], pair[0])
    heads = jnp.concatenate([ramp[0:1, :], ramp_other[0:1, :], jnp.zeros((NOTES - 2, width), F32)], 0)
    pres = jnp.concatenate([ramp[2:3, :], ramp_other[2:3, :], jnp.zeros((NOTES - 2, width), F32)], 0)
    upper[half:, :width] = heads.astype(BF)
    upper[half:, width:] = pres.astype(BF)
    for i, (_, target) in enumerate(loads):
        landed(target, sems.at[i])
    for target, span in ((lower, slice(0, half)), (upper, slice(half, width))):
        total = dot(left[span, :], right[...]) + dot(left_other[span, :], right_other[...])
        target[0:half, :] = total.astype(BF)


def up_grad_kernel(left, left_other, right, right_other_in, *refs):
    lower, upper, sums, right_other, sems = refs
    begin(right_other_in, right_other, sems.at[0])
    own_sum = column_sum(right[...].astype(F32))
    landed(right_other, sems.at[0])
    sums[...] = own_sum + column_sum(right_other[...].astype(F32))
    pair_product((left, left_other), (right, right_other), lower, upper)


def branch_kernel(masks_p, masks_q, info, vec, sums_in, delta, other_delta, second, normed, root, *refs):
    up, vo = refs[0:4], refs[4:8]
    total_out, datt, branch_p, grads = refs[8:12]
    wu, wo, right, flip, rows_q, wide, sems = refs[12:]
    me = info[0]
    width = normed.shape[1]
    half = width // 2
    load(up, wu, sems.at[pl.ds(5, 4)], (0, delta.shape[1]))
    begin(other_delta, right, sems.at[4])
    load(vo, wo, sems.at[pl.ds(0, 4)], (half, half))
    gain = vec[GAIN_1 : GAIN_1 + 1, :]
    parts = []
    for i in range(2):
        span = slice(i * half, (i + 1) * half)
        landed(wu.at[0, pl.ds(i * half, half), :], sems.at[5 + i])
        parts.append(dot(wu[0, span, :], delta[...], NT))
    landed(right, sems.at[4])
    for i in range(2):
        span = slice(i * half, (i + 1) * half)
        landed(wu.at[1, pl.ds(i * half, half), :], sems.at[7 + i])
        parts[i] = parts[i] + dot(wu[1, span, :], right[...], NT)
    to_rows(jnp.concatenate(parts, 0), wide, masks_p, me)
    dfirst = second[...] + wide[...].T
    own_normed = normed[...]
    total = norm_backward(dfirst, own_normed, root[:, 0:1], gain)
    total_out[...] = total
    flip[...] = total.astype(BF).T
    to_blocks(flip, branch_p, masks_p, me)
    to_blocks(flip, rows_q, masks_q, me)
    grads[0:1, :] = column_sum(total)
    grads[1:2, :] = column_sum(dfirst * own_normed)
    grads[2:3, :] = column_sum(dfirst)
    grads[3 : SHARED + 1, :] = sums_in[...]
    grads[SHARED + 1 :, :] = jnp.zeros((grads.shape[0] - SHARED - 1, width), F32)
    left = rows_q[...].T
    for h in range(2):
        loaded(wo, h, sems)
        datt[:, h * half : (h + 1) * half] = dot(left, wo[h]).astype(BF)


def back_kernel(q, k, v, att_own, att_other, datt, p, *refs):
    qk_own, v_own, qk_other, v_other = refs[0:4]
    att, dq, dk, dv = refs[4:]
    length, width = q.shape
    half = width // 2
    att[:, :half] = att_own[...]
    att[:, half:] = att_other[...]
    lane = lax.broadcasted_iota(jnp.int32, (1, LANES), 1)
    pairs = width // LANES

    for pair in range(pairs):
        cols = slice(pair * LANES, (pair + 1) * LANES)
        do = datt[:, cols]
        product = do.astype(F32) * att[:, cols].astype(F32)
        k_pair, v_pair = k[:, cols], v[:, cols]
        q_t = q[:, cols].T
        do_t = do.T
        dq_sum = None
        dk_parts, dv_parts = [], []
        for a in range(2):
            mine = (lane < HD) if a == 0 else (lane >= HD)
            shift = jnp.sum(jnp.where(mine, product, 0.0), -1, keepdims=True)
            dprobs = dot(jnp.where(mine, do, 0.0).astype(BF), v_pair, NT)
            probs = p[pair, a]
            dscores = (probs.astype(F32) * (dprobs - shift)).astype(BF)
            term = dot(dscores, jnp.where(mine, k_pair, 0.0).astype(BF))
            dq_sum = term if dq_sum is None else dq_sum + term
            own = slice(a * HD, (a + 1) * HD)
            dk_parts.append(dot(q_t[own], dscores))
            dv_parts.append(dot(do_t[own], probs))
        dq[:, cols] = (dq_sum * (1.0 / math.sqrt(HD))).astype(BF)
        dk[:, cols] = jnp.concatenate(dk_parts, 0).T.astype(BF)
        dv[:, cols] = jnp.concatenate(dv_parts, 0).T.astype(BF)
    for h, (qk, values) in enumerate(((qk_own, v_own), (qk_other, v_other))):
        own = slice(h * half, (h + 1) * half)
        qk[:, :half] = dq[:, own]
        qk[:, half:] = dk[:, own]
        values[...] = dv[:, own]


def out_grad_kernel(branch_t, other_branch_t, att, other_att, grad):
    grad[...] = (dot(branch_t[...], att[...]) + dot(other_branch_t[...], other_att[...])).astype(BF)


def input_grad_kernel(
    masks_p, info, sums_in, sums_other, up_sums, x_p, x_q, other_p, other_q, qk, qk_in, values, values_in, out_grad,
    *refs
):
    qk_pieces, vo_pieces = refs[0:2], refs[2:4]
    extra = refs[4]
    me = info[0]
    width = x_p.shape[0]
    half = width // 2
    rows = width // BLOCKS
    query_sum = column_sum(qk[:, :half].astype(F32)) + column_sum(qk_in[:, :half].astype(F32))
    value_sum = column_sum(values[...].astype(F32)) + column_sum(values_in[...].astype(F32))
    pack_vectors(sums_in[...] + sums_other[...], query_sum, value_sum, up_sums[...], extra)
    for i, target in enumerate(vo_pieces):
        span = slice(i * half, (i + 1) * half)
        total = dot(x_p[span, :], values[...]) + dot(other_p[span, :], values_in[...])
        target[:, 0:half] = total.astype(BF)
        target[:, half:width] = out_grad[span, :]
        for j in range(BLOCKS // 2):
            at = row_block(me, masks_p[i * (BLOCKS // 2) + j], rows)
            target[j * rows : (j + 1) * rows, width:] = extra[at, :].astype(BF)
    pair_product((x_q, other_q), (qk, qk_in), *qk_pieces)


def hop_kernel(*refs):
    sent, kept = refs[-2:]
    at = 0
    for own, arrived in zip(refs[0:-2:2], refs[1:-2:2]):
        half, _, width = sent.shape[0], 0, own.shape[2]
        cols = slice(at, at + width)
        sent[:, :, cols] = own[half:] + arrived[half:]
        kept[:, :, cols] = own[:half] + arrived[:half]
        at += width


def noted_hop_kernel(count, notes, own, arrived, sent, kept):
    cut = sent.shape[0] - NOTES
    sent[0:cut, :] = own[cut:, :] + arrived[cut : 2 * cut, :]
    kept[...] = own[0:cut, :] + arrived[0:cut, :]
    low, high = notes[0:NOTES, :].astype(F32), arrived[2 * cut :, :].astype(F32)
    rows = lax.broadcasted_iota(jnp.int32, (NOTES, 1), 0)
    sent[cut:, :] = jnp.where(rows < count, low, jnp.where(rows < 2 * count, pltpu.roll(high, count, 0), 0.0)).astype(BF)


def ramp_grad_kernel(info, notes, arrived, out, flip):
    rows, width = out.shape
    both = jnp.concatenate([notes[...], arrived[...]], 0).astype(F32)
    flip[...] = both[:, :width].T
    own = flip[pl.ds(pl.multiple_of(info[0] * rows, 16), rows), :].astype(BF)
    out[...] = dot(own, both[:, width:].astype(BF))


def finish_kernel(kept, arrived, input_out, out_out, pair_out, up_out, class_bias_out, class_out, *vectors):
    share = kept[0].astype(F32) + arrived[0].astype(F32)
    rows, half = input_out.shape[1:]
    for i in range(3):
        input_out[i] = share[:, i * half : (i + 1) * half]
    out_out[...] = share[:, 3 * half : 4 * half]
    extra = share[:, 4 * half :]
    for i, target in enumerate(vectors):
        target[...] = extra[i : i + 1, 0:rows]
    pair_out[0:1, :] = extra[PAIR_ROW : PAIR_ROW + 1, 0 : rows // 2]
    pair_out[1:2, :] = extra[PAIR_ROW : PAIR_ROW + 1, rows // 2 : rows]
    up_out[...] = extra[UP_ROW : UP_ROW + 1, 0 : 2 * rows]
    class_bias_out[...] = extra[CLASS_ROW : CLASS_ROW + 1, 0 : class_bias_out.shape[1]]
    class_out[...] = extra[len(vectors) : SHARED, 0:rows]


def arrange_kernel(info, block_own, block_other, grad_own, grad_other, block_out, grad_out, held, sems):
    core = info[1]
    moves = (
        (block_own, block_out, core),
        (block_other, block_out, 1 - core),
        (grad_own, grad_out, core),
        (grad_other, grad_out, 1 - core),
    )
    for i, (source, _, _) in enumerate(moves):
        begin(source, held.at[i], sems.at[i])
    for i, (_, target, side) in enumerate(moves):
        landed(held.at[i], sems.at[i])
        begin(held.at[i], target.at[side], sems.at[4 + i])
    for i in range(4):
        landed(held.at[i], sems.at[4 + i])


def input_kernel(masks_p, masks_q, info, qk_own, v_own, qk_other, v_other, total, *refs):
    qk, vo = refs[0:4], refs[4:8]
    out, wa, wv, wide, wide_v, sems = refs[8:]
    me = info[0]
    width = total.shape[1]
    half = width // 2
    load(vo, wv, sems.at[pl.ds(0, 4)], (0, half))
    load(qk, wa, sems.at[pl.ds(4, 4)])
    for h in range(2):
        loaded(wv, h, sems.at[pl.ds(0, 4)])
    to_rows(row_product(wv, (v_own[...], v_other[...])), wide_v, masks_q, me)
    for h in range(2):
        loaded(wa, h, sems.at[pl.ds(4, 4)])
    to_rows(row_product(wa, (qk_own[...], qk_other[...])), wide, masks_p, me)
    out[...] = (total[...] + (wide[...] + wide_v[...]).T).astype(BF)


def costing(micros):
    return pl.CostEstimate(flops=micros * FLOPS_PER_MICROSECOND, bytes_accessed=1024, transcendentals=0)


def call(body, name, micros, mib, in_specs, outs, scratch, sems, args):
    return pl.pallas_call(
        body,
        name=name,
        in_specs=in_specs,
        out_specs=[spec for _, spec in outs],
        out_shape=[shape for shape, _ in outs],
        scratch_shapes=[pltpu.VMEM(s, d) for s, d in scratch] + [pltpu.SemaphoreType.DMA((sems,))] * (sems > 0),
        compiler_params=pltpu.CompilerParams(vmem_limit_bytes=mib * MIB),
        cost_estimate=costing(micros),
    )(*args)


def orders(size):
    bits = [1 << k for k in range(size.bit_length() - 1)]
    high = bits[2:][::-1]
    x_last, y_last = high + [2, 1], high + [1, 2]
    return (x_last, x_last, x_last, [1] + high + [2]), (y_last, x_last, [2] + high + [1], [1] + high + [2])


def block_mask(index, order):
    mask = 0
    for k, bit in enumerate(order):
        if (index >> k) & 1:
            mask ^= bit
    return mask


def swap(array, mask):
    size = lax.axis_size("dp")
    return lax.ppermute(array, "dp", [(i, i ^ mask) for i in range(size)])


def swap_core(array):
    return lax.ppermute(array, "tensor", [(0, 1), (1, 0)])


def after(array, *others):
    return lax.optimization_barrier((array, *others))[0]


def join(left, right):
    return jnp.concatenate([left, right], 0)


def gather_blocks(shard, order):
    held = shard[None]
    for mask in order:
        held = join(held, swap(held, mask))
    return held


def hop(blocks, arrived):
    half = blocks.shape[0] // 2
    return blocks[half:] + arrived[half:], blocks[:half] + arrived[:half]


def scatter_blocks(blocks, order):
    for mask in order[::-1]:
        half = blocks.shape[0] // 2
        blocks = blocks[:half] + swap(blocks[half:], mask)
    return blocks[0]


def in_order(blocks, order, me):
    size = len(blocks)
    place = [0] * size
    for j in range(size):
        place[block_mask(j, order)] = j
    chosen = jnp.array(place)[jnp.arange(size) ^ me]
    return jnp.take(blocks, chosen, axis=0)


def out_of_order(blocks, order, me):
    owners = jnp.array([block_mask(j, order) for j in range(len(blocks))]) ^ me
    return jnp.take(blocks, owners, axis=0)


def extra_columns(shared, pair, up, rows):
    def lanes(array):
        return jnp.pad(array, ((0, 0), (0, 0), (0, LANES - array.shape[2])))

    columns = jnp.concatenate([lanes(shared), lanes(pair), lanes(up)], 1)
    return jnp.pad(columns, ((0, 0), (0, rows - columns.shape[1]), (0, 0)))


def per_device(
    hidden_in,
    lengths,
    labels,
    out_cot,
    input_weight,
    input_bias,
    out_weight,
    out_bias,
    first_gain,
    first_shift,
    up_weight,
    up_bias,
    down_weight,
    down_bias,
    second_gain,
    second_shift,
    pool_weight,
    pool_bias,
    class_weight,
    class_bias,
):
    size = lax.axis_size("dp")
    me = lax.axis_index("dp")
    core = lax.axis_index("tensor")
    length, width = hidden_in.shape[2:]
    rows = width // size
    half = input_weight.shape[2]
    hidden_half = up_weight.shape[1]
    hidden_width = 2 * hidden_half
    classes = class_bias.shape[0]
    pairs = width // LANES
    block = width // BLOCKS
    lower = BLOCKS // 2
    direct = size == BLOCKS
    (order_a, order_b, order_u, order_d), (back_a, back_b, back_u, back_d) = orders(size)

    def kernel_masks(order):
        return [block_mask(j, order) if direct else j for j in range(BLOCKS)]

    (a_masks, b_masks, u_masks, d_masks), back_masks = [[kernel_masks(o) for o in part] for part in orders(size)]

    inputs = hidden_in.reshape(2, length, width)
    cotangents = out_cot.reshape(2, length, width)
    info = jnp.concatenate(
        [
            jnp.stack([me if direct else jnp.zeros_like(me), core]).astype(jnp.int32),
            lengths.reshape(-1),
            labels.reshape(-1),
        ]
    )

    def shape(*dims, dtype=BF):
        return jax.ShapeDtypeStruct(dims, dtype)

    def of(s):
        return (s.shape, s.dtype)

    def in_vmem(*shapes):
        return [(s, VMEM) for s in shapes]

    def in_hbm(*shapes):
        return [(s, HBM) for s in shapes]

    row = shape(length, width)
    flat = shape(width, length)
    x_p, x_q, other_p, other_q, x_rows = call(
        functools.partial(prepare_kernel, back_masks[1], back_masks[0]),
        "prepare",
        0,
        8,
        [SCALARS, HBM],
        in_hbm(flat, flat, flat, flat) + in_vmem(row),
        [of(row), of(row), of(flat), ((4, width, length), BF)],
        6,
        (info, inputs),
    )

    pool_half = lax.dynamic_slice_in_dim(pool_weight, core * half, half, 1)
    a_shard = jnp.concatenate([input_weight[0], input_weight[1]], 1)
    vo_shard = jnp.concatenate([input_weight[2], out_weight.T], 1)
    u_shard = up_weight
    d_shard = jnp.concatenate([down_weight.T, pool_half], 1)
    shared = jnp.concatenate(
        [
            jnp.stack(
                [out_bias, first_gain, first_shift, down_bias, second_gain, second_shift, pool_bias]
            ),
            class_weight.T,
        ],
        0,
    )
    def with_other(lo, hi):
        return flat_rows(lo, hi, swap_core(lo), swap_core(hi))

    def flat_rows(*arrays):
        return tuple(array.reshape(-1, array.shape[2]) for array in arrays)

    def by_block(arrays):
        return [array.reshape(lower, block, array.shape[1]) for array in arrays]

    if direct:
        extra = extra_columns(
            shared[None], input_bias[None], up_bias.reshape(1, 1, 2 * rows), rows
        )
        b_shard = jnp.concatenate([vo_shard, after(extra, a_shard)[0]], 1)
        a0, b0, u0, d0 = a_shard[None], b_shard[None], u_shard[None], d_shard[None]
        z1, z0 = order_a[0], order_a[1]
        a1, b1, d1 = swap(a0, z1), swap(b0, z1), swap(d0, 1)
        a2, b2 = join(a0, a1), join(b0, b1)
        a2_in, b2_in = swap(a2, z0), swap(b2, z0)
        u1 = swap(after(u0, a2, b2), z1)
        a4, b4 = join(a2, a2_in), join(b2, b2_in)
        a4_in, b4_in = swap(a4, 2), swap(b4, 2)
        u2 = after(join(u0, u1), a4, b4)
        u2_in = swap(u2, z0)
        a8, b8 = join(a4, a4_in), join(b4, b4_in)
        a8_in, b8_in = swap(a8, 1), swap(b8, 1)
        u4 = after(join(u2, u2_in), a8, b8)
        d2 = after(join(d0, d1), a4, b4)
        u4_in, d2_in = swap(u4, 2), swap(d2, z1)
        d4 = after(join(d2, d2_in), u4, a8_in, x_rows)
        d4_in = swap(d4, z0)
        a8_other, b8_other = swap_core(a8), swap_core(b8)
        u8 = after(join(u4, u4_in), a8_in, b8_in, d4)
        u8_in = swap(u8, 1)
        d8 = after(join(d4, d4_in), u8)
        d8_in = swap(d8, 2)
        info = after(info, u8, d8)
        qk = flat_rows(a8, a8_in, a8_other, swap_core(a8_in))
        vo = flat_rows(b8, b8_in, b8_other, swap_core(b8_in))
        pieces = [(u8, u8_in), (d8, d8_in)]
    else:

        def whole(shard, order):
            return in_order(gather_blocks(shard, order), order, me)

        def cut(array):
            blocks = array.reshape(BLOCKS, block, -1)
            return blocks[:lower], blocks[lower:]

        shared = whole(shared, order_a).transpose(1, 0, 2).reshape(-1, BLOCKS, block)
        pair = whole(input_bias, order_a).transpose(1, 0, 2).reshape(2, BLOCKS, block // 2)
        extra = extra_columns(
            shared.transpose(1, 0, 2),
            pair.transpose(1, 0, 2),
            whole(up_bias, order_a).reshape(BLOCKS, 1, 2 * block),
            block,
        )
        vo = cut(whole(vo_shard, order_b))
        vo = jnp.concatenate([vo[0], extra[:lower]], 2), jnp.concatenate([vo[1], extra[lower:]], 2)
        qk, vo = with_other(*cut(whole(a_shard, order_a))), with_other(*vo)
        pieces = [cut(whole(u_shard, order_u)), cut(whole(d_shard, order_d))]

    wide = shape(length, hidden_width)
    norm = shape(length, width, dtype=F32)
    roots = shape(length, LANES, dtype=F32)
    eight = shape(8, width, dtype=F32)
    vectors = shape(16, width, dtype=F32)
    probs = shape(pairs, 2, length, length)

    def grad(columns):
        return [shape(half, columns)] * 2

    part = width + LANES
    slim = shape(length, half)
    halved = shape(length, hidden_half)
    thirds = shape(length, 3 * half)
    matrix = shape(width, hidden_width)

    def blocks_of(columns):
        return shape(2, width, columns)

    q, k, v, att, att_other, p, first, first_p, first_back, normed, root, vec = call(
        functools.partial(attend_kernel, a_masks, back_masks[2]),
        "attend",
        0,
        18,
        [SCALARS, HBM, VMEM] + [HBM] * 8,
        in_vmem(row, row, row, slim, slim, probs, row, flat, flat, norm, roots, vectors),
        [of(row), of(blocks_of(width)), of(blocks_of(part)), of(row), of(flat), ((width, length), F32)]
        + [((width, LANES), F32)],
        10,
        (info, inputs, x_rows, *qk, *vo),
    )
    (up_lo, up_hi), (down_lo, down_hi) = pieces
    up = with_other(up_lo, after(up_hi, first))
    first_in, att_in = swap_core(first_back), swap_core(att_other)
    act, act_other, slope = call(
        up_kernel,
        "up",
        0,
        8,
        [VMEM, VMEM] + [HBM] * 4,
        in_vmem(halved, halved, wide),
        [of(blocks_of(hidden_half))],
        4,
        (vec, first_p, *up),
    )
    act_in = swap_core(act_other)
    down = with_other(down_lo, after(down_hi, act))
    block_out, ramp, feed, feed_back, second, sums_two = call(
        functools.partial(ramp_kernel, d_masks, d_masks, back_masks[3]),
        "ramp",
        15,
        18,
        [SCALARS, SCALARS, VMEM, HBM, VMEM, HBM, VMEM] + [HBM] * 8,
        in_vmem(row, eight, flat, flat, norm, eight),
        [of(blocks_of(hidden_half)), of(row), of(halved), of(blocks_of(half)), of(flat), ((width, length), F32), ((width, 2 * LANES), F32)]
        + [of(eight)],
        10,
        (info, class_bias.astype(F32), vec, cotangents, act, act_other, first, *down, *down),
    )
    feed_in, ramp_in = swap_core(feed_back), swap_core(ramp)

    def hidden(h, feed):
        (made,) = call(
            functools.partial(hidden_kernel, h),
            "hidden",
            400,
            6,
            [VMEM] * 2 + [HBM] * 2,
            in_vmem(halved),
            [((1, width, hidden_half), BF)],
            2,
            (feed, slope, *down[2 * h : 2 * h + 2]),
        )
        return made

    delta_other = hidden(1, after(feed, act_in, first_in, att_in))
    delta_in = swap_core(delta_other)
    delta = hidden(0, after(feed, delta_other))

    def first_hop(pieces, order):
        return swap(pieces[1], order[-1]) if direct else None

    def add(*streams):
        columns = sum(own.shape[2] for own, _ in streams)
        return call(
            hop_kernel,
            "hop",
            0,
            2,
            [VMEM] * (2 * len(streams)),
            in_vmem(*[shape(streams[0][0].shape[0] // 2, block, columns)] * 2),
            [],
            0,
            tuple(array for stream in streams for array in stream),
        )

    def next_hop(kept, arrived, mask, start):
        if not direct:
            return kept, None
        sent, kept = add((after(kept, start), arrived))
        return kept, swap(sent, mask)


    def noted_hop(kept, notes, arrived, k, start):
        if not direct:
            return kept, notes, None
        cut = kept.shape[0] // 2
        sent, kept = call(
            functools.partial(noted_hop_kernel, 2 << (2 - k)),
            "noted_hop",
            0,
            4,
            [VMEM] * 3,
            in_vmem(shape(cut + NOTES, hidden_half), shape(cut, hidden_half)),
            [],
            0,
            (notes, after(kept, start), arrived),
        )
        return kept, sent[cut:], swap(sent, back_d[k])

    *up_grad, up_sums = call(
        up_grad_kernel,
        "up_grad",
        0,
        6,
        [VMEM] * 3 + [HBM],
        in_vmem(*grad(hidden_half), shape(1, hidden_half, dtype=F32)),
        [of(halved)],
        1,
        (after(first_back, delta), first_in, delta, delta_in),
    )
    up_grad = by_block(up_grad)
    up_arrived = first_hop(up_grad, back_u)
    block_in = swap_core(after(block_out, up_sums))
    *down_grad, logits_out = call(
        down_grad_kernel,
        "down_grad",
        400,
        6,
        [SCALARS, VMEM, VMEM, HBM, HBM, VMEM, HBM],
        in_vmem(shape(half, hidden_half), shape(half + NOTES, hidden_half), shape(2, classes, dtype=F32)),
        [of(flat), of(flat), of(halved)],
        3,
        (after(info, up_grad[0]), ramp, ramp_in, feed_back, feed_in, act, act_in),
    )

    down_arrived = swap(down_grad[1], back_d[-1]) if direct else None
    total, datt, branch, sums_one = call(
        functools.partial(branch_kernel, u_masks, b_masks),
        "branch",
        0,
        16,
        [SCALARS] + [VMEM] * 3 + [HBM] + [VMEM] * 3 + [HBM] * 8,
        in_vmem(norm, row, flat, vectors),
        [of(blocks_of(hidden_half)), of(blocks_of(half)), of(halved), of(flat), of(flat), ((width, length), F32)],
        9,
        (after(info, down_grad[0]), vec, sums_two, delta, delta_other, second, normed, root, *up, *vo),
    )
    branch_in, sums_in = swap_core(branch), swap_core(sums_one)
    dqk, dv, dqk_other, dv_other = call(
        back_kernel,
        "back",
        0,
        10,
        [VMEM] * 7,
        in_vmem(row, slim, row, slim),
        [of(row)] * 4,
        0,
        (q, k, v, att, att_other, after(datt, block_in), p),
    )
    dqk_in, dv_in = swap_core(dqk_other), swap_core(dv_other)
    (out_grad,) = call(
        out_grad_kernel,
        "out_grad",
        0,
        3,
        [VMEM] * 4,
        in_vmem(shape(width, half)),
        [],
        0,
        (after(branch, dqk, sums_in), branch_in, att, att_in),
    )
    up_kept, up_arrived = next_hop(up_grad[0], up_arrived, back_u[2], out_grad)
    input_grads = call(
        functools.partial(input_grad_kernel, back_masks[1]),
        "input_grad",
        0,
        4,
        [SCALARS] + [VMEM] * 12,
        in_vmem(*grad(width), *grad(part)),
        [((width, LANES), F32)],
        0,
        (after(info, up_kept), sums_one, sums_in, up_sums, x_p, x_q, other_p, other_q, dqk, dqk_in, dv, dv_in, out_grad),
    )
    qk_grad, vo_grad = by_block(input_grads[:2]), by_block(input_grads[2:])
    qk_arrived, vo_arrived = first_hop(qk_grad, back_a), first_hop(vo_grad, back_b)
    (input_delta,) = call(
        functools.partial(input_kernel, a_masks, b_masks),
        "input",
        0,
        9,
        [SCALARS] + [VMEM] * 5 + [HBM] * 8,
        in_vmem(row),
        [of(blocks_of(width)), of(blocks_of(half)), ((width, length), F32), ((width, length), F32)],
        8,
        (after(info, qk_grad[0]), dqk, dv, dqk_other, dv_other, total, *qk, *vo),
    )
    input_delta_in = swap_core(input_delta)
    down_kept, notes, down_arrived = noted_hop(down_grad[0], down_grad[1][half:], down_arrived, 2, qk_grad[0])
    up_kept, up_arrived = next_hop(up_kept, up_arrived, back_u[1], down_kept)
    vo_kept, vo_arrived = next_hop(vo_grad[0], vo_arrived, back_b[2], up_kept)
    qk_kept, qk_arrived = next_hop(qk_grad[0], qk_arrived, back_a[2], vo_kept)
    blocks_out, input_grad = call(
        arrange_kernel,
        "arrange",
        0,
        4,
        [SCALARS] + [HBM] * 4,
        in_hbm(*[shape(2, length, width)] * 2),
        [((4, length, width), BF)],
        8,
        (after(info, qk_kept), block_out, block_in, input_delta, input_delta_in),
    )
    if direct:
        sent, kept = add((after(qk_kept, blocks_out), qk_arrived), (vo_kept, vo_arrived))
        arrived = swap(sent, back_a[1])
        down_kept, notes, down_arrived = noted_hop(down_kept, notes, down_arrived, 1, kept)
        up_kept, up_arrived = next_hop(up_kept, up_arrived, back_u[0], kept)
        sent, kept = add((after(kept, up_kept), arrived))
        arrived = swap(sent, back_a[0])
        down_kept, notes, down_arrived = noted_hop(down_kept, notes, down_arrived, 0, kept)
        down_kept, up_kept = after(down_kept, kept), after(up_kept, kept)
        down_share, up_share = down_kept + down_arrived[:rows], (up_kept + up_arrived)[0]
        (pool_grad,) = call(
            ramp_grad_kernel,
            "ramp_grad",
            0,
            2,
            [SCALARS, VMEM, VMEM],
            in_vmem(shape(rows, width, dtype=F32)),
            [((width, 2 * NOTES), F32)],
            0,
            (info, notes, after(down_arrived[rows:], kept)),
        )
        kept = after(kept, down_share, up_share)
    else:

        def spread(pieces, order):
            return scatter_blocks(out_of_order(join(*pieces).reshape(size, rows, -1), order, me), order)

        down_halves = by_block([down_grad[0], down_grad[1][:half]])
        down_share, up_share = spread(down_halves, back_d), spread(up_grad, back_u)
        notes = lax.all_gather(down_grad[1][half : half + 2], "dp", axis=0, tiled=True)
        own_heads = lax.dynamic_slice_in_dim(notes[:, :width], me * rows, rows, 1)
        pool_grad = dot(own_heads, notes[:, width:], TN)
        qk_share = spread(qk_grad, back_a)
    if direct:
        input_share, out_share, pair_share, up_bias_share, class_bias_grad, class_grad, *vector_grads = call(
            finish_kernel,
            "finish",
            0,
            2,
            [VMEM] * 2,
            in_vmem(
                shape(3, rows, half, dtype=F32),
                shape(rows, half, dtype=F32),
                shape(2, rows // 2, dtype=F32),
                shape(1, 2 * rows, dtype=F32),
                shape(1, classes, dtype=F32),
                shape(classes, rows, dtype=F32),
                *[shape(1, rows, dtype=F32)] * 7,
            ),
            [],
            0,
            (kept, arrived),
        )
        out_share, class_grad = out_share.T, class_grad.T
        up_bias_share, class_bias_grad = up_bias_share.reshape(-1), class_bias_grad.reshape(-1)
        vector_grads = [array.reshape(-1) for array in vector_grads]
    else:
        vo_share = spread([piece[:, :, :width] for piece in vo_grad], back_b)
        extra_sum = lax.psum(join(*[piece[:, :, width:] for piece in vo_grad]).astype(F32), "dp")

        def own(array, count):
            return lax.dynamic_slice_in_dim(array, me * count, count, array.ndim - 1)

        vector_grads = own(extra_sum[:, :SHARED, :block].transpose(1, 0, 2).reshape(SHARED, width), rows)
        pair_sums = extra_sum[:, PAIR_ROW, :block].reshape(BLOCKS, 2, block // 2)
        pair_share = own(pair_sums.transpose(1, 0, 2).reshape(2, half), rows // 2)
        up_bias_share = own(extra_sum[:, UP_ROW, : 2 * block].reshape(-1), 2 * rows)
        class_bias_grad = extra_sum[0, CLASS_ROW, :classes]
        vector_grads, class_grad = vector_grads[:7], vector_grads[7:].T
        input_share = jnp.stack([qk_share[:, :half], qk_share[:, half:], vo_share[:, :half]])
        out_share = vo_share[:, half:width].T
    return (
        blocks_out[:, None],
        logits_out[:, None],
        input_grad[:, None],
        input_share.astype(F32),
        pair_share.astype(F32),
        out_share.astype(F32),
        vector_grads[0],
        vector_grads[1],
        vector_grads[2],
        up_share.astype(F32),
        up_bias_share.astype(F32),
        down_share.T.astype(F32),
        vector_grads[5],
        vector_grads[3],
        vector_grads[4],
        pool_grad,
        vector_grads[6],
        class_grad,
        class_bias_grad.astype(F32),
    )


def solution(mesh):
    placed = (
        P(None, "dp", None, None),
        P(None, "dp"),
        P(None, "dp"),
        P(None, "dp", None, None),
        P(None, "dp", "tensor"),
        P(None, ("tensor", "dp")),
        P("tensor", "dp"),
        P("dp"),
        P("dp"),
        P("dp"),
        P("dp", "tensor"),
        P(("tensor", "dp")),
        P("tensor", "dp"),
        P("dp"),
        P("dp"),
        P("dp"),
        P("dp", None),
        P("dp"),
        P("dp", None),
        P(),
    )
    return jax.shard_map(
        per_device,
        mesh=mesh,
        in_specs=placed,
        out_specs=(
            P(None, "dp", None, None),
            P(None, "dp", None),
            P(None, "dp", None, None),
            P(None, "dp", "tensor"),
            P(None, ("tensor", "dp")),
            P("tensor", "dp"),
            P("dp"),
            P("dp"),
            P("dp"),
            P("dp", "tensor"),
            P(("tensor", "dp")),
            P("tensor", "dp"),
            P("dp"),
            P("dp"),
            P("dp"),
            P("dp", None),
            P("dp"),
            P("dp", None),
            P(),
        ),
        check_vma=False,
    )
```
